32 devices in a mesh: dp: 8 (over z, y), tensor: 4 (over x, core).
Axes of the slice: x: 2, y: 2, z: 4, core: 2. Of those that a mesh axis runs over, the one named last changes fastest.
Arguments:
- frames: bfloat16 [23552, 768], P('dp'), may hold values from -6 to 6
- segment_ids: int32 [32, 736], P('dp'), may hold values from 0 to 3, never falling along the last dimension, each value on 1 to 368 neighbouring positions
- valid_frames: int32 [32, 736], P('dp'), may hold values from 0 to 1, as said below
- inward_weight: bfloat16 [1, 3, 768, 768], P(None, None, None, 'tensor'), may hold values from -0.21875 to 0.21875
- inward_bias: bfloat16 [1, 2, 12, 64], P(None, None, 'tensor'), may hold values from -4 to 4
- output_weight: bfloat16 [1, 768, 768], P(None, 'tensor'), may hold values from -2 to 2
- upward_weight: bfloat16 [1, 768, 3072], P(None, None, 'tensor'), may hold values from -0.21875 to 0.21875
- upward_bias: bfloat16 [1, 24, 128], P(None, 'tensor'), may hold values from -4 to 4
- downward_weight: bfloat16 [1, 3072, 768], P(None, 'tensor'), may hold values from -0.109375 to 0.109375
- norm_gains: float32 [1, 2, 768], replicated, may hold values from 0.5 to 1.5
- offsets: float32 [1, 4, 768], replicated, may hold values from -4 to 4
- cotangent: float32 [23552, 768], P('dp'), may hold values from -6 to 6
Outputs:
- layer_output: bfloat16 [23552, 768], P('dp')
- grad_frames: float32 [23552, 768], P('dp')
- grad_inward_weight: float32 [1, 3, 768, 768], P(None, None, 'dp', 'tensor')
- grad_inward_bias: float32 [1, 2, 12, 64], P(None, None, 'tensor', 'dp')
- grad_output_weight: float32 [1, 768, 768], P(None, 'tensor', 'dp')
- grad_upward_weight: float32 [1, 768, 3072], P(None, 'dp', 'tensor')
- grad_upward_bias: float32 [1, 24, 128], P(None, 'tensor', 'dp')
- grad_downward_weight: float32 [1, 3072, 768], P(None, 'tensor', 'dp')
- grad_norm_gains: float32 [1, 2, 768], P(None, None, 'dp')
- grad_offsets: float32 [1, 4, 768], P(None, None, 'dp')
The draws below stay inside these ranges and needn't reach their ends.
Inputs may be any that keep to these rules, and one draw needn't show every extreme that they name: `segment_ids`: within a row the clip numbers never fall; a clip holds at most 368 frames. `valid_frames`: in each row the frames that count come first and the padding last; at least 552 frames of a row count.
All inputs are finite; a program needn't handle non-finite values.
Results may differ from the reference program's by a relative error of at most 0.013.
The reference program's roundings to bfloat16 on the way count: a program that leaves them out, or rounds other values in their place, can miss the bound.
Values may be sent and summed in bfloat16 or wider, within the bound.
A program may use at most 192 MiB of HBM per device.

```python
import math
import jax
import jax.numpy as jnp
import numpy as np
from jax import lax

D = 768
FF = 3072
HEADS = 12
HEAD_SIZE = 64
FRAMES = 736
LAYERS = 1
ROWS = 32
TOKENS = 23552


def draw_valid_frames(key, part):
    key = jax.random.fold_in(key, 11)
    shortest = FRAMES - FRAMES // 4
    lengths = jax.random.randint(key, (ROWS,), shortest, FRAMES + 1)
    lengths = jnp.where(jnp.arange(ROWS) == 0, shortest, lengths)
    return (jnp.arange(FRAMES)[None, :] < lengths[:, None]).astype(jnp.int32)


def with_spikes(array, own_key, source, target, parts, factor):
    def block_of(axis_at):
        return (jnp.arange(array.shape[axis_at]) // (array.shape[axis_at] // parts)).reshape((-1,) + (1,) * (array.ndim - 1 - axis_at))

    first = jax.random.permutation(own_key, parts)[block_of(target)]
    other_side = (block_of(target) + parts // 2) % parts
    return jnp.where((block_of(source) == first) | (block_of(source) == other_side), factor * array, array)


def level_of(stream_key, dims, shards, least, top_value):
    def one(dim, parts):
        heights = jax.random.uniform(jax.random.fold_in(jax.random.fold_in(stream_key, 6), dim), (parts,), jnp.float32, least / len(shards), top_value / len(shards))
        return jnp.repeat(jnp.exp(heights), dims[dim] // parts).reshape((-1,) + (1,) * (len(dims) - dim - 1))

    level = one(*shards[0])
    for cut in shards[1:]:
        level = level * one(*cut)
    return level


def length_profile(number_of, total, bound, skew):
    loads = [(1 << 20) // math.isqrt(rank ** skew) + 1 for rank in range(2, number_of + 1)]
    surplus, given = total - bound - (number_of - 1), [1] * (number_of - 1)
    while surplus > 0:
        candidates = [i for i in range(number_of - 1) if given[i] < bound]
        whole, left = sum([loads[i] for i in candidates]), surplus
        for i in candidates:
            more = min(bound - given[i], max(1, left * loads[i] // whole), surplus)
            given[i] = given[i] + more
            surplus = surplus - more
    return np.array([bound] + given)


def ragged(stream_key, count, total, most, skew):
    if count == 2:
        one = jax.random.randint(stream_key, (), max(1, total - most), min(most, total - 1) + 1)
        return jnp.stack([one, total - one])
    sizes = jnp.asarray(length_profile(count, total, most, skew), jnp.int32)
    pairs = (count - 1) // 2
    donor, sink = sizes[1:1 + 2 * pairs:2], sizes[2:2 + 2 * pairs:2]
    margin = jnp.minimum(donor - 1, most - sink)
    passed = jax.random.randint(jax.random.fold_in(stream_key, 1), (pairs,), 0, 1 << 20) % (margin + 1)
    sizes = sizes.at[1:1 + 2 * pairs:2].set(donor - passed).at[2:2 + 2 * pairs:2].set(sink + passed)
    return sizes[jax.random.permutation(jax.random.fold_in(stream_key, 2), count)]


def noise(stream_key, dims, spread, bound, shards=(), kind=jnp.bfloat16):
    values = spread * jax.random.normal(stream_key, dims, jnp.float32)
    if shards:
        values = values * level_of(stream_key, dims, shards, -0.22, 0.18)
    return jnp.clip(values, -bound, bound).astype(kind)


def bell_draw_with(rng, extent, deviation, limit, shards, heavy, held_as=jnp.bfloat16):
    drawn = deviation * jax.random.normal(rng, extent, jnp.float32)
    if shards:
        drawn = drawn * level_of(rng, extent, shards, -0.22, 0.18)
    return jnp.clip(with_spikes(drawn, jax.random.fold_in(rng, 3), *heavy), -limit, limit).astype(held_as)


def setup_inputs(seed: int = 0) -> dict:
    key_list = jax.random.split(jax.random.key(seed), 13)
    frames = noise(key_list[0], (TOKENS, D), 1.0, 6.0, ((0, 8),))
    segment_ids = jax.vmap(lambda own: jnp.searchsorted(jnp.cumsum(ragged(own, 4, FRAMES, FRAMES // 2, 0)), jnp.arange(FRAMES), side="right"))(jax.random.split(key_list[1], ROWS)).reshape((ROWS, FRAMES)).astype(jnp.int32)
    valid_frames = draw_valid_frames(jax.random.fold_in(key_list[12], 71), 0)
    inward_weight = noise(key_list[3], (LAYERS, 3, D, D), D ** -0.5, 0.21875, ((3, 4),))
    inward_bias = noise(key_list[4], (LAYERS, 2, HEADS, HEAD_SIZE), 0.3, 4.0, ((2, 4),))
    output_weight = noise(key_list[5], (LAYERS, D, D), (D // 96) ** -0.5, 2.0, ((1, 4),))
    upward_weight = noise(key_list[6], (LAYERS, D, FF), D ** -0.5, 0.21875, ((2, 4),))
    upward_bias = noise(key_list[7], (LAYERS, FF // 128, 128), 0.3, 4.0, ((1, 4),))
    downward_weight = noise(key_list[8], (LAYERS, FF, D), FF ** -0.5, 0.109375, ((1, 4),))
    norm_gains = jnp.clip(1.0 + 0.1 * jax.random.normal(key_list[9], (LAYERS, 2, D), jnp.float32), 0.5, 1.5)
    offsets = noise(key_list[10], (LAYERS, 4, D), 0.3, 4.0, (), jnp.float32)
    cotangent = bell_draw_with(key_list[11], (TOKENS, D), 1.0, 6.0, ((0, 8),), (0, 1, 8, 2.0), jnp.float32)
    return dict(frames=frames, segment_ids=segment_ids, valid_frames=valid_frames, inward_weight=inward_weight, inward_bias=inward_bias, output_weight=output_weight, upward_weight=upward_weight, upward_bias=upward_bias, downward_weight=downward_weight, norm_gains=norm_gains, offsets=offsets, cotangent=cotangent)


@jax.custom_vjp
def low(v):
    return lax.optimization_barrier(v.astype(jnp.bfloat16)).astype(jnp.float32)

@jax.custom_vjp
def low_back(v):
    return v

def low_keep(v):
    return (low(v), None)

def low_pass(kept, grad):
    return (grad,)

def back_keep(v):
    return (v, None)

def back_low(kept, grad):
    return (low(grad),)
low.defvjp(low_keep, low_pass)
low_back.defvjp(back_keep, back_low)
epsilon = 1e-05
highest = lax.Precision.HIGHEST

def product(left_side, right_side):
    return jnp.dot(left_side, right_side, precision=highest, preferred_element_type=jnp.float32)

def layer_norm(values, gain, offset):
    centred = values - lax.optimization_barrier(jnp.mean(values, axis=-1, keepdims=True))
    variance = lax.optimization_barrier(jnp.mean(centred * centred, axis=-1, keepdims=True))
    return centred * lax.rsqrt(variance + epsilon) * gain + offset

def attend_row(packed):
    queries, key_rows, value_rows, segments, valid_mask = packed
    frame_count = queries.shape[0]
    split_queries = queries.reshape(frame_count, HEADS, HEAD_SIZE)
    split_keys = key_rows.reshape(frame_count, HEADS, HEAD_SIZE)
    split_values = value_rows.reshape(frame_count, HEADS, HEAD_SIZE)
    scores = jnp.einsum('qhd,khd->hqk', split_queries, split_keys, precision=highest) * 0.125
    places = jnp.arange(frame_count)
    allowed = (segments[:, None] == segments[None, :]) & ((valid_mask[None, :] > 0) | (places[:, None] == places[None, :]))
    scores = low_back(jnp.where(allowed[None], scores, -1000000000.0))
    largest = lax.optimization_barrier(jnp.max(scores, axis=-1, keepdims=True))
    weights = jnp.exp(scores - largest)
    softmax_low = low(weights / lax.optimization_barrier(jnp.sum(weights, axis=-1, keepdims=True)))
    context = jnp.einsum('hqk,khd->qhd', softmax_low, split_values, precision=highest)
    return context.reshape(frame_count, HEADS * HEAD_SIZE)

def reference(frames, segment_ids, valid_frames, inward_weight, inward_bias, output_weight, upward_weight, upward_bias, downward_weight, norm_gains, offsets, cotangent):

    def forward(current, inward, inward_pair, out_matrix, up_matrix, up_vector, down_matrix, gain_table, offset_table):
        for layer_index in range(LAYERS):
            inputs_low = low(current)
            bias_pair = inward_pair[layer_index].reshape(2, D)
            queries = low(low_back(product(inputs_low, inward[layer_index, 0]) + bias_pair[0]))
            key_rows = low(low_back(product(inputs_low, inward[layer_index, 1])))
            value_rows = low(low_back(product(inputs_low, inward[layer_index, 2]) + bias_pair[1]))
            context = lax.map(jax.checkpoint(attend_row), (queries.reshape(ROWS, FRAMES, D), key_rows.reshape(ROWS, FRAMES, D), value_rows.reshape(ROWS, FRAMES, D), segment_ids, valid_frames))
            context = low(low_back(context.reshape(TOKENS, D)))
            mixed_sum = current + low_back(product(context, out_matrix[layer_index])) + offset_table[layer_index, 0]
            normed = layer_norm(mixed_sum, gain_table[layer_index, 0], offset_table[layer_index, 2])
            upward = low_back(product(low(normed), up_matrix[layer_index]) + up_vector[layer_index].reshape(FF))
            activated = low(jax.nn.gelu(upward, approximate=False))
            second = normed + low_back(product(activated, down_matrix[layer_index])) + offset_table[layer_index, 1]
            current = layer_norm(second, gain_table[layer_index, 1], offset_table[layer_index, 3])
        return current
    arguments = (frames, inward_weight, inward_bias, output_weight, upward_weight, upward_bias, downward_weight, norm_gains, offsets)
    arguments = tuple((item.astype(jnp.float32) for item in arguments))
    result, pullback = jax.vjp(forward, *arguments)
    grads = pullback(cotangent.astype(jnp.float32))
    return (result.astype(jnp.bfloat16), grads[0], grads[1], grads[2], grads[3], grads[4], grads[5], grads[6], grads[7], grads[8])
```

```python
import jax
import jax.numpy as jnp
from jax import lax
from jax.sharding import PartitionSpec as P

HEAD_SIZE = 64


epsilon = 1e-05
masked_score = -1000000000.0


def product(left_side, right_side):
    return jnp.dot(left_side, right_side, preferred_element_type=jnp.float32)


def contract_rows(left_side, right_side):
    return lax.dot_general(
        left_side, right_side, (((0,), (0,)), ((), ())), preferred_element_type=jnp.float32
    )


def contract_columns(left_side, right_side):
    return lax.dot_general(
        left_side, right_side, (((1,), (1,)), ((), ())), preferred_element_type=jnp.float32
    )


def layer_norm(values, gain, offset):
    centred = values - jnp.mean(values, axis=-1, keepdims=True)
    variance = jnp.mean(centred * centred, axis=-1, keepdims=True)
    return centred * lax.rsqrt(variance + epsilon) * gain + offset


def exact_gelu(values):
    return jax.nn.gelu(values, approximate=False)


def norm_backward(grad_rows, values, gain, offset):
    _, norm_pull = jax.vjp(layer_norm, values, gain, offset)
    return norm_pull(grad_rows)


def allowed_mask(segments, valid_mask):
    places = jnp.arange(segments.shape[0])
    same_clip = segments[:, None] == segments[None, :]
    return same_clip & ((valid_mask[None, :] > 0) | (places[:, None] == places[None, :]))


def split_heads(values):
    return values.reshape(values.shape[0], values.shape[1] // HEAD_SIZE, HEAD_SIZE)


def masked_scores(split_queries, split_keys, allowed):
    scores = (
        jnp.einsum("qhd,khd->hqk", split_queries, split_keys, preferred_element_type=jnp.float32)
        * 0.125
    )
    return jnp.where(allowed[None], scores, masked_score)


def attend_forward(packed):
    queries, key_rows, value_rows, allowed = packed
    scores = masked_scores(split_heads(queries), split_heads(key_rows), allowed)
    largest = jnp.max(scores, axis=-1, keepdims=True)
    weights = jnp.exp(scores - largest)
    denominator = jnp.sum(weights, axis=-1, keepdims=True)
    softmax_low = (weights / denominator).astype(jnp.bfloat16)
    context = jnp.einsum(
        "hqk,khd->qhd", softmax_low, split_heads(value_rows), preferred_element_type=jnp.float32
    )
    return (context.reshape(queries.shape), (largest + jnp.log(denominator))[..., 0])


def attend_backward(packed):
    queries, key_rows, value_rows, allowed, log_totals, context_grad = packed
    split_queries = split_heads(queries)
    split_keys = split_heads(key_rows)
    split_values = split_heads(value_rows)
    split_grad = split_heads(context_grad)
    scores = masked_scores(split_queries, split_keys, allowed)
    softmax_out = jnp.exp(scores - log_totals[..., None])
    softmax_low = softmax_out.astype(jnp.bfloat16)
    context = jnp.einsum(
        "hqk,khd->qhd", softmax_low, split_values, preferred_element_type=jnp.float32
    )
    value_grad = jnp.einsum(
        "hqk,qhd->khd", softmax_low, split_grad, preferred_element_type=jnp.float32
    ).astype(jnp.bfloat16)
    prob_grad = jnp.einsum(
        "qhd,khd->hqk", split_grad, split_values, preferred_element_type=jnp.float32
    )
    row_inner = jnp.sum(prob_grad * softmax_out, axis=-1, keepdims=True)
    score_grad = (softmax_out * (prob_grad - row_inner)).astype(jnp.bfloat16)
    query_grad = (
        jnp.einsum("hqk,khd->qhd", score_grad, split_keys, preferred_element_type=jnp.float32)
        * 0.125
    ).astype(jnp.bfloat16)
    key_grad = (
        jnp.einsum("hqk,qhd->khd", score_grad, split_queries, preferred_element_type=jnp.float32)
        * 0.125
    ).astype(jnp.bfloat16)
    row_shape = queries.shape
    return (
        context.reshape(row_shape).astype(jnp.bfloat16),
        query_grad.reshape(row_shape),
        key_grad.reshape(row_shape),
        value_grad.reshape(row_shape),
    )


def split_rows(values, row_count):
    return values.reshape(row_count, values.shape[0] // row_count, values.shape[1])


def project_inputs(inputs_low, inward, inward_pair):
    queries = (product(inputs_low, inward[0]) + inward_pair[0]).astype(jnp.bfloat16)
    key_rows = product(inputs_low, inward[1]).astype(jnp.bfloat16)
    value_rows = (product(inputs_low, inward[2]) + inward_pair[1]).astype(jnp.bfloat16)
    return (queries, key_rows, value_rows)


def layer_forward(current, params, allowed, row_count):
    inward, inward_pair, out_matrix, up_matrix, up_vector, down_matrix, gain_pair, offset_four = (
        params
    )
    token_count = current.shape[0]
    inputs_low = current.astype(jnp.bfloat16)
    queries, key_rows, value_rows = project_inputs(inputs_low, inward, inward_pair)
    context, log_totals = lax.map(
        attend_forward,
        (
            split_rows(queries, row_count),
            split_rows(key_rows, row_count),
            split_rows(value_rows, row_count),
            allowed,
        ),
    )
    context_low = context.reshape(token_count, -1).astype(jnp.bfloat16)
    attention_term = product(context_low, out_matrix)
    mixed_sum = current + attention_term + offset_four[0]
    normed_own = layer_norm(mixed_sum, gain_pair[0], offset_four[2])
    normed_low = normed_own.astype(jnp.bfloat16)
    upward = product(normed_low, up_matrix) + up_vector
    feed_term = product(exact_gelu(upward).astype(jnp.bfloat16), down_matrix)
    second = normed_own + feed_term + offset_four[1]
    outputs_own = layer_norm(second, gain_pair[1], offset_four[3])
    return (outputs_own, outputs_own, (inputs_low, mixed_sum, second, normed_low, log_totals))


def layer_backward(incoming, kept_state, params, allowed, row_count):
    inward, inward_pair, out_matrix, up_matrix, up_vector, down_matrix, gain_pair, offset_four = (
        params
    )
    inputs_low, mixed_sum, second, normed_low, log_totals = kept_state
    token_count = inputs_low.shape[0]
    second_part, gain_two, offset_two = norm_backward(
        incoming, second, gain_pair[1], offset_four[3]
    )
    down_bias_grad = jnp.sum(second_part, axis=0)
    second_low = second_part.astype(jnp.bfloat16)
    upward = product(normed_low, up_matrix) + up_vector
    activated, gelu_pull = jax.vjp(exact_gelu, upward)
    down_grad = contract_rows(activated.astype(jnp.bfloat16), second_low)
    (upward_grad,) = gelu_pull(contract_columns(second_low, down_matrix))
    upward_low = upward_grad.astype(jnp.bfloat16)
    up_grad = contract_rows(normed_low, upward_low)
    up_bias_grad = jnp.sum(upward_low.astype(jnp.float32), axis=0)
    normed_term = contract_columns(upward_low, up_matrix)
    normed_grad = second_part + normed_term
    mixed_part, gain_one, offset_one = norm_backward(
        normed_grad, mixed_sum, gain_pair[0], offset_four[2]
    )
    out_bias_grad = jnp.sum(mixed_part, axis=0)
    mixed_low = mixed_part.astype(jnp.bfloat16)
    queries, key_rows, value_rows = project_inputs(inputs_low, inward, inward_pair)
    context_grad = contract_columns(mixed_low, out_matrix).astype(jnp.bfloat16)
    context_low, query_grad, key_grad, value_grad = lax.map(
        attend_backward,
        (
            split_rows(queries, row_count),
            split_rows(key_rows, row_count),
            split_rows(value_rows, row_count),
            allowed,
            log_totals,
            split_rows(context_grad, row_count),
        ),
    )
    context_low = context_low.reshape(token_count, -1)
    query_grad = query_grad.reshape(token_count, -1)
    key_grad = key_grad.reshape(token_count, -1)
    value_grad = value_grad.reshape(token_count, -1)
    out_grad = contract_rows(context_low, mixed_low)
    inward_grad = jnp.stack(
        [
            contract_rows(inputs_low, query_grad),
            contract_rows(inputs_low, key_grad),
            contract_rows(inputs_low, value_grad),
        ]
    )
    inward_bias_grad = jnp.stack(
        [
            jnp.sum(query_grad.astype(jnp.float32), axis=0),
            jnp.sum(value_grad.astype(jnp.float32), axis=0),
        ]
    ).reshape(2, -1, HEAD_SIZE)
    input_term = (
        contract_columns(query_grad, inward[0])
        + contract_columns(key_grad, inward[1])
        + contract_columns(value_grad, inward[2])
    )
    input_grad = mixed_part + input_term
    gain_grad = jnp.stack([gain_one, gain_two])
    offset_grad = jnp.stack([out_bias_grad, down_bias_grad, offset_one, offset_two])
    layer_grads = (
        inward_grad,
        inward_bias_grad,
        out_grad,
        up_grad,
        up_bias_grad.reshape(-1, 128),
        down_grad,
        gain_grad,
        offset_grad,
    )
    return (input_grad, layer_grads)


def shards(
    frames,
    segment_ids,
    valid_frames,
    inward_weight,
    inward_bias,
    output_weight,
    upward_weight,
    upward_bias,
    downward_weight,
    norm_gains,
    offsets,
    cotangent,
):
    row_count = segment_ids.shape[0]
    part_count = lax.axis_size("tensor")
    own_rows = row_count // part_count
    token_count = frames.shape[0] // part_count
    place = lax.axis_index("tensor")

    def own(values, count):
        return lax.dynamic_slice_in_dim(values, place * count, count, 0)

    def whole(values, axis):
        return lax.all_gather(values, "tensor", axis=axis, tiled=True)

    allowed = jax.vmap(allowed_mask)(own(segment_ids, own_rows), own(valid_frames, own_rows))
    params = (
        whole(inward_weight[0], 2),
        whole(inward_bias[0], 1).reshape(2, -1),
        whole(output_weight[0], 0),
        whole(upward_weight[0], 1),
        whole(upward_bias[0], 0).reshape(-1),
        whole(downward_weight[0], 0),
        norm_gains[0],
        offsets[0],
    )
    current = own(frames, token_count).astype(jnp.float32)
    current, _, kept_state = layer_forward(current, params, allowed, own_rows)
    layer_output = whole(current.astype(jnp.bfloat16), 0)
    incoming, grads = layer_backward(
        own(cotangent, token_count), kept_state, params, allowed, own_rows
    )
    grad_frames = whole(incoming.astype(jnp.bfloat16), 0).astype(jnp.float32)

    def scatter(values, tensor_dim, dp_dim, low=True):
        if low:
            values = values.astype(jnp.bfloat16)
        if tensor_dim is None:
            values = lax.psum(values, "tensor")
        else:
            values = lax.psum_scatter(values, "tensor", scatter_dimension=tensor_dim, tiled=True)
        values = lax.psum_scatter(values, "dp", scatter_dimension=dp_dim, tiled=True)
        return values.astype(jnp.float32)[None]

    return (
        layer_output,
        grad_frames,
        scatter(grads[0], 2, 1),
        scatter(grads[1], 1, 2, False),
        scatter(grads[2], 0, 1),
        scatter(grads[3], 1, 0),
        scatter(grads[4], 0, 1, False),
        scatter(grads[5], 0, 1),
        scatter(grads[6], None, 1, False),
        scatter(grads[7], None, 1, False),
    )


def solution(mesh):
    in_specs = (
        P("dp", None),
        P("dp", None),
        P("dp", None),
        P(None, None, None, "tensor"),
        P(None, None, "tensor", None),
        P(None, "tensor", None),
        P(None, None, "tensor"),
        P(None, "tensor", None),
        P(None, "tensor", None),
        P(),
        P(),
        P("dp", None),
    )
    out_specs = (
        P("dp", None),
        P("dp", None),
        P(None, None, "dp", "tensor"),
        P(None, None, "tensor", "dp"),
        P(None, "tensor", "dp"),
        P(None, "dp", "tensor"),
        P(None, "tensor", "dp"),
        P(None, "tensor", "dp"),
        P(None, None, "dp"),
        P(None, None, "dp"),
    )
    return jax.shard_map(shards, mesh=mesh, in_specs=in_specs, out_specs=out_specs, check_vma=False)
```

```python
import functools
import itertools

import jax
import jax.numpy as jnp
from jax import lax
from jax.experimental import pallas as pl
from jax.experimental.pallas import tpu as pltpu
from jax.sharding import PartitionSpec as P

HEAD_SIZE = 64
LANES = 128
PAD = 128
LONGEST_CLIP_SHARE = 2
EPSILON = 1e-05
FAR = float(2**30)
LOW = jnp.bfloat16
WIDE = jnp.float32
MESH = pl.DeviceIdType.MESH
VMEM_BYTES = 60 << 20


def nn(left_side, right_side):
    return jnp.dot(left_side, right_side, preferred_element_type=WIDE)


def nt(left_side, right_side):
    return lax.dot_general(
        left_side, right_side, (((1,), (1,)), ((), ())), preferred_element_type=WIDE
    )


def padded(count):
    return -(-count // LANES) * LANES


def row_blocks(count, size=256):
    return [(start, min(size, count - start)) for start in range(0, count, size)]


def key_range(start, size, count):
    reach = count // LONGEST_CLIP_SHARE - 1
    low = max(0, (start - reach) // LANES * LANES)
    high = min(padded(count), padded(start + size + reach))
    return (low, high)


class Places:
    def __init__(self, bits):
        self.dp = lax.axis_index("dp")
        self.t = lax.axis_index("tensor")
        core = self.t % 2
        self.core = (self.dp, self.t + 1 - 2 * core)
        self.x = (self.dp, (self.t + 2) % 4)
        self.diagonal = (self.dp, 3 - self.t)
        self.bit = [(self.dp // 2**b) % 2 for b in range(bits)]
        self.step = [
            (self.dp + (1 - 2 * self.bit[b]) * 2**b, self.t) for b in range(bits)
        ]

    def greet(self, devices):
        barrier = pltpu.get_barrier_semaphore()
        for device in devices:
            pl.semaphore_signal(barrier, inc=1, device_id=device, device_id_type=MESH)
        pl.semaphore_wait(barrier, len(devices))


class Links:
    def __init__(self, send, recv, local):
        self.send, self.recv, self.local = send, recv, local
        self.used = self.used_local = 0

    def remote(self, source, target, device):
        place = self.used
        self.used += 1
        return pltpu.make_async_remote_copy(
            src_ref=source,
            dst_ref=target,
            send_sem=self.send.at[place],
            recv_sem=self.recv.at[place],
            device_id=device,
            device_id_type=MESH,
        )

    def near(self, source, target):
        place = self.used_local
        self.used_local += 1
        copy = pltpu.make_async_copy(source, target, self.local.at[place])
        copy.start()
        return copy


def start(copies):
    for copy in copies:
        copy.start()


def arrived(copies):
    for copy in copies:
        copy.wait_recv()


def sent(copies):
    for copy in copies:
        copy.wait_send()


def lane_numbers():
    return lax.broadcasted_iota(jnp.int32, (1, LANES), 1)


def add_corner(scores, low, corner, corner_start):
    cut = corner_start - low
    return jnp.concatenate([scores[:, :cut], scores[:, cut:] + corner], axis=1)


def forward_kernel(
    count,
    frames,
    p_own,
    h_own,
    u_own,
    d_own,
    b_own,
    qf_ref,
    kf_ref,
    corner_ref,
    norm_ref,
    a_all,
    u_all,
    d_all,
    b_all,
    q_out,
    k_out,
    v_out,
    ctx_out,
    lse_out,
    mixed_out,
    a_vm,
    b_vm,
    x_vm,
    acc,
    send_sems,
    recv_sems,
    local_sems,
):
    places = Places(1)
    links = Links(send_sems, recv_sems, local_sems)
    mine = places.bit[0]
    wide_count = padded(count)
    features = x_vm.shape[1]
    half_rows = features // 2
    places.greet([places.core, places.x, places.diagonal, places.step[0]])

    def own(matrix, half):
        if matrix == 0:
            kinds = pl.ds(0, 4) if half is None else pl.ds(2 * half, 2)
            return [p_own.at[kinds], h_own.at[kinds]]
        ref = u_own if matrix == 1 else d_own
        if half is None:
            return [ref]
        return [ref.at[pl.ds(half * half_rows, half_rows)]]

    def slot(matrix, number, half):
        if matrix == 0:
            kinds = pl.ds(0, 4) if half is None else pl.ds(2 * half, 2)
            group, odd = number // 2, number % 2
            return [
                a_vm.at[group, kinds, pl.ds(256 if odd else 0, 128)],
                a_vm.at[group, kinds, pl.ds(192 if odd else 128, 64)],
            ]
        ref = u_all if matrix == 1 else d_all
        if half is None:
            return [ref.at[number]]
        return [ref.at[number, pl.ds(half * half_rows, half_rows)]]

    def remotes(sources, targets, device):
        return [links.remote(s, t, device) for s, t in zip(sources, targets)]

    core, across, along, first, second = {}, {}, {}, {}, {}
    for matrix in range(3):
        core[matrix] = remotes(own(matrix, None), slot(matrix, 1, None), places.core)
        across[matrix] = remotes(own(matrix, mine), slot(matrix, 2, mine), places.x)
        along[matrix] = remotes(slot(matrix, 2, mine), slot(matrix, 2, mine), places.step[0])
        first[matrix] = remotes(slot(matrix, 2, mine), slot(matrix, 3, mine), places.core)
        second[matrix] = remotes(
            slot(matrix, 2, 1 - mine), slot(matrix, 3, 1 - mine), places.core
        )
    biases = [
        links.remote(b_own.at[1], b_vm.at[1], places.core),
        links.remote(b_own.at[0], b_vm.at[2], places.x),
        links.remote(b_own.at[1], b_vm.at[3], places.diagonal),
    ]
    start(across[0])
    start(core[0])
    start(biases)
    loads = [
        links.near(frames.at[pl.ds(places.t * count, count)], x_vm),
        links.near(b_own.at[0], b_vm.at[0]),
    ]
    for source, target in zip(own(0, None), slot(0, 0, None)):
        loads.append(links.near(source, target))
    later = [links.near(u_own, u_all.at[0]), links.near(d_own, d_all.at[0])]
    for copy in loads:
        copy.wait()
    left = lane_numbers() < HEAD_SIZE
    one = jnp.ones((), LOW)
    tail = jnp.zeros((wide_count - count, LANES), LOW)

    def project(group):
        weights = a_vm[group, 0:3].reshape(3 * 384, features)
        bias = b_vm[2 * group, 0:1, 0:1152] + b_vm[2 * group + 1, 0:1, 0:1152]
        for low, size in row_blocks(count):
            result = (nt(x_vm[low : low + size], weights) + bias).astype(LOW)
            for pair in range(3):
                place = 3 * group + pair
                at = LANES * pair
                q_out[place, low : low + size] = result[:, at : at + LANES] * 0.125
                k_out[place, low : low + size] = result[:, 384 + at : 384 + at + LANES]
                v_out[place, low : low + size] = result[:, 768 + at : 768 + at + LANES]
        for pair in range(3):
            place = 3 * group + pair
            q_out[place, count:] = tail
            k_out[place, count:] = tail
            v_out[place, count:] = tail

    def attend(group):
        def body(pair, carry):
            place = 3 * group + pair
            keys, values, key_marks = k_out[place], v_out[place], kf_ref[...]
            key_sides = [jnp.where(left, keys, key_marks), jnp.where(left, key_marks, keys)]
            value_sides = [jnp.where(left, values, one), jnp.where(left, one, values)]
            for low, size in row_blocks(count):
                begin, end = key_range(low, size, count)
                rows = q_out[place, low : low + size]
                marks = qf_ref[low : low + size]
                query_sides = [jnp.where(left, rows, marks), jnp.where(left, marks, rows)]
                scores = [
                    nt(query, key[begin:end]) for query, key in zip(query_sides, key_sides)
                ]
                if low + size == count:
                    scores = [add_corner(s, begin, corner_ref[...], low) for s in scores]
                largest = [jnp.max(s, axis=1, keepdims=True) for s in scores]
                weights = [jnp.exp(s - m).astype(LOW) for s, m in zip(scores, largest)]
                sums = [nn(w, v[begin:end]) for w, v in zip(weights, value_sides)]
                numerator = jnp.where(left, sums[0], sums[1])
                denominator = pltpu.roll(jnp.where(left, sums[1], sums[0]), HEAD_SIZE, 1)
                ctx_out[place, low : low + size] = numerator / denominator
                lse_out[place, low : low + size] = jnp.where(
                    left, largest[0], largest[1]
                ) + jnp.log(denominator)
            return carry

        lax.fori_loop(0, 3, body, 0)

    def mix(group):
        weights = a_vm[group, 3]
        for low, size in row_blocks(count):
            rows = jnp.concatenate(
                [ctx_out[3 * group + p, low : low + size].astype(LOW) for p in range(3)], axis=1
            )
            term = nn(rows, weights)
            if group == 0:
                acc[low : low + size] = term
            else:
                total = x_vm[low : low + size].astype(WIDE) + (acc[low : low + size] + term)
                mixed_out[low : low + size] = total + norm_ref[2:3]

    arrived(core[0])
    arrived(biases)
    start(core[1])
    start(core[2])
    project(0)
    attend(0)
    mix(0)
    arrived(across[0])
    start(along[0])
    start(first[0])
    sent(across[0])
    start(across[1])
    arrived(along[0])
    start(second[0])
    arrived(first[0])
    arrived(second[0])
    project(1)
    arrived(across[1])
    start(along[1])
    start(first[1])
    sent(across[1])
    start(across[2])
    attend(1)
    arrived(along[1])
    start(second[1])
    mix(1)
    b_all[...] = b_vm[...]
    keep = links.near(a_vm, a_all)
    arrived(across[2])
    start(along[2])
    start(first[2])
    arrived(along[2])
    start(second[2])
    for matrix in range(1, 3):
        arrived(core[matrix])
        arrived(first[matrix])
        arrived(second[matrix])
    for matrix in range(3):
        sent(core[matrix])
        sent(along[matrix])
        sent(first[matrix])
        sent(second[matrix])
    sent(across[2])
    sent(biases)
    for copy in later:
        copy.wait()
    keep.wait()


def normalize(values):
    centred = values - jnp.mean(values, axis=-1, keepdims=True)
    rate = lax.rsqrt(jnp.mean(centred * centred, axis=-1, keepdims=True) + EPSILON)
    return (centred * rate, rate)


def normalize_back(grad, unit, rate, gain):
    scaled = grad * gain
    inner = jnp.mean(scaled * unit, axis=-1, keepdims=True)
    return rate * (scaled - jnp.mean(scaled, axis=-1, keepdims=True) - unit * inner)


def row_sum(values):
    return jnp.sum(values, axis=0, keepdims=True)


def gelu_pair(values):
    phi = 0.5 * (1.0 + lax.erf(values * 0.7071067811865476))
    density = jnp.exp(-0.5 * values * values) * 0.3989422804014327
    return (values * phi, phi + values * density)


def feed_kernel(
    count,
    mixed_ref,
    cotangent,
    u_all,
    d_all,
    b_ref,
    norm_ref,
    out_all,
    dm_out,
    parts_out,
    small_out,
    u_vm,
    d_vm,
    act,
    slope,
    low_vm,
    low_t,
    grad_t,
    acc,
    dsecond,
    cot_vm,
    out_vm,
    upper,
    staged,
    landed,
    send_sems,
    recv_sems,
    local_sems,
):
    places = Places(0)
    links = Links(send_sems, recv_sems, local_sems)
    wide_count = padded(count)
    features = low_vm.shape[1]
    loads = []
    for number in range(4):
        loads.append(
            [
                links.near(u_all.at[number], u_vm.at[number]),
                links.near(d_all.at[number], d_vm.at[number]),
            ]
        )
    cot_load = links.near(cotangent.at[pl.ds(places.t * count, count)], cot_vm)
    places.greet([places.core, places.x])
    tail = jnp.zeros((wide_count - count, features), LOW)
    gain_one, gain_two = norm_ref[0:1], norm_ref[1:2]
    for low, size in row_blocks(count):
        unit, _ = normalize(mixed_ref[low : low + size])
        rows = unit * gain_one + norm_ref[4:5]
        low_vm[low : low + size] = rows.astype(LOW)
        acc[low : low + size] = rows + norm_ref[3:4]
    low_vm[count:] = tail
    upper[count:] = tail
    for copies in loads:
        for copy in copies:
            copy.wait()

    def ahead(number, carry):
        bias = b_ref[number, 0:1, 1152:1920]
        for low, size in row_blocks(count):
            upward = nn(low_vm[low : low + size], u_vm[number]) + bias
            value, rate = gelu_pair(upward)
            value = value.astype(LOW)
            act[number, low : low + size] = value
            slope[number, low : low + size] = rate.astype(LOW)
            acc[low : low + size] += nn(value, d_vm[number])
        act[number, count:] = tail
        return carry

    lax.fori_loop(0, 4, ahead, 0)
    cot_load.wait()
    sums = [jnp.zeros((1, features), WIDE) for _ in range(3)]
    for low, size in row_blocks(count):
        unit, rate = normalize(acc[low : low + size])
        out_vm[low : low + size] = (unit * gain_two + norm_ref[5:6]).astype(LOW)
        grad = cot_vm[low : low + size]
        back = normalize_back(grad, unit, rate, gain_two)
        dsecond[low : low + size] = back
        sums = [
            sums[0] + row_sum(grad * unit),
            sums[1] + row_sum(grad),
            sums[2] + row_sum(back),
        ]
    gain_two_sum, shift_two_sum, down_bias_sum = sums
    to_core = links.remote(out_vm, out_all.at[places.t], places.core)
    to_x = links.remote(out_vm, out_all.at[places.t], places.x)
    passed = links.remote(out_all.at[places.x[1]], out_all.at[places.x[1]], places.core)
    to_x.start()
    to_core.start()
    kept = links.near(out_vm, out_all.at[places.t])
    low_t[...] = low_vm[...].T
    second_low = acc
    for low, size in row_blocks(count):
        low_vm[low : low + size] = dsecond[low : low + size].astype(LOW)
    grad_t[...] = low_vm[...].T

    def back(number):
        total = jnp.zeros((1, features), WIDE)
        for low, size in row_blocks(count):
            inner = nt(low_vm[low : low + size], d_vm[number])
            rows = (slope[number, low : low + size].astype(WIDE) * inner).astype(LOW)
            upper[low : low + size] = rows
            total += row_sum(rows.astype(WIDE))
            dsecond[low : low + size] += nt(rows, u_vm[number])
        return total

    def grads(number, finish):
        for low, size in row_blocks(features):
            finish(0, low, size, nn(grad_t[low : low + size], act[number]))
            finish(1, low, size, nn(low_t[low : low + size], upper[...]))

    swaps = [
        [links.remote(staged.at[u, odd], landed.at[u, odd], places.core) for u in range(2)]
        for odd in range(2)
    ]

    def give(odd):
        def finish(unit, low, size, value):
            staged[unit, odd, low : low + size] = value.astype(LOW)

        return finish

    def take(even):
        def finish(unit, low, size, value):
            total = value + landed[unit, even, low : low + size].astype(WIDE)
            staged[unit, 2 + even, low : low + size] = total.astype(LOW)

        return finish

    up_bias = {}
    for odd, number in ((1, 3), (0, 1)):
        up_bias[number] = back(number)
        grads(number, give(odd))
        start(swaps[odd])
    stores = []
    for even, number in ((1, 2), (0, 0)):
        up_bias[number] = back(number)
        arrived(swaps[even])
        grads(number, take(even))
        for unit in range(2):
            stores.append(links.near(staged.at[unit, 2 + even], parts_out.at[unit, even]))
    sums = [jnp.zeros((1, features), WIDE) for _ in range(3)]
    for low, size in row_blocks(count):
        unit, rate = normalize(mixed_ref[low : low + size])
        grad = dsecond[low : low + size]
        back_rows = normalize_back(grad, unit, rate, gain_one)
        dm_out[low : low + size] = back_rows
        sums = [
            sums[0] + row_sum(grad * unit),
            sums[1] + row_sum(grad),
            sums[2] + row_sum(back_rows),
        ]
    gain_one_sum, shift_one_sum, out_bias_sum = sums
    small_out[...] = jnp.zeros_like(small_out)
    for place, number in ((0, 0), (1, 2), (3, 1), (4, 3)):
        small_out[place, 0:1] = up_bias[number]
    for place, row in enumerate(
        (gain_one_sum, gain_two_sum, out_bias_sum, down_bias_sum, shift_one_sum, shift_two_sum)
    ):
        small_out[2, place : place + 1] = row
    to_x.wait_recv()
    passed.start()
    to_core.wait()
    to_x.wait_send()
    passed.wait()
    kept.wait()
    for odd in range(2):
        sent(swaps[odd])
    for copy in stores:
        copy.wait()


class Stream:
    def __init__(self, bits, places, links, parts, buffers, out, columns, order):
        self.bits, self.places = bits, places
        self.parts, self.buffers, self.out = parts, buffers, out
        self.columns, self.order = columns, order
        self.sends = []
        for number, dim in enumerate(order):
            keep = self.fixed(number)
            device = places.x if dim == "x" else places.step[dim]
            copies = {}
            for slot in (1, 0) if number == 0 and dim != "x" else (None,):
                fixed = dict(keep)
                fixed[dim] = self.other(dim)
                target = buffers[number]
                if slot is not None:
                    fixed["x"] = slot
                    target = target.at[slot]
                copies[slot] = links.remote(self.view(fixed), target, device)
            self.sends.append(copies)

    def own(self, dim):
        return 0 if dim == "x" else self.places.bit[dim]

    def other(self, dim):
        return 1 if dim == "x" else 1 - self.places.bit[dim]

    def fixed(self, number):
        return {dim: self.own(dim) for dim in self.order[:number]}

    def index(self, fixed):
        dims = ["x"] + list(range(self.bits))[::-1]
        place = tuple(fixed.get(dim, slice(None)) for dim in dims)
        return place + (slice(None), pl.ds(self.columns[0], self.columns[1]))

    def view(self, fixed):
        return self.parts.at[self.index(fixed)]

    def begin(self, number, slots=None):
        for slot, copy in self.sends[number].items():
            if slots is None or slot in slots:
                copy.start()

    def finish(self, number):
        arrived(self.sends[number].values())
        keep = self.fixed(number + 1)
        rest = [dim for dim in ["x"] + list(range(self.bits))[::-1] if dim not in keep]
        buffer = self.buffers[number]
        for values in itertools.product(range(2), repeat=len(rest)):
            fixed = dict(keep)
            fixed.update(zip(rest, values))
            place = self.index(fixed)
            total = self.parts[place].astype(WIDE) + buffer[values].astype(WIDE)
            if rest:
                self.parts[place] = total.astype(LOW)
            else:
                self.out[:, self.columns[0] : self.columns[0] + self.columns[1]] = total

    def close(self):
        for copies in self.sends:
            sent(copies.values())


def stream_shapes(bits, rows, columns, order):
    dims = ["x"] + list(range(bits))[::-1]
    shapes = []
    for number in range(len(order)):
        rest = [dim for dim in dims if dim not in order[: number + 1]]
        shapes.append((2,) * len(rest) + (rows, columns))
    return shapes


def stream_plan(bits, features):
    high = tuple(range(2, bits))
    third = features // 3
    plan = [(0, (0, features), ("x", 0, 1) + high), (1, (0, features), (0, "x", 1) + high)]
    plan.append((2, (0, third), (0, 1, "x") + high))
    plan.append((2, (third, third), (1, 0, "x") + high))
    plan.append((2, (2 * third, third), (1, 0, "x") + high))
    return plan


def back_kernel(
    count,
    bits,
    plan,
    frames,
    parts_in,
    a_all,
    q_ref,
    k_ref,
    v_ref,
    ctx_ref,
    lse_ref,
    dm_ref,
    small_ref,
    qf_ref,
    kf_ref,
    corner_ref,
    frames_out,
    down_out,
    up_out,
    inward_out,
    small_out,
    parts,
    a_vm,
    x_vm,
    x_t,
    m_low,
    m_t,
    acc,
    own_out,
    grad_rows,
    grad_t,
    query_t,
    dk_t,
    dv_t,
    dqkv,
    ctx_low,
    even_wide,
    staged,
    landed,
    bias_sums,
    small,
    small_in,
    pair_vm,
    pair_in,
    *rest,
):
    buffers, (send_sems, recv_sems, local_sems) = rest[:-3], rest[-3:]
    places = Places(bits)
    links = Links(send_sems, recv_sems, local_sems)
    wide_count = padded(count)
    features = x_vm.shape[1]
    grid = parts.shape[1:-1]
    outs = (down_out, up_out, inward_out)
    streams, used = [], 0
    for unit, columns, order in plan:
        own_buffers = buffers[used : used + len(order)]
        used += len(order)
        streams.append(
            Stream(
                bits, places, links, parts.at[unit], own_buffers, outs[unit], columns, order
            )
        )
    part_loads = [links.near(parts_in.at[unit], parts.at[unit]) for unit in range(2)]
    x_load = links.near(frames.at[pl.ds(places.t * count, count)], x_vm.at[pl.ds(0, count)])
    a_load = links.near(a_all, a_vm)
    places.greet([places.core, places.x] + places.step)
    for unit in range(2):
        part_loads[unit].wait()
        streams[unit].begin(0)
    x_load.wait()
    tail = jnp.zeros((wide_count - count, features), LOW)
    x_vm[count:] = tail
    x_t[...] = x_vm[...].T
    for low, size in row_blocks(count):
        rows = dm_ref[low : low + size]
        acc[low : low + size] = rows
        m_low[low : low + size] = rows.astype(LOW)
    m_low[count:] = tail
    m_t[...] = m_low[...].T
    a_load.wait()
    lanes = lane_numbers()
    left = lanes < HEAD_SIZE
    mark = lanes % HEAD_SIZE
    ctx_low[count:] = jnp.zeros((wide_count - count, 384), LOW)
    dqkv[count:] = jnp.zeros((wide_count - count, 1152), LOW)
    value_marks = jnp.where(mark < 3, 1.0, 0.0).astype(LOW)

    def thirds(values):
        high = values.astype(LOW)
        rest_one = values - high.astype(WIDE)
        middle = rest_one.astype(LOW)
        return (high, middle, (rest_one - middle.astype(WIDE)).astype(LOW))

    def context_grads(group):
        for low, size in row_blocks(count):
            rows = nt(m_low[low : low + size], a_vm[group, 3]).astype(LOW)
            for pair in range(3):
                at = LANES * pair
                grad_rows[pair, low : low + size] = rows[:, at : at + LANES]
                ctx_low[low : low + size, at : at + LANES] = ctx_ref[
                    3 * group + pair, low : low + size
                ].astype(LOW)
        for pair in range(3):
            grad_rows[pair, count:] = jnp.zeros((wide_count - count, LANES), LOW)

    def attend(group):
        def body(pair, carry):
            place = 3 * group + pair
            keys, values, key_marks = k_ref[place], v_ref[place], kf_ref[...]
            key_sides = [jnp.where(left, keys, key_marks), jnp.where(left, key_marks, keys)]
            value_sides = [
                jnp.where(left, values, value_marks),
                jnp.where(left, value_marks, values),
            ]
            query_t[...] = q_ref[place].T
            grad_t[...] = grad_rows[pair].T
            at = pl.multiple_of(pair * LANES, LANES)
            query_sum = jnp.zeros((1, LANES), WIDE)
            for number, (low, size) in enumerate(row_blocks(count)):
                begin, end = key_range(low, size, count)
                rows = q_ref[place, low : low + size]
                total = pltpu.roll(lse_ref[place, low : low + size], HEAD_SIZE, 1)
                high, middle, rest_low = thirds(-total)
                marks = jnp.where(
                    mark == 6,
                    high,
                    jnp.where(
                        mark == 7,
                        middle,
                        jnp.where(mark == 8, rest_low, qf_ref[low : low + size]),
                    ),
                )
                query_sides = [jnp.where(left, rows, marks), jnp.where(left, marks, rows)]
                grad = grad_rows[pair, low : low + size]
                product = grad.astype(WIDE) * ctx_ref[place, low : low + size]
                inner_left = jnp.sum(jnp.where(left, product, 0.0), axis=1, keepdims=True)
                inner_right = jnp.sum(jnp.where(left, 0.0, product), axis=1, keepdims=True)
                high, middle, rest_low = thirds(-jnp.where(left, inner_right, inner_left))
                grad_marks = jnp.where(
                    mark == 0,
                    high,
                    jnp.where(
                        mark == 1, middle, jnp.where(mark == 2, rest_low, jnp.zeros((), LOW))
                    ),
                )
                grad_sides = [
                    jnp.where(left, grad, grad_marks),
                    jnp.where(left, grad_marks, grad),
                ]
                scores = [
                    nt(query, key[begin:end]) for query, key in zip(query_sides, key_sides)
                ]
                if low + size == count:
                    scores = [add_corner(s, begin, corner_ref[...], low) for s in scores]
                probs = [jnp.exp(s) for s in scores]
                prob_grads = [
                    nt(one, value[begin:end]) for one, value in zip(grad_sides, value_sides)
                ]
                probs_low = [p.astype(LOW) for p in probs]
                score_grads = [(p * g).astype(LOW) for p, g in zip(probs, prob_grads)]
                query_grads = [
                    nn(s, key[begin:end]) for s, key in zip(score_grads, key_sides)
                ]
                query_grad = (jnp.where(left, query_grads[0], query_grads[1]) * 0.125).astype(LOW)
                dqkv[low : low + size, pl.ds(at, LANES)] = query_grad
                query_sum += row_sum(query_grad.astype(WIDE))
                for side in range(2):
                    part = slice(HEAD_SIZE * side, HEAD_SIZE * side + HEAD_SIZE)
                    value_term = nn(grad_t[part, low : low + size], probs_low[side])
                    key_term = nn(query_t[part, low : low + size], score_grads[side])
                    if number == 0:
                        dv_t[part, begin:end] = value_term
                        dk_t[part, begin:end] = key_term
                        if end < wide_count:
                            blank = jnp.zeros((HEAD_SIZE, wide_count - end), WIDE)
                            dv_t[part, end:] = blank
                            dk_t[part, end:] = blank
                    else:
                        dv_t[part, begin:end] += value_term
                        dk_t[part, begin:end] += key_term
            key_grad = dk_t[...].astype(LOW).T
            value_grad = dv_t[...].astype(LOW).T
            dqkv[:, pl.ds(384 + at, LANES)] = key_grad
            dqkv[:, pl.ds(768 + at, LANES)] = value_grad
            bias_sums[pair, 0:1] = query_sum
            bias_sums[pair, 1:2] = row_sum(value_grad.astype(WIDE))
            return carry

        lax.fori_loop(0, 3, body, 0)

    def other_side(values):
        return pltpu.roll(values, HEAD_SIZE, 1)

    def packed(blocks, odd):
        outer = [b[2] if odd else b[0] for b in blocks]
        joined = []
        for one, two in zip(blocks[0::2], blocks[1::2]):
            if odd:
                joined.append(jnp.where(left, other_side(one[1]), two[1]))
            else:
                joined.append(jnp.where(left, one[1], other_side(two[1])))
        return jnp.concatenate(outer + joined, axis=1)

    def weight_grads(group):
        for low, size in row_blocks(features):
            inward = nn(x_t[low : low + size], dqkv[...])
            outward = nn(m_t[low : low + size], ctx_low[...])
            blocks = [
                [inward[:, 384 * kind + LANES * p : 384 * kind + LANES * (p + 1)] for p in range(3)]
                for kind in range(3)
            ]
            blocks.append([outward[:, LANES * p : LANES * (p + 1)] for p in range(3)])
            staged[group, low : low + size] = packed(blocks, True).astype(LOW)
            even_wide[low : low + size] = packed(blocks, False)

    def bias_grads(group):
        rows = [[bias_sums[p, kind : kind + 1] for p in range(3)] for kind in range(2)]
        for place, odd in ((1 if group else 0, False), (4 if group else 3, True)):
            small[place, 1:2, 0:384] = packed(rows, odd)

    def input_grads(group):
        weights = a_vm[group, 0:3].reshape(3 * 384, features)
        for low, size in row_blocks(count):
            acc[low : low + size] += nn(dqkv[low : low + size], weights)

    swaps = [links.remote(staged.at[g], landed.at[g], places.core) for g in range(2)]

    def combine(group):
        arrived([swaps[group]])
        for index in itertools.product(range(2), repeat=bits):
            block = sum(bit * 2 ** (bits - 1 - n) for n, bit in enumerate(index))
            rows = slice(block * grid[-1], (block + 1) * grid[-1])
            total = even_wide[rows] + landed[group, rows].astype(WIDE)
            parts[(2, group) + index] = total.astype(LOW)

    small[...] = small_ref[...]
    context_grads(1)
    attend(1)
    weight_grads(1)
    start([swaps[1]])
    bias_grads(1)
    streams[0].finish(0)
    streams[0].begin(1)
    streams[1].finish(0)
    streams[1].begin(1)
    input_grads(1)
    combine(1)
    for stream in streams[2:]:
        stream.begin(0, (1,))
    context_grads(0)
    attend(0)
    input_grads(0)
    for low, size in row_blocks(count):
        own_out[low : low + size] = acc[low : low + size].astype(LOW)
    to_core = links.remote(own_out, frames_out.at[places.t], places.core)
    to_x = links.remote(own_out, frames_out.at[places.t], places.x)
    passed = links.remote(frames_out.at[places.x[1]], frames_out.at[places.x[1]], places.core)
    to_x.start()
    to_core.start()
    kept = links.near(own_out, frames_out.at[places.t])
    weight_grads(0)
    start([swaps[0]])
    bias_grads(0)
    for number in (1, 2):
        for stream in streams[:2]:
            stream.finish(number)
            stream.begin(number + 1)
    combine(0)
    for stream in streams[2:]:
        stream.begin(0, (0,))
    small_core = links.remote(small.at[pl.ds(2, 3)], small_in.at[0], places.core)
    small_core.start()
    small_core.wait()
    small[2] += small_in[0, 0]
    small[0] += small_in[0, 1]
    small[1] += small_in[0, 2]
    small_x = links.remote(small.at[pl.ds(1, 2)], small_in.at[1, pl.ds(0, 2)], places.x)
    small_x.start()
    small_x.wait()
    pair_vm[0, 0] = small[0] + small_in[1, 0]
    pair_vm[0, 1] = small[2] + small_in[1, 1]
    small_steps = [
        links.remote(pair_vm.at[b], pair_in.at[b], places.step[b]) for b in range(bits)
    ]
    for b in range(bits):
        small_steps[b].start()
        small_steps[b].wait()
        pair_vm[b + 1] = pair_vm[b] + pair_in[b]
    small_out[...] = pair_vm[bits]
    depth = bits + 1
    for number in range(3, depth):
        for stream in streams[:2]:
            stream.finish(number)
            if number + 1 < depth:
                stream.begin(number + 1)
    for number in range(depth):
        for stream in streams[2:]:
            stream.finish(number)
            if number + 1 < depth:
                stream.begin(number + 1)
    to_x.wait_recv()
    passed.start()
    to_core.wait()
    to_x.wait_send()
    passed.wait()
    kept.wait()
    for stream in streams:
        stream.close()
    sent(swaps)


def anywhere():
    return pl.BlockSpec(memory_space=pl.ANY)


def inside():
    return pl.BlockSpec(memory_space=pltpu.VMEM)


def call(kernel, name, number, inputs, outputs, scratch, copies, near):
    semaphores = [
        pltpu.SemaphoreType.DMA((copies,)),
        pltpu.SemaphoreType.DMA((copies,)),
        pltpu.SemaphoreType.DMA((near,)),
    ]
    return pl.pallas_call(
        kernel,
        name=name,
        in_specs=[spec for spec, _ in inputs],
        out_specs=[spec for spec, _ in outputs],
        out_shape=[jax.ShapeDtypeStruct(shape, dtype) for _, (shape, dtype) in outputs],
        scratch_shapes=[pltpu.VMEM(shape, dtype) for shape, dtype in scratch] + semaphores,
        compiler_params=pltpu.CompilerParams(
            collective_id=number, has_side_effects=True, vmem_limit_bytes=VMEM_BYTES
        ),
    )(*[value for _, value in inputs])


def mask_marks(segments, valid, count):
    wide_count = padded(count)
    corner_start = row_blocks(count)[-1][0]
    lanes = jnp.arange(LANES)[None, :] % HEAD_SIZE
    rows = jnp.arange(count)[:, None]
    query = jnp.where(
        lanes < 4,
        jnp.where(segments[:, None] == lanes, 0.0, -FAR),
        jnp.where(
            (lanes == 4) | ((lanes == 5) & (rows < corner_start)), -FAR, 0.0
        ),
    )
    more = wide_count - count
    padded_segments = jnp.pad(segments, (0, more), constant_values=-1)[:, None]
    padded_valid = jnp.pad(valid, (0, more), constant_values=1)[:, None]
    keys = jnp.arange(wide_count)[:, None]
    key = jnp.where(
        lanes < 4,
        padded_segments == lanes,
        jnp.where(
            lanes == 4,
            keys >= count,
            jnp.where(lanes == 5, padded_valid == 0, (lanes >= 6) & (lanes < 9)),
        ),
    )
    corner_rows = jnp.arange(corner_start, count)[:, None]
    corner_keys = jnp.arange(corner_start, wide_count)[None, :]
    open_keys = jnp.pad(valid, (0, more))[None, corner_start:] > 0
    corner = jnp.where(open_keys | (corner_rows == corner_keys), 0.0, -FAR)
    return (query.astype(LOW), key.astype(LOW), corner.astype(WIDE))


def shards(
    bits,
    frames,
    segment_ids,
    valid_frames,
    inward_weight,
    inward_bias,
    output_weight,
    upward_weight,
    upward_bias,
    downward_weight,
    norm_gains,
    offsets,
    cotangent,
):
    place = lax.axis_index("tensor")
    dp_place = lax.axis_index("dp")
    features = frames.shape[1]
    count = segment_ids.shape[1]
    wide_count = padded(count)
    hidden = upward_weight.shape[2]
    rows = features // 2**bits
    segments = lax.dynamic_index_in_dim(segment_ids, place, 0, False)
    valid = lax.dynamic_index_in_dim(valid_frames, place, 0, False)
    query_marks, key_marks, corner = mask_marks(segments, valid, count)
    kinds = jnp.concatenate([jnp.swapaxes(inward_weight[0], 1, 2), output_weight], axis=0)
    p_own, h_own = kinds[:, :128], kinds[:, 128:]
    pair_bias = inward_bias[0].reshape(2, 192).astype(WIDE)
    nothing = jnp.zeros((192,), WIDE)
    swapped = jnp.concatenate([pair_bias[:, 128:], pair_bias[:, :128]], axis=1)
    empty = jnp.zeros((384,), WIDE)
    up_row = upward_bias[0].reshape(-1).astype(WIDE)
    b_own = jnp.stack(
        [
            jnp.concatenate([pair_bias[0], nothing, empty, pair_bias[1], nothing, up_row]),
            jnp.concatenate([nothing, swapped[0], empty, nothing, swapped[1], up_row]),
        ]
    )
    b_own = jnp.pad(b_own[:, None], ((0, 0), (0, 7), (0, 0)))
    norm_rows = jnp.concatenate(
        [norm_gains[0], offsets[0], jnp.zeros((2, features), WIDE)], axis=0
    )
    heads = ((6, wide_count, LANES), LOW)
    heads_wide = ((6, count, LANES), WIDE)
    whole = ((4, features, hidden), LOW)
    a_shape = ((2, 4, 384, features), LOW)
    b_shape = ((4, 8, 1920), WIDE)
    rows_wide = ((count, features), WIDE)
    rows_low = ((count, features), LOW)
    square = ((wide_count, features), LOW)
    a_all, u_all, d_all, b_all, q, k, v, ctx, lse, mixed = call(
        functools.partial(forward_kernel, count),
        "attention_forward",
        1,
        [
            (anywhere(), frames),
            (anywhere(), p_own),
            (anywhere(), h_own),
            (anywhere(), upward_weight[0]),
            (anywhere(), downward_weight[0]),
            (anywhere(), b_own),
            (inside(), query_marks),
            (inside(), key_marks),
            (inside(), corner),
            (inside(), norm_rows),
        ],
        [
            (anywhere(), a_shape),
            (anywhere(), whole),
            (anywhere(), whole),
            (inside(), b_shape),
            (inside(), heads),
            (inside(), heads),
            (inside(), heads),
            (inside(), heads_wide),
            (inside(), heads_wide),
            (inside(), rows_wide),
        ],
        [a_shape, b_shape, rows_low, rows_wide],
        32,
        8,
    )
    small_shape = ((5, 8, features), WIDE)
    parts_shape = ((2, 2, features, hidden), LOW)
    out_all, d_mixed, parts, small = call(
        functools.partial(feed_kernel, count),
        "feed_forward",
        2,
        [
            (inside(), mixed),
            (anywhere(), cotangent),
            (anywhere(), u_all),
            (anywhere(), d_all),
            (inside(), b_all),
            (inside(), norm_rows),
        ],
        [
            (anywhere(), ((4, count, features), LOW)),
            (inside(), rows_wide),
            (anywhere(), parts_shape),
            (inside(), small_shape),
        ],
        [
            whole,
            whole,
            ((4, wide_count, hidden), LOW),
            ((4, count, hidden), LOW),
            square,
            ((features, wide_count), LOW),
            ((features, wide_count), LOW),
            rows_wide,
            rows_wide,
            rows_wide,
            rows_low,
            ((wide_count, hidden), LOW),
            ((2, 4, features, hidden), LOW),
            ((2, 2, features, hidden), LOW),
        ],
        8,
        16,
    )
    plan = stream_plan(bits, features)
    grid = (2,) * bits + (rows,)
    buffers = []
    for _, columns, order in plan:
        buffers += [(shape, LOW) for shape in stream_shapes(bits, rows, columns[1], order)]
    own_chunk = ((rows, hidden), WIDE)
    frames_all, down_rows, up_rows, inward_rows, sums = call(
        functools.partial(back_kernel, count, bits, plan),
        "attention_backward",
        3,
        [
            (anywhere(), frames),
            (anywhere(), parts.reshape((2, 2) + grid + (hidden,))),
            (anywhere(), a_all),
            (inside(), q),
            (inside(), k),
            (inside(), v),
            (inside(), ctx),
            (inside(), lse),
            (inside(), d_mixed),
            (inside(), small),
            (inside(), query_marks),
            (inside(), key_marks),
            (inside(), corner),
        ],
        [
            (anywhere(), ((4, count, features), LOW)),
            (inside(), own_chunk),
            (inside(), own_chunk),
            (inside(), own_chunk),
            (inside(), ((2, 8, features), WIDE)),
        ],
        [
            ((3, 2) + grid + (hidden,), LOW),
            a_shape,
            square,
            ((features, wide_count), LOW),
            square,
            ((features, wide_count), LOW),
            rows_wide,
            rows_low,
            ((3, wide_count, LANES), LOW),
            ((LANES, wide_count), LOW),
            ((LANES, wide_count), LOW),
            ((LANES, wide_count), WIDE),
            ((LANES, wide_count), WIDE),
            ((wide_count, 1152), LOW),
            ((wide_count, 384), LOW),
            ((features, hidden), WIDE),
            ((2, features, hidden), LOW),
            ((2, features, hidden), LOW),
            ((3, 8, LANES), WIDE),
            small_shape,
            ((2, 3, 8, features), WIDE),
            ((bits + 1, 2, 8, features), WIDE),
            ((bits, 2, 8, features), WIDE),
        ]
        + buffers,
        64,
        8,
    )
    token_count = frames.shape[0]

    def own_part(values, axis):
        size = values.shape[axis] // 2**bits
        return lax.dynamic_slice_in_dim(values, dp_place * size, size, axis)

    def kind(number):
        outer = inward_rows[:, 128 * number : 128 * number + 128]
        inner = inward_rows[:, 512 + 64 * number : 576 + 64 * number]
        return jnp.concatenate([outer, inner], axis=1)

    bias_row = sums[0, 1]
    bias_sets = jnp.stack(
        [
            jnp.concatenate([bias_row[0:128], bias_row[256:320]]),
            jnp.concatenate([bias_row[128:256], bias_row[320:384]]),
        ]
    ).reshape(2, 3, HEAD_SIZE)
    return (
        out_all.reshape(token_count, features),
        frames_all.reshape(token_count, features).astype(WIDE),
        jnp.stack([kind(0), kind(1), kind(2)])[None],
        own_part(bias_sets, 2)[None],
        kind(3).T[None],
        up_rows[None],
        own_part(sums[0, 0].reshape(-1, 128), 1)[None],
        down_rows.T[None],
        own_part(sums[1, 0:2], 1)[None],
        own_part(sums[1, 2:6], 1)[None],
    )


def solution(mesh):
    bits = mesh.shape["dp"].bit_length() - 1
    in_specs = (
        P("dp", None),
        P("dp", None),
        P("dp", None),
        P(None, None, None, "tensor"),
        P(None, None, "tensor", None),
        P(None, "tensor", None),
        P(None, None, "tensor"),
        P(None, "tensor", None),
        P(None, "tensor", None),
        P(),
        P(),
        P("dp", None),
    )
    out_specs = (
        P("dp", None),
        P("dp", None),
        P(None, None, "dp", "tensor"),
        P(None, None, "tensor", "dp"),
        P(None, "tensor", "dp"),
        P(None, "dp", "tensor"),
        P(None, "tensor", "dp"),
        P(None, "tensor", "dp"),
        P(None, None, "dp"),
        P(None, None, "dp"),
    )
    return jax.shard_map(
        functools.partial(shards, bits),
        mesh=mesh,
        in_specs=in_specs,
        out_specs=out_specs,
        check_vma=False,
    )
```

```python
import functools
import itertools

import jax
import jax.numpy as jnp
from jax import lax
from jax.experimental import pallas as pl
from jax.experimental.pallas import tpu as pltpu
from jax.sharding import PartitionSpec as P

HEAD_SIZE = 64
LANES = 128
PAD = 128
LONGEST_CLIP_SHARE = 2
EPSILON = 1e-05
FAR = float(2**30)
LOW = jnp.bfloat16
WIDE = jnp.float32
MESH = pl.DeviceIdType.MESH
VMEM_BYTES = 127 << 19


def nn(left_side, right_side):
    return jnp.dot(left_side, right_side, preferred_element_type=WIDE)


def nt(left_side, right_side):
    return lax.dot_general(
        left_side, right_side, (((1,), (1,)), ((), ())), preferred_element_type=WIDE
    )


def padded(count):
    return -(-count // LANES) * LANES


def row_blocks(count, size=256):
    return [(start, min(size, count - start)) for start in range(0, count, size)]


def key_range(start, size, count):
    reach = count // LONGEST_CLIP_SHARE - 1
    low = max(0, (start - reach) // LANES * LANES)
    high = min(padded(count), padded(start + size + reach))
    return (low, high)


class Places:
    def __init__(self, bits):
        self.dp = lax.axis_index("dp")
        self.t = lax.axis_index("tensor")
        core = self.t % 2
        self.core = (self.dp, self.t + 1 - 2 * core)
        self.x = (self.dp, (self.t + 2) % 4)
        self.diagonal = (self.dp, 3 - self.t)
        self.bit = [(self.dp // 2**b) % 2 for b in range(bits)]
        self.step = [
            (self.dp + (1 - 2 * self.bit[b]) * 2**b, self.t) for b in range(bits)
        ]

    def greet(self, devices):
        barrier = pltpu.get_barrier_semaphore()
        for device in devices:
            pl.semaphore_signal(barrier, inc=1, device_id=device, device_id_type=MESH)
        pl.semaphore_wait(barrier, len(devices))


class Links:
    def __init__(self, send, recv, local):
        self.send, self.recv, self.local = send, recv, local
        self.used = self.used_local = 0

    def remote(self, source, target, device):
        place = self.used
        self.used += 1
        return pltpu.make_async_remote_copy(
            src_ref=source,
            dst_ref=target,
            send_sem=self.send.at[place],
            recv_sem=self.recv.at[place],
            device_id=device,
            device_id_type=MESH,
        )

    def near(self, source, target):
        place = self.used_local
        self.used_local += 1
        copy = pltpu.make_async_copy(source, target, self.local.at[place])
        copy.start()
        return copy


def start(copies):
    for copy in copies:
        copy.start()


def arrived(copies):
    for copy in copies:
        copy.wait_recv()


def sent(copies):
    for copy in copies:
        copy.wait_send()


def lane_numbers():
    return lax.broadcasted_iota(jnp.int32, (1, LANES), 1)


def add_corner(scores, low, corner, corner_start):
    cut = corner_start - low
    return jnp.concatenate([scores[:, :cut], scores[:, cut:] + corner], axis=1)


def forward_kernel(
    count,
    frames,
    w_own,
    o_own,
    u_own,
    d_own,
    pair_bias,
    up_bias,
    seg_ref,
    valid_ref,
    gain_ref,
    offset_ref,
    a_all,
    u_all,
    d_all,
    q_out,
    k_out,
    v_out,
    ctx_out,
    lse_out,
    mixed_out,
    b_out,
    qf_out,
    kf_out,
    corner_out,
    a_vm,
    b_vm,
    b_own,
    x_vm,
    w_vm,
    q_vm,
    k_vm,
    v_vm,
    ctx_vm,
    lse_vm,
    acc,
    row_vm,
    send_sems,
    recv_sems,
    local_sems,
):
    places = Places(2)
    links = Links(send_sems, recv_sems, local_sems)
    wide_count = padded(count)
    features = x_vm.shape[1]
    quarter_rows = features // 4
    w_load = links.near(w_own, w_vm)
    o_loads = [
        links.near(o_own.at[pl.ds(0, 128)], a_vm.at[0, 3, pl.ds(0, 128)]),
        links.near(o_own.at[pl.ds(128, 64)], a_vm.at[0, 3, pl.ds(128, 64)]),
    ]
    x_load = links.near(frames.at[pl.ds(places.t * count, count)], x_vm)

    def slot(matrix, number, quarter):
        if matrix == 0:
            kinds = pl.ds(0, 4) if quarter is None else pl.ds(quarter, 1)
            group, odd = number // 2, number % 2
            return [
                a_vm.at[group, kinds, pl.ds(256 if odd else 0, 128)],
                a_vm.at[group, kinds, pl.ds(192 if odd else 128, 64)],
            ]
        if number == 0:
            ref = u_own if matrix == 1 else d_own
        else:
            ref = (u_all if matrix == 1 else d_all).at[number - 1]
        if quarter is None:
            return [ref]
        return [ref.at[pl.ds(quarter * quarter_rows, quarter_rows)]]

    def remotes(source, target, device):
        return [links.remote(s, t, device) for s, t in zip(source, target)]

    class Gather:
        def __init__(self, matrix, one, two):
            flip = [1 - places.bit[0], 1 - places.bit[1]]

            def quarter(flips):
                low = flip[0] if 0 in flips else places.bit[0]
                high = flip[1] if 1 in flips else places.bit[1]
                return 2 * high + low

            def move(source, target, flips, device):
                return remotes(
                    slot(matrix, source, quarter(flips)),
                    slot(matrix, target, quarter(flips)),
                    device,
                )

            self.core = remotes(slot(matrix, 0, None), slot(matrix, 1, None), places.core)
            self.across = move(0, 2, (), places.x)
            self.one = move(2, 2, (), places.step[one])
            self.two = [
                move(2, 2, (), places.step[two]),
                move(2, 2, (one,), places.step[two]),
            ]
            self.passed = [
                move(2, 3, flips, places.core) for flips in ((), (one,), (two,), (one, two))
            ]

        def begin(self):
            start(self.across)

        def second(self):
            for n, copy in enumerate(self.across):
                copy.wait_recv()
                self.one[n].start()
                self.two[0][n].start()
                self.passed[0][n].start()

        def third(self):
            for n, copy in enumerate(self.one):
                copy.wait_recv()
                self.two[1][n].start()
                self.passed[1][n].start()

        def fourth(self):
            for number in range(2):
                for n, copy in enumerate(self.two[number]):
                    copy.wait_recv()
                    self.passed[2 + number][n].start()

        def ready(self):
            for copies in self.passed:
                arrived(copies)

        def close(self):
            for copies in [self.core, self.across, self.one] + self.two + self.passed:
                sent(copies)

    gathers = [Gather(0, 1, 0), Gather(1, 0, 1), Gather(2, 1, 0)]
    bias_copies = [
        links.remote(b_own.at[1], b_vm.at[1], places.core),
        links.remote(b_own.at[0], b_vm.at[2], places.x),
        links.remote(b_own.at[1], b_vm.at[3], places.diagonal),
    ]
    identity = (
        lax.broadcasted_iota(jnp.int32, (192, 192), 0)
        == lax.broadcasted_iota(jnp.int32, (192, 192), 1)
    ).astype(LOW)
    w_load.wait()
    for kind in range(3):
        turned = nt(identity, w_vm[kind]).astype(LOW)
        a_vm[0, kind, 0:192] = turned
    for copy in o_loads:
        copy.wait()
    places.greet([places.core, places.x, places.diagonal] + places.step)
    gathers[0].begin()
    start(gathers[0].core)
    left = lane_numbers() < HEAD_SIZE
    one = jnp.ones((), LOW)
    b_own[...] = jnp.zeros_like(b_own)
    for kind, at in ((0, 0), (1, 768)):
        heads = [pair_bias[kind, h : h + 1].astype(WIDE) for h in range(3)]
        blank = jnp.zeros_like(heads[0])
        first_pair = jnp.concatenate([heads[0], heads[1]], axis=1)
        b_own[0, 0:1, at : at + 128] = first_pair
        b_own[0, 0:1, at + 128 : at + 256] = jnp.concatenate([heads[2], blank], axis=1)
        b_own[1, 0:1, at + 128 : at + 256] = jnp.concatenate([blank, heads[2]], axis=1)
        b_own[1, 0:1, at + 256 : at + 384] = first_pair
    for line in range(up_bias.shape[0]):
        at = 1152 + LANES * line
        row = up_bias[line : line + 1].astype(WIDE)
        b_own[0, 0:1, at : at + LANES] = row
        b_own[1, 0:1, at : at + LANES] = row
    start(bias_copies)
    b_vm[0] = b_own[0]
    row_vm[0:8] = jnp.full((8, wide_count), -1, jnp.int32)
    row_vm[8:16] = jnp.zeros((8, wide_count), jnp.int32)
    row_vm[0:1, 0:count] = seg_ref[pl.ds(places.t, 1)]
    row_vm[8:9, 0:count] = valid_ref[pl.ds(places.t, 1)]
    corner_start = row_blocks(count)[-1][0]
    segments = jnp.broadcast_to(row_vm[0:1], (LANES, wide_count))
    valid = jnp.broadcast_to(row_vm[8:9], (LANES, wide_count))
    mark = lax.broadcasted_iota(jnp.int32, (LANES, wide_count), 0) % HEAD_SIZE
    frame = lax.broadcasted_iota(jnp.int32, (LANES, wide_count), 1)
    same = segments == mark
    query_marks = jnp.where(
        mark < 4,
        jnp.where(same, 0.0, -FAR),
        jnp.where(
            mark == 4,
            -FAR,
            jnp.where(mark == 5, jnp.where(frame < corner_start, -FAR, 0.0), 0.0),
        ),
    )
    key_marks_t = jnp.where(
        mark < 4,
        jnp.where(same, 1.0, 0.0),
        jnp.where(
            mark == 4,
            jnp.where(frame >= count, 1.0, 0.0),
            jnp.where(
                mark == 5,
                jnp.where(valid > 0, 0.0, 1.0),
                jnp.where(mark < 9, 1.0, 0.0),
            ),
        ),
    )
    qf_out[...] = query_marks.astype(LOW).T
    kf_out[...] = key_marks_t.astype(LOW).T
    corner_shape = (count - corner_start, wide_count - corner_start)
    open_keys = jnp.broadcast_to(row_vm[8:9, corner_start:], corner_shape) > 0
    itself = lax.broadcasted_iota(jnp.int32, corner_shape, 0) == lax.broadcasted_iota(
        jnp.int32, corner_shape, 1
    )
    corner_out[...] = jnp.where(open_keys | itself, 0.0, -FAR)
    tail = jnp.zeros((wide_count - count, features), LOW)
    q_vm[count:] = tail
    k_vm[count:] = tail
    v_vm[count:] = tail
    x_load.wait()

    def project(group):
        weights = a_vm[group, 0:3].reshape(3 * 384, features)
        bias = b_vm[2 * group, 0:1, 0:1152] + b_vm[2 * group + 1, 0:1, 0:1152]
        at = 384 * group
        for low, size in row_blocks(count):
            result = (nt(x_vm[low : low + size], weights) + bias).astype(LOW)
            q_vm[low : low + size, at : at + 384] = result[:, 0:384] * 0.125
            k_vm[low : low + size, at : at + 384] = result[:, 384:768]
            v_vm[low : low + size, at : at + 384] = result[:, 768:1152]

    def attend(first, last):
        def body(pair, carry):
            at = pl.ds(pl.multiple_of(pair * LANES, LANES), LANES)
            keys, values, key_marks = k_vm[:, at], v_vm[:, at], kf_out[...]
            key_sides = [jnp.where(left, keys, key_marks), jnp.where(left, key_marks, keys)]
            value_sides = [jnp.where(left, values, one), jnp.where(left, one, values)]
            for low, size in row_blocks(count):
                begin, end = key_range(low, size, count)
                rows = q_vm[low : low + size, at]
                marks = qf_out[low : low + size]
                query_sides = [jnp.where(left, rows, marks), jnp.where(left, marks, rows)]
                scores = [
                    nt(query, key[begin:end]) for query, key in zip(query_sides, key_sides)
                ]
                if low + size == count:
                    scores = [add_corner(s, begin, corner_out[...], low) for s in scores]
                largest = [jnp.max(s, axis=1, keepdims=True) for s in scores]
                weights = [jnp.exp(s - m).astype(LOW) for s, m in zip(scores, largest)]
                sums = [nn(w, v[begin:end]) for w, v in zip(weights, value_sides)]
                numerator = jnp.where(left, sums[0], sums[1])
                denominator = pltpu.roll(jnp.where(left, sums[1], sums[0]), HEAD_SIZE, 1)
                ctx_vm[low : low + size, at] = numerator / denominator
                lse_vm[low : low + size, at] = jnp.where(
                    left, largest[0], largest[1]
                ) + jnp.log(denominator)
            return carry

        lax.fori_loop(first, last, body, 0)

    def mix(group):
        weights = a_vm[group, 3]
        at = 384 * group
        for low, size in row_blocks(count):
            term = nn(ctx_vm[low : low + size, at : at + 384].astype(LOW), weights)
            if group == 0:
                acc[low : low + size] = x_vm[low : low + size].astype(WIDE) + term
            else:
                acc[low : low + size] += term + offset_ref[0:1]

    stores = []
    arrived(gathers[0].core)
    arrived(bias_copies)
    start(gathers[1].core)
    project(0)
    gathers[0].second()
    gathers[1].begin()
    attend(0, 1)
    gathers[0].third()
    start(gathers[2].core)
    attend(1, 3)
    gathers[0].fourth()
    gathers[1].second()
    gathers[2].begin()
    mix(0)
    gathers[0].ready()
    stores.append(links.near(a_vm, a_all))
    project(1)
    for source, target in ((q_vm, q_out), (k_vm, k_out), (v_vm, v_out)):
        stores.append(links.near(source, target))
    gathers[1].third()
    gathers[2].second()
    attend(3, 5)
    gathers[1].fourth()
    gathers[2].third()
    attend(5, 6)
    stores.append(links.near(ctx_vm, ctx_out))
    stores.append(links.near(lse_vm, lse_out))
    mix(1)
    stores.append(links.near(acc, mixed_out))
    b_out[...] = b_vm[...]
    gathers[2].fourth()
    for gather in gathers[1:]:
        arrived(gather.core)
        gather.ready()
    for gather in gathers:
        gather.close()
    sent(bias_copies)
    for copy in stores:
        copy.wait()


def normalize(values):
    centred = values - jnp.mean(values, axis=-1, keepdims=True)
    rate = lax.rsqrt(jnp.mean(centred * centred, axis=-1, keepdims=True) + EPSILON)
    return (centred * rate, rate)


def normalize_back(grad, unit, rate, gain):
    scaled = grad * gain
    inner = jnp.mean(scaled * unit, axis=-1, keepdims=True)
    return rate * (scaled - jnp.mean(scaled, axis=-1, keepdims=True) - unit * inner)


def row_sum(values):
    return jnp.sum(values, axis=0, keepdims=True)


def gelu_pair(values):
    phi = 0.5 * (1.0 + lax.erf(values * 0.7071067811865476))
    density = jnp.exp(-0.5 * values * values) * 0.3989422804014327
    return (values * phi, phi + values * density)


class Stream:
    def __init__(self, bits, places, links, parts, buffers, out, columns, order):
        self.bits, self.places = bits, places
        self.parts, self.buffers, self.out = parts, buffers, out
        self.columns, self.order = columns, order
        self.sends = []
        for number, dim in enumerate(order):
            keep = self.fixed(number)
            device = places.x if dim == "x" else places.step[dim]
            copies = {}
            for slot in (1, 0) if number == 0 and dim != "x" else (None,):
                fixed = dict(keep)
                fixed[dim] = self.other(dim)
                target = buffers[number]
                if slot is not None:
                    fixed["x"] = slot
                    target = target.at[slot]
                copies[slot] = links.remote(self.view(fixed), target, device)
            self.sends.append(copies)

    def own(self, dim):
        return 0 if dim == "x" else self.places.bit[dim]

    def other(self, dim):
        return 1 if dim == "x" else 1 - self.places.bit[dim]

    def fixed(self, number):
        return {dim: self.own(dim) for dim in self.order[:number]}

    def index(self, fixed):
        dims = ["x"] + list(range(self.bits))[::-1]
        place = tuple(fixed.get(dim, slice(None)) for dim in dims)
        return place + (slice(None), pl.ds(self.columns[0], self.columns[1]))

    def view(self, fixed):
        return self.parts.at[self.index(fixed)]

    def begin(self, number, slots=None):
        for slot, copy in self.sends[number].items():
            if slots is None or slot in slots:
                copy.start()

    def finish(self, number):
        arrived(self.sends[number].values())
        keep = self.fixed(number + 1)
        rest = [dim for dim in ["x"] + list(range(self.bits))[::-1] if dim not in keep]
        buffer = self.buffers[number]
        for values in itertools.product(range(2), repeat=len(rest)):
            fixed = dict(keep)
            fixed.update(zip(rest, values))
            place = self.index(fixed)
            total = self.parts[place].astype(WIDE) + buffer[values].astype(WIDE)
            if rest:
                self.parts[place] = total.astype(LOW)
            else:
                self.out[:, self.columns[0] : self.columns[0] + self.columns[1]] = total

    def close(self):
        for copies in self.sends:
            sent(copies.values())


def stream_shapes(bits, rows, columns, order):
    dims = ["x"] + list(range(bits))[::-1]
    shapes = []
    for number in range(len(order)):
        rest = [dim for dim in dims if dim not in order[: number + 1]]
        shapes.append((2,) * len(rest) + (rows, columns))
    return shapes


def stream_plan(bits, features):
    high = tuple(range(2, bits))
    third = features // 3
    plan = [(0, (0, features), ("x", 0, 1) + high), (1, (0, features), (0, 1) + high + ("x",))]
    plan.append((2, (0, third), (0, 1, "x") + high))
    plan.append((2, (third, third), (1, 0, "x") + high))
    plan.append((2, (2 * third, third), (1, 0, "x") + high))
    return plan


def back_kernel(
    count,
    bits,
    plan,
    frames,
    cotangent,
    mixed,
    u_own,
    d_own,
    u_all,
    d_all,
    a_all,
    q_in,
    k_in,
    v_in,
    ctx_in,
    lse_in,
    b_ref,
    gain_ref,
    offset_ref,
    qf_ref,
    kf_ref,
    corner_ref,
    out_all,
    frames_out,
    down_out,
    up_out,
    inward_out,
    small_out,
    w_vm,
    act,
    slope,
    low_vm,
    low_t,
    grad_t,
    upper,
    grads_vm,
    acc,
    dsecond,
    cot_vm,
    parts,
    staged,
    landed,
    query_t,
    pair_grad_t,
    dk_t,
    dv_t,
    bias_sums,
    small,
    small_in,
    pair_vm,
    pair_in,
    *rest,
):
    buffers, (send_sems, recv_sems, local_sems) = rest[:-3], rest[-3:]
    places = Places(bits)
    links = Links(send_sems, recv_sems, local_sems)
    wide_count = padded(count)
    features = low_vm.shape[1]
    frames_at = pl.ds(0, count)
    mixed_vm = dsecond
    mixed_load = links.near(mixed, mixed_vm.at[frames_at])
    loads = []
    for number in range(4):
        u_from = u_own if number == 0 else u_all.at[number - 1]
        d_from = d_own if number == 0 else d_all.at[number - 1]
        loads.append(
            [links.near(u_from, w_vm.at[number]), links.near(d_from, w_vm.at[4 + number])]
        )
    cot_load = links.near(
        cotangent.at[pl.ds(places.t * count, count)], cot_vm.at[frames_at]
    )
    places.greet([places.core, places.x] + places.step)
    grid = parts.shape[2:-1]
    outs = (down_out, up_out, inward_out)
    streams, used = [], 0
    for unit, columns, order in plan:
        own_buffers = buffers[used : used + len(order)]
        used += len(order)
        streams.append(
            Stream(
                bits, places, links, parts.at[unit], own_buffers, outs[unit], columns, order
            )
        )
    tail = jnp.zeros((wide_count - count, features), LOW)
    gain_one, gain_two = gain_ref[0:1], gain_ref[1:2]
    mixed_load.wait()
    for low, size in row_blocks(count):
        unit, _ = normalize(mixed_vm[low : low + size])
        rows = unit * gain_one + offset_ref[2:3]
        low_vm[low : low + size] = rows.astype(LOW)
        acc[low : low + size] = rows + offset_ref[1:2]
    low_vm[count:] = tail
    upper[count:] = tail
    for copies in loads:
        for copy in copies:
            copy.wait()

    def ahead(number, carry):
        bias = b_ref[number, 0:1, 1152:1920]
        for low, size in row_blocks(count):
            upward = nn(low_vm[low : low + size], w_vm[number]) + bias
            value, rate = gelu_pair(upward)
            value = value.astype(LOW)
            act[number, low : low + size] = value
            slope[number, low : low + size] = rate.astype(LOW)
            acc[low : low + size] += nn(value, w_vm[4 + number])
        act[number, count:] = tail
        return carry

    lax.fori_loop(0, 4, ahead, 0)
    cot_load.wait()
    sums = [jnp.zeros((1, features), WIDE) for _ in range(3)]
    out_vm = grads_vm
    for low, size in row_blocks(count):
        unit, rate = normalize(acc[low : low + size])
        out_vm[low : low + size] = (unit * gain_two + offset_ref[3:4]).astype(LOW)
        grad = cot_vm[low : low + size]
        back = normalize_back(grad, unit, rate, gain_two)
        acc[low : low + size] = back
        sums = [
            sums[0] + row_sum(grad * unit),
            sums[1] + row_sum(grad),
            sums[2] + row_sum(back),
        ]
    gain_two_sum, shift_two_sum, down_bias_sum = sums

    class Spread:
        def __init__(self, source, target):
            own = target.at[places.t]
            self.to_core = links.remote(source.at[frames_at], own, places.core)
            self.to_x = links.remote(source.at[frames_at], own, places.x)
            beside = target.at[places.x[1]]
            self.passed = links.remote(beside, beside, places.core)
            self.to_x.start()
            self.to_core.start()
            self.kept = links.near(source.at[frames_at], own)

        def hand_on(self):
            self.to_x.wait_recv()
            self.passed.start()

        def source_free(self):
            self.to_core.wait_send()
            self.to_x.wait_send()
            self.kept.wait()

        def close(self):
            self.to_core.wait_recv()
            self.passed.wait()

    out_spread = Spread(out_vm, out_all)
    low_t[...] = low_vm[...].T
    for low, size in row_blocks(count):
        low_vm[low : low + size] = acc[low : low + size].astype(LOW)
    grad_t[...] = low_vm[...].T

    def back(number):
        total = jnp.zeros((1, features), WIDE)
        for low, size in row_blocks(count):
            inner = nt(low_vm[low : low + size], w_vm[4 + number])
            rows = (slope[number, low : low + size].astype(WIDE) * inner).astype(LOW)
            upper[low : low + size] = rows
            total += row_sum(rows.astype(WIDE))
            acc[low : low + size] += nt(rows, w_vm[number])
        return total

    def grads(number, finish):
        for low, size in row_blocks(features):
            finish(0, low, size, nn(grad_t[low : low + size], act[number]))
            finish(1, low, size, nn(low_t[low : low + size], upper[...]))

    swaps = [
        [links.remote(staged.at[u], landed.at[u, odd], places.core) for u in range(2)]
        for odd in range(2)
    ]
    chunk = grid[-1]
    indices = list(itertools.product(range(2), repeat=bits))

    def put(unit, even, low, value):
        for place, index in enumerate(indices):
            begin = place * chunk
            if low <= begin and begin + chunk <= low + value.shape[0]:
                parts[(unit, even) + index] = value[begin - low : begin - low + chunk]
            elif low <= begin < low + value.shape[0]:
                cut = low + value.shape[0] - begin
                parts[(unit, even) + index + (slice(0, cut),)] = value[begin - low :]
            elif begin < low < begin + chunk:
                cut = low - begin
                parts[(unit, even) + index + (slice(cut, chunk),)] = value[: chunk - cut]

    def give(unit, low, size, value):
        staged[unit, low : low + size] = value.astype(LOW)

    def take(even):
        def finish(unit, low, size, value):
            total = value + landed[unit, even, low : low + size].astype(WIDE)
            put(unit, even, low, total.astype(LOW))

        return finish

    up_bias = {}
    up_bias[3] = back(3)
    grads(3, give)
    start(swaps[1])
    up_bias[1] = back(1)
    sent(swaps[1])
    grads(1, give)
    start(swaps[0])
    up_bias[2] = back(2)
    arrived(swaps[1])
    grads(2, take(1))
    streams[0].begin(0)
    streams[1].begin(0, (1,))
    up_bias[0] = back(0)
    arrived(swaps[0])
    a_load = links.near(a_all, w_vm.at[pl.ds(0, 4)])
    grads(0, take(0))
    streams[1].begin(0, (0,))
    sent(swaps[0])
    x_load = links.near(frames.at[pl.ds(places.t * count, count)], upper.at[frames_at])
    head_loads = [
        links.near(source, act.at[n]) for n, source in enumerate((q_in, k_in, v_in))
    ]
    ctx_load = links.near(ctx_in, cot_vm.at[frames_at])
    sums = [jnp.zeros((1, features), WIDE) for _ in range(3)]
    for low, size in row_blocks(count):
        unit, rate = normalize(mixed_vm[low : low + size])
        grad = acc[low : low + size]
        back_rows = normalize_back(grad, unit, rate, gain_one)
        acc[low : low + size] = back_rows
        low_vm[low : low + size] = back_rows.astype(LOW)
        sums = [
            sums[0] + row_sum(grad * unit),
            sums[1] + row_sum(grad),
            sums[2] + row_sum(back_rows),
        ]
    gain_one_sum, shift_one_sum, out_bias_sum = sums
    lse_vm = dsecond
    lse_load = links.near(lse_in, lse_vm.at[frames_at])
    small[...] = jnp.zeros_like(small)
    for place, number in ((0, 0), (1, 2), (3, 1), (4, 3)):
        small[place, 0:1] = up_bias[number]
    for place, row in enumerate(
        (gain_one_sum, gain_two_sum, out_bias_sum, down_bias_sum, shift_one_sum, shift_two_sum)
    ):
        small[2, place : place + 1] = row
    m_low, m_t, x_vm, x_t = low_vm, low_t, upper, grad_t
    m_t[...] = m_low[...].T
    x_load.wait()
    x_t[...] = x_vm[...].T
    out_spread.source_free()
    a_load.wait()
    ctx_load.wait()
    ctx_vm = cot_vm
    lanes = lane_numbers()
    left = lanes < HEAD_SIZE
    mark = lanes % HEAD_SIZE
    value_marks = jnp.where(mark < 3, 1.0, 0.0).astype(LOW)
    grads_vm[count:] = tail
    for number in range(4):
        slope[number, count:] = tail
    for group in range(2):
        for low, size in row_blocks(count):
            at = 384 * group
            rows = nt(m_low[low : low + size], w_vm[2 * group + 1, 384:768])
            grads_vm[low : low + size, at : at + 384] = rows.astype(LOW)
            slope[2 + group, low : low + size, 384:768] = ctx_vm[
                low : low + size, at : at + 384
            ].astype(LOW)
    for copy in head_loads:
        copy.wait()
    lse_load.wait()

    def thirds(values):
        high = values.astype(LOW)
        rest_one = values - high.astype(WIDE)
        middle = rest_one.astype(LOW)
        return (high, middle, (rest_one - middle.astype(WIDE)).astype(LOW))

    def attend(group, first, last):
        def body(pair, carry):
            at = pl.ds(pl.multiple_of((3 * group + pair) * LANES, LANES), LANES)
            at_query = pl.ds(pl.multiple_of(pair * LANES, LANES), LANES)
            at_key = pl.ds(pl.multiple_of(384 + pair * LANES, LANES), LANES)
            keys, values, key_marks = act[1, :, at], act[2, :, at], kf_ref[...]
            key_sides = [jnp.where(left, keys, key_marks), jnp.where(left, key_marks, keys)]
            value_sides = [
                jnp.where(left, values, value_marks),
                jnp.where(left, value_marks, values),
            ]
            query_t[...] = act[0, :, at].T
            pair_grad_t[...] = grads_vm[:, at].T
            query_sum = jnp.zeros((1, LANES), WIDE)
            for number, (low, size) in enumerate(row_blocks(count)):
                begin, end = key_range(low, size, count)
                rows = act[0, low : low + size, at]
                total = pltpu.roll(lse_vm[low : low + size, at], HEAD_SIZE, 1)
                high, middle, rest_low = thirds(-total)
                marks = jnp.where(
                    mark == 6,
                    high,
                    jnp.where(
                        mark == 7,
                        middle,
                        jnp.where(mark == 8, rest_low, qf_ref[low : low + size]),
                    ),
                )
                query_sides = [jnp.where(left, rows, marks), jnp.where(left, marks, rows)]
                grad = grads_vm[low : low + size, at]
                product = grad.astype(WIDE) * ctx_vm[low : low + size, at]
                inner_left = jnp.sum(jnp.where(left, product, 0.0), axis=1, keepdims=True)
                inner_right = jnp.sum(jnp.where(left, 0.0, product), axis=1, keepdims=True)
                high, middle, rest_low = thirds(-jnp.where(left, inner_right, inner_left))
                grad_marks = jnp.where(
                    mark == 0,
                    high,
                    jnp.where(
                        mark == 1, middle, jnp.where(mark == 2, rest_low, jnp.zeros((), LOW))
                    ),
                )
                grad_sides = [
                    jnp.where(left, grad, grad_marks),
                    jnp.where(left, grad_marks, grad),
                ]
                scores = [
                    nt(query, key[begin:end]) for query, key in zip(query_sides, key_sides)
                ]
                if low + size == count:
                    scores = [add_corner(s, begin, corner_ref[...], low) for s in scores]
                probs = [jnp.exp(s) for s in scores]
                prob_grads = [
                    nt(one, value[begin:end]) for one, value in zip(grad_sides, value_sides)
                ]
                probs_low = [p.astype(LOW) for p in probs]
                score_grads = [(p * g).astype(LOW) for p, g in zip(probs, prob_grads)]
                query_grads = [
                    nn(s, key[begin:end]) for s, key in zip(score_grads, key_sides)
                ]
                query_grad = (jnp.where(left, query_grads[0], query_grads[1]) * 0.125).astype(LOW)
                slope[group, low : low + size, at_query] = query_grad
                query_sum += row_sum(query_grad.astype(WIDE))
                for side in range(2):
                    part = slice(HEAD_SIZE * side, HEAD_SIZE * side + HEAD_SIZE)
                    value_term = nn(pair_grad_t[part, low : low + size], probs_low[side])
                    key_term = nn(query_t[part, low : low + size], score_grads[side])
                    if number == 0:
                        dv_t[part, begin:end] = value_term
                        dk_t[part, begin:end] = key_term
                        if end < wide_count:
                            blank = jnp.zeros((HEAD_SIZE, wide_count - end), WIDE)
                            dv_t[part, end:] = blank
                            dk_t[part, end:] = blank
                    else:
                        dv_t[part, begin:end] += value_term
                        dk_t[part, begin:end] += key_term
            key_grad = dk_t[...].astype(LOW).T
            value_grad = dv_t[...].astype(LOW).T
            slope[group, :, at_key] = key_grad
            slope[2 + group, :, at_query] = value_grad
            bias_sums[pair, 0:1] = query_sum
            bias_sums[pair, 1:2] = row_sum(value_grad.astype(WIDE))
            return carry

        lax.fori_loop(first, last, body, 0)

    def other_side(values):
        return pltpu.roll(values, HEAD_SIZE, 1)

    def packed(blocks, odd):
        outer = [b[2] if odd else b[0] for b in blocks]
        joined = []
        for one, two in zip(blocks[0::2], blocks[1::2]):
            if odd:
                joined.append(jnp.where(left, other_side(one[1]), two[1]))
            else:
                joined.append(jnp.where(left, one[1], other_side(two[1])))
        return jnp.concatenate(outer + joined, axis=1)

    def split(values):
        return [values[:, LANES * p : LANES * (p + 1)] for p in range(3)]

    def weight_grads(group):
        for low, size in row_blocks(features):
            pair = nn(x_t[low : low + size], slope[group])
            value = nn(x_t[low : low + size], slope[2 + group, :, 0:384])
            outward = nn(m_t[low : low + size], slope[2 + group, :, 384:768])
            blocks = [split(pair[:, :384]), split(pair[:, 384:]), split(value), split(outward)]
            staged[group, low : low + size] = packed(blocks, True).astype(LOW)
            put(2, group, low, packed(blocks, False).astype(LOW))

    def bias_grads(group):
        rows = [[bias_sums[p, kind : kind + 1] for p in range(3)] for kind in range(2)]
        for place, odd in ((1 if group else 0, False), (4 if group else 3, True)):
            small[place, 1:2, 0:384] = packed(rows, odd)

    def input_grads(group):
        for low, size in row_blocks(count):
            acc[low : low + size] += nn(slope[group, low : low + size], w_vm[2 * group]) + nn(
                slope[2 + group, low : low + size, 0:384], w_vm[2 * group + 1, 0:384]
            )

    last_swaps = [links.remote(staged.at[g], landed.at[2, g], places.core) for g in range(2)]

    def combine(group):
        arrived([last_swaps[group]])
        for place, index in enumerate(indices):
            rows = slice(place * chunk, (place + 1) * chunk)
            total = parts[(2, group) + index].astype(WIDE) + landed[2, group, rows].astype(WIDE)
            parts[(2, group) + index] = total.astype(LOW)

    depth = bits + 1

    def advance(stream, number):
        stream.finish(number)
        if number + 1 < depth:
            stream.begin(number + 1)

    out_spread.hand_on()
    attend(1, 0, 3)
    weight_grads(1)
    start([last_swaps[1]])
    bias_grads(1)
    input_grads(1)
    combine(1)
    for stream in streams[2:]:
        stream.begin(0, (1,))
    attend(0, 0, 1)
    advance(streams[1], 0)
    attend(0, 1, 2)
    advance(streams[0], 0)
    attend(0, 2, 3)
    input_grads(0)
    out_spread.close()
    own_out = grads_vm
    for low, size in row_blocks(count):
        own_out[low : low + size] = acc[low : low + size].astype(LOW)
    frames_spread = Spread(own_out, frames_out)
    weight_grads(0)
    start([last_swaps[0]])
    bias_grads(0)
    small_core = links.remote(small.at[pl.ds(2, 3)], small_in.at[0], places.core)
    small_core.start()
    combine(0)
    for stream in streams[2:]:
        stream.begin(0, (0,))
    small_core.wait()
    small[2] += small_in[0, 0]
    small[0] += small_in[0, 1]
    small[1] += small_in[0, 2]
    small_x = links.remote(small.at[pl.ds(1, 2)], small_in.at[1, pl.ds(0, 2)], places.x)
    small_x.start()
    advance(streams[1], 1)
    advance(streams[0], 1)
    small_x.wait()
    pair_vm[0, 0] = small[0] + small_in[1, 0]
    pair_vm[0, 1] = small[2] + small_in[1, 1]
    small_steps = [
        links.remote(pair_vm.at[b], pair_in.at[b], places.step[b]) for b in range(bits)
    ]
    small_steps[0].start()
    for number in range(depth):
        for stream in streams[2:]:
            advance(stream, number)
        if number < bits:
            small_steps[number].wait()
            pair_vm[number + 1] = pair_vm[number] + pair_in[number]
            if number + 1 < bits:
                small_steps[number + 1].start()
        if number + 2 < depth:
            advance(streams[1], number + 2)
            advance(streams[0], number + 2)
    small_out[...] = pair_vm[bits]
    frames_spread.hand_on()
    frames_spread.source_free()
    frames_spread.close()
    for stream in streams:
        stream.close()
    sent(last_swaps)


def finish_kernel(
    size,
    bits,
    out_all,
    frames_all,
    down_rows,
    up_rows,
    inward_rows,
    sums,
    out_ref,
    frames_ref,
    inward_ref,
    inward_bias_ref,
    outward_ref,
    up_ref,
    up_bias_ref,
    down_ref,
    gain_ref,
    offset_ref,
    out_vm,
    low_vm,
    wide_vm,
    sems,
):
    pieces = out_vm.shape[0]
    tokens = out_vm.shape[1]
    dp_place = lax.axis_index("dp")
    low_loads, out_loads = [], []
    for n in range(pieces):
        at = pl.ds(n * tokens, tokens)
        low_loads.append(pltpu.make_async_copy(frames_all.at[at], low_vm.at[n], sems.at[0, n]))
        out_loads.append(pltpu.make_async_copy(out_all.at[at], out_vm.at[n], sems.at[1, n]))
    start(low_loads)
    start(out_loads)
    rows = down_rows.shape[0]
    up_ref[0] = up_rows[...]

    def turned(values):
        filled = jnp.concatenate([values, jnp.zeros((LANES - rows, values.shape[1]), WIDE)], axis=0)
        return filled.T[:, :rows]

    def kind(number):
        outer = inward_rows[:, 128 * number : 128 * number + 128]
        inner = inward_rows[:, 512 + 128 * (number // 2) : 640 + 128 * (number // 2)]
        if number % 2:
            inner = pltpu.roll(inner, HEAD_SIZE, 1)
        return outer, inner

    for number in range(3):
        outer, inner = kind(number)
        inward_ref[0, number, :, 0:128] = outer
        inward_ref[0, number, :, 128:192] = inner[:, :HEAD_SIZE]
    outer, inner = kind(3)
    outward_ref[0, 0:128] = turned(outer)
    outward_ref[0, 128:192] = turned(inner)[:HEAD_SIZE]
    down_ref[0] = turned(down_rows[...])

    def own_part(values, part):
        width = values.shape[1]
        return pltpu.roll(values, lax.rem(width - dp_place * part, width), 1)[:, :part]

    share = down_rows.shape[1] // 2**bits
    table = sums[1]
    wide_share = own_part(table, share)
    gain_ref[0] = wide_share[0:2]
    offset_ref[0] = wide_share[2:6]
    lines = up_bias_ref.shape[1]
    part = LANES // 2**bits
    for line in range(lines):
        block = sums[0, 0:8, LANES * line : LANES * (line + 1)]
        up_bias_ref[0, line : line + 1] = own_part(block, part)[0:1]
    part = HEAD_SIZE // 2**bits
    for number in range(2):
        outer = sums[0, 0:8, 128 * number : 128 * number + 128]
        inner = sums[0, 0:8, 256:384]
        if number:
            inner = pltpu.roll(inner, HEAD_SIZE, 1)
        for head, block in enumerate((outer, pltpu.roll(outer, HEAD_SIZE, 1), inner)):
            inward_bias_ref[0, number, head : head + 1] = own_part(block, part)[1:2]
    stores = []
    for n in range(pieces):
        at = pl.ds(n * tokens, tokens)
        low_loads[n].wait()
        wide_vm[n] = low_vm[n].astype(WIDE)
        stores.append(pltpu.make_async_copy(wide_vm.at[n], frames_ref.at[at], sems.at[2, n]))
        stores[-1].start()
        out_loads[n].wait()
        stores.append(pltpu.make_async_copy(out_vm.at[n], out_ref.at[at], sems.at[3, n]))
        stores[-1].start()
    for copy in stores:
        copy.wait()


def anywhere():
    return pl.BlockSpec(memory_space=pl.ANY)


def inside():
    return pl.BlockSpec(memory_space=pltpu.VMEM)


def call(kernel, name, number, inputs, outputs, scratch, semaphores):
    return pl.pallas_call(
        kernel,
        name=name,
        in_specs=[spec for spec, _ in inputs],
        out_specs=[spec for spec, _ in outputs],
        out_shape=[jax.ShapeDtypeStruct(shape, dtype) for _, (shape, dtype) in outputs],
        scratch_shapes=[pltpu.VMEM(shape, dtype) for shape, dtype in scratch]
        + [pltpu.SemaphoreType.DMA(shape) for shape in semaphores],
        compiler_params=pltpu.CompilerParams(
            collective_id=number,
            has_side_effects=number is not None,
            vmem_limit_bytes=VMEM_BYTES,
        ),
    )(*[value for _, value in inputs])


def shards(
    bits,
    frames,
    segment_ids,
    valid_frames,
    inward_weight,
    inward_bias,
    output_weight,
    upward_weight,
    upward_bias,
    downward_weight,
    norm_gains,
    offsets,
    cotangent,
):
    token_count, features = frames.shape
    count = segment_ids.shape[1]
    wide_count = padded(count)
    hidden = upward_weight.shape[2]
    rows = features // 2**bits
    corner_start = row_blocks(count)[-1][0]
    square = ((wide_count, features), LOW)
    square_wide = ((wide_count, features), WIDE)
    rows_wide = ((count, features), WIDE)
    rows_low = ((count, features), LOW)
    others = ((3, features, hidden), LOW)
    a_shape = ((2, 4, 384, features), LOW)
    b_shape = ((4, 8, 1920), WIDE)
    marks = ((wide_count, LANES), LOW)
    corner_shape = ((count - corner_start, wide_count - corner_start), WIDE)
    (
        a_all,
        u_all,
        d_all,
        q,
        k,
        v,
        ctx,
        lse,
        mixed,
        b_all,
        query_marks,
        key_marks,
        corner,
    ) = call(
        functools.partial(forward_kernel, count),
        "attention_forward",
        1,
        [
            (anywhere(), frames),
            (anywhere(), inward_weight[0]),
            (anywhere(), output_weight[0]),
            (anywhere(), upward_weight[0]),
            (anywhere(), downward_weight[0]),
            (inside(), inward_bias[0]),
            (inside(), upward_bias[0]),
            (inside(), segment_ids),
            (inside(), valid_frames),
            (inside(), norm_gains[0]),
            (inside(), offsets[0]),
        ],
        [(anywhere(), shape) for shape in (a_shape, others, others)]
        + [(anywhere(), shape) for shape in (square, square, square)]
        + [(anywhere(), rows_wide)] * 3
        + [(inside(), shape) for shape in (b_shape, marks, marks, corner_shape)],
        [
            a_shape,
            b_shape,
            ((2, 8, 1920), WIDE),
            rows_low,
            ((3, features, 192), LOW),
            square,
            square,
            square,
            rows_wide,
            rows_wide,
            rows_wide,
            ((16, wide_count), jnp.int32),
        ],
        [(48,), (48,), (16,)],
    )
    plan = stream_plan(bits, features)
    grid = (2,) * bits + (rows,)
    buffers = []
    for _, columns, order in plan:
        buffers += [(shape, LOW) for shape in stream_shapes(bits, rows, columns[1], order)]
    own_chunk = ((rows, hidden), WIDE)
    small_shape = ((5, 8, features), WIDE)
    all_rows = ((4, count, features), LOW)
    out_all, frames_all, down_rows, up_rows, inward_rows, sums = call(
        functools.partial(back_kernel, count, bits, plan),
        "feed_forward_and_backward",
        2,
        [
            (anywhere(), frames),
            (anywhere(), cotangent),
            (anywhere(), mixed),
            (anywhere(), upward_weight[0]),
            (anywhere(), downward_weight[0]),
            (anywhere(), u_all),
            (anywhere(), d_all),
            (anywhere(), a_all.reshape(4, 768, features)),
            (anywhere(), q),
            (anywhere(), k),
            (anywhere(), v),
            (anywhere(), ctx),
            (anywhere(), lse),
            (inside(), b_all),
            (inside(), norm_gains[0]),
            (inside(), offsets[0]),
            (inside(), query_marks),
            (inside(), key_marks),
            (inside(), corner),
        ],
        [
            (anywhere(), all_rows),
            (anywhere(), all_rows),
            (inside(), own_chunk),
            (inside(), own_chunk),
            (inside(), own_chunk),
            (inside(), ((2, 8, features), WIDE)),
        ],
        [
            ((8, features, hidden), LOW),
            ((4, wide_count, hidden), LOW),
            ((4, wide_count, hidden), LOW),
            square,
            square,
            square,
            square,
            square,
            square_wide,
            square_wide,
            square_wide,
            ((3, 2) + grid + (hidden,), LOW),
            ((2, features, hidden), LOW),
            ((3, 2, features, hidden), LOW),
            ((LANES, wide_count), LOW),
            ((LANES, wide_count), LOW),
            ((LANES, wide_count), WIDE),
            ((LANES, wide_count), WIDE),
            ((3, 8, LANES), WIDE),
            small_shape,
            ((2, 3, 8, features), WIDE),
            ((bits + 1, 2, 8, features), WIDE),
            ((bits, 2, 8, features), WIDE),
        ]
        + buffers,
        [(64,), (64,), (24,)],
    )
    pieces = 8
    tokens = token_count // pieces
    lines = upward_bias.shape[1]
    return call(
        functools.partial(finish_kernel, rows, bits),
        "finish",
        None,
        [
            (anywhere(), out_all.reshape(token_count, features)),
            (anywhere(), frames_all.reshape(token_count, features)),
            (inside(), down_rows),
            (inside(), up_rows),
            (inside(), inward_rows),
            (inside(), sums),
        ],
        [
            (anywhere(), ((token_count, features), LOW)),
            (anywhere(), ((token_count, features), WIDE)),
            (inside(), ((1, 3, rows, 192), WIDE)),
            (inside(), ((1, 2, 3, HEAD_SIZE // 2**bits), WIDE)),
            (inside(), ((1, 192, rows), WIDE)),
            (inside(), ((1, rows, hidden), WIDE)),
            (inside(), ((1, lines, LANES // 2**bits), WIDE)),
            (inside(), ((1, hidden, rows), WIDE)),
            (inside(), ((1, 2, rows), WIDE)),
            (inside(), ((1, 4, rows), WIDE)),
        ],
        [
            ((pieces, tokens, features), LOW),
            ((pieces, tokens, features), LOW),
            ((pieces, tokens, features), WIDE),
        ],
        [(4, pieces)],
    )


def solution(mesh):
    bits = mesh.shape["dp"].bit_length() - 1
    in_specs = (
        P("dp", None),
        P("dp", None),
        P("dp", None),
        P(None, None, None, "tensor"),
        P(None, None, "tensor", None),
        P(None, "tensor", None),
        P(None, None, "tensor"),
        P(None, "tensor", None),
        P(None, "tensor", None),
        P(),
        P(),
        P("dp", None),
    )
    out_specs = (
        P("dp", None),
        P("dp", None),
        P(None, None, "dp", "tensor"),
        P(None, None, "tensor", "dp"),
        P(None, "tensor", "dp"),
        P(None, "dp", "tensor"),
        P(None, "tensor", "dp"),
        P(None, "tensor", "dp"),
        P(None, None, "dp"),
        P(None, None, "dp"),
    )
    return jax.shard_map(
        functools.partial(shards, bits),
        mesh=mesh,
        in_specs=in_specs,
        out_specs=out_specs,
        check_vma=False,
    )
```

```python
import functools
import itertools

import jax
import jax.numpy as jnp
from jax import lax
from jax.experimental import pallas as pl
from jax.experimental.pallas import tpu as pltpu
from jax.sharding import PartitionSpec as P

HEAD_SIZE = 64
LANES = 128
PAD = 128
LONGEST_CLIP_SHARE = 2
EPSILON = 1e-05
FAR = float(2**30)
LOW = jnp.bfloat16
WIDE = jnp.float32
MESH = pl.DeviceIdType.MESH
VMEM_BYTES = 61 << 20


def nn(left_side, right_side):
    return jnp.dot(left_side, right_side, preferred_element_type=WIDE)


def nt(left_side, right_side):
    return lax.dot_general(
        left_side, right_side, (((1,), (1,)), ((), ())), preferred_element_type=WIDE
    )


def padded(count):
    return -(-count // LANES) * LANES


def row_blocks(count, size=256):
    return [(start, min(size, count - start)) for start in range(0, count, size)]


def key_range(start, size, count):
    reach = count // LONGEST_CLIP_SHARE - 1
    low = max(0, (start - reach) // LANES * LANES)
    high = min(padded(count), padded(start + size + reach))
    return (low, high)


class Places:
    def __init__(self, bits):
        self.dp = lax.axis_index("dp")
        self.t = lax.axis_index("tensor")
        core = self.t % 2
        self.core = (self.dp, self.t + 1 - 2 * core)
        self.x = (self.dp, (self.t + 2) % 4)
        self.diagonal = (self.dp, 3 - self.t)
        self.bit = [(self.dp // 2**b) % 2 for b in range(bits)]
        self.step = [
            (self.dp + (1 - 2 * self.bit[b]) * 2**b, self.t) for b in range(bits)
        ]

    def greet(self, devices):
        barrier = pltpu.get_barrier_semaphore()
        for device in devices:
            pl.semaphore_signal(barrier, inc=1, device_id=device, device_id_type=MESH)
        pl.semaphore_wait(barrier, len(devices))


class Links:
    def __init__(self, send, recv, local):
        self.send, self.recv, self.local = send, recv, local
        self.used = self.used_local = 0

    def remote(self, source, target, device):
        place = self.used
        self.used += 1
        return pltpu.make_async_remote_copy(
            src_ref=source,
            dst_ref=target,
            send_sem=self.send.at[place],
            recv_sem=self.recv.at[place],
            device_id=device,
            device_id_type=MESH,
        )

    def near(self, source, target):
        place = self.used_local
        self.used_local += 1
        copy = pltpu.make_async_copy(source, target, self.local.at[place])
        copy.start()
        return copy


def start(copies):
    for copy in copies:
        copy.start()


def arrived(copies):
    for copy in copies:
        copy.wait_recv()


def sent(copies):
    for copy in copies:
        copy.wait_send()


class Gather:
    def __init__(self, places, links, part):
        self.places = places
        own, opposite = self.quarter(()), self.quarter((0, 1))

        def move(source, target, quarter, device):
            pairs = zip(part(source, quarter), part(target, quarter))
            return [links.remote(s, t, device) for s, t in pairs]

        self.core = move(0, 1, None, places.core)
        self.across = [move(0, 2, own, places.x), move(0, 2, opposite, places.x)]
        self.along = [move(2, 2, own, places.step[b]) for b in range(2)]
        self.passed = [
            move(2, 3, quarter, places.core)
            for quarter in (own, opposite, self.quarter((0,)), self.quarter((1,)))
        ]

    def quarter(self, flips):
        low, high = [
            1 - self.places.bit[b] if b in flips else self.places.bit[b] for b in range(2)
        ]
        return 2 * high + low

    def begin(self, number):
        start(self.across[number])

    def second(self):
        arrived(self.across[0])
        start(self.along[0] + self.along[1] + self.passed[0])

    def third(self):
        arrived(self.across[1])
        start(self.passed[1])

    def fourth(self):
        for b in range(2):
            arrived(self.along[b])
            start(self.passed[2 + b])

    def ready(self):
        for copies in self.passed:
            arrived(copies)

    def close(self):
        for copies in [self.core] + self.across + self.along + self.passed:
            sent(copies)


def lane_numbers():
    return lax.broadcasted_iota(jnp.int32, (1, LANES), 1)


def add_corner(scores, low, corner, corner_start):
    cut = corner_start - low
    return jnp.concatenate([scores[:, :cut], scores[:, cut:] + corner], axis=1)


def normalize(values):
    centred = values - jnp.mean(values, axis=-1, keepdims=True)
    rate = lax.rsqrt(jnp.mean(centred * centred, axis=-1, keepdims=True) + EPSILON)
    return (centred * rate, rate)


def normalize_back(grad, unit, rate, gain):
    scaled = grad * gain
    inner = jnp.mean(scaled * unit, axis=-1, keepdims=True)
    return rate * (scaled - jnp.mean(scaled, axis=-1, keepdims=True) - unit * inner)


def row_sum(values):
    return jnp.sum(values, axis=0, keepdims=True)


def gelu_pair(values):
    phi = 0.5 * (1.0 + lax.erf(values * 0.7071067811865476))
    density = jnp.exp(-0.5 * values * values) * 0.3989422804014327
    return (values * phi, phi + values * density)


class Stream:
    def __init__(self, bits, places, links, parts, buffers, out, columns, order, base):
        self.places = places
        self.dims = ["x"] + list(range(bits))[::-1]
        self.parts, self.buffers, self.out = parts, buffers, out
        self.columns, self.order, self.base = columns, order, base
        self.sends, self.done = [], 0
        for number, dim in enumerate(order):
            device = places.x if dim == "x" else places.step[dim]
            copies = {}
            split = number == 0 and dim != "x" and not base
            for slot in (1, 0) if split else (None,):
                fixed = self.fixed(number)
                fixed[dim] = 1 if dim == "x" else 1 - places.bit[dim]
                target = buffers[number]
                if slot is not None:
                    fixed["x"] = slot
                    target = target.at[slot]
                copies[slot] = links.remote(parts.at[self.index(fixed)], target, device)
            self.sends.append(copies)

    def fixed(self, number):
        fixed = {dim: 0 if dim == "x" else self.places.bit[dim] for dim in self.order[:number]}
        return {**fixed, **self.base}

    def index(self, fixed):
        place = tuple(fixed.get(dim, slice(None)) for dim in self.dims)
        return place + (slice(None), pl.ds(self.columns[0], self.columns[1]))

    def begin(self, number, slots=None):
        for slot, copy in self.sends[number].items():
            if slots is None or slot in slots:
                copy.start()

    def finish(self, number):
        arrived(self.sends[number].values())
        buffer = self.buffers[number]
        ends = slice(self.columns[0], self.columns[0] + self.columns[1])
        if self.base.get("x") == 1 and self.order[number] == "x":
            self.out[:, ends] += buffer[...].astype(WIDE)
            return
        keep = self.fixed(number + 1)
        rest = [dim for dim in self.dims if dim not in keep]
        for values in itertools.product(range(2), repeat=len(rest)):
            fixed = dict(keep)
            fixed.update(zip(rest, values))
            place = self.index(fixed)
            total = self.parts[place].astype(WIDE) + buffer[values].astype(WIDE)
            if number + 1 < len(self.order):
                self.parts[place] = total.astype(LOW)
            else:
                self.out[:, ends] = total

    def step(self):
        self.finish(self.done)
        self.done += 1
        if self.done < len(self.order):
            self.begin(self.done)

    def close(self):
        for copies in self.sends:
            sent(copies.values())


def stream_shapes(bits, rows, columns, order, base):
    dims = ["x"] + list(range(bits))
    shapes = []
    for number in range(len(order)):
        rest = [dim for dim in dims if dim not in order[: number + 1] and dim not in base]
        shapes.append((2,) * len(rest) + (rows, columns))
    return shapes


def stream_plan(bits, features):
    high = tuple(range(2, bits))
    third = features // 3
    down = [(0, 1, "x") + high] * 3
    up = [("x", 1, 0) + high, (1, 0, "x") + high, (0, "x", 1) + high]
    late = [(0, 1) + high] * 3
    plan = []
    for unit, orders in enumerate((down, up, late)):
        for number, order in enumerate(orders):
            columns = (third * number, third)
            if unit < 2:
                plan.append((unit, columns, order, {}))
            else:
                plan.append((unit, columns, order, {"x": 0}))
                plan.append((unit, columns, order + ("x",), {"x": 1}))
    return plan


def layer_kernel(
    count,
    bits,
    plan,
    frames,
    cotangent,
    w_own,
    o_own,
    u_own,
    d_own,
    pair_bias,
    up_bias_ref,
    seg_ref,
    valid_ref,
    gain_ref,
    offset_ref,
    out_all,
    frames_out,
    a_all,
    q_all,
    k_all,
    v_all,
    ctx_all,
    lse_all,
    down_out,
    up_out,
    inward_out,
    small_out,
    w_vm,
    act,
    slope,
    low_vm,
    low_t,
    grad_t,
    upper,
    grads_vm,
    out_vm,
    acc,
    dsecond,
    cot_vm,
    parts,
    staged,
    landed,
    query_t,
    pair_grad_t,
    dk_t,
    dv_t,
    bias_sums,
    small,
    small_in,
    pair_vm,
    pair_in,
    b_vm,
    b_own,
    row_vm,
    qf_ref,
    kf_ref,
    corner_ref,
    *rest,
):
    buffers, (send_sems, recv_sems, local_sems, free) = rest[:-4], rest[-4:]
    places = Places(bits)
    links = Links(send_sems, recv_sems, local_sems)
    wide_count = padded(count)
    features = low_vm.shape[1]
    frames_at = pl.ds(0, count)
    quarter_rows = features // 4
    own_rows = o_own.shape[0]
    part_rows = own_rows // 4
    x_vm, ctx_vm, lse_vm, a_vm = upper, cot_vm, dsecond, slope
    b_own[...] = jnp.zeros_like(b_own)
    for kind, at in ((0, 0), (1, 768)):
        heads = [pair_bias[h, kind : kind + 1].astype(WIDE) for h in range(3)]
        blank = jnp.zeros_like(heads[0])
        b_own[0, 0:1, at : at + 128] = jnp.concatenate([heads[0], heads[1]], axis=1)
        b_own[0, 0:1, at + 128 : at + 256] = jnp.concatenate([heads[2], blank], axis=1)
        b_own[1, 0:1, at + 128 : at + 256] = jnp.concatenate([blank, heads[0]], axis=1)
        b_own[1, 0:1, at + 256 : at + 384] = jnp.concatenate([heads[1], heads[2]], axis=1)
    for line in range(up_bias_ref.shape[0]):
        at = 1152 + LANES * line
        row = up_bias_ref[line : line + 1].astype(WIDE)
        b_own[0, 0:1, at : at + LANES] = row
        b_own[1, 0:1, at : at + LANES] = row
    places.greet([places.core, places.x, places.diagonal] + places.step)

    def span(quarter, rows):
        return (0, 4 * rows) if quarter is None else (quarter * rows, rows)

    def a_views(number, quarter, kinds):
        low, size = span(quarter, part_rows)
        if number == 0:
            return [o_own.at[pl.ds(low, size)] if k == 3 else w_own.at[k, pl.ds(low, size)] for k in kinds]
        group, at = number // 2, own_rows * (number % 2) + low
        return [
            a_vm.at[2 * group + k // 2, pl.ds(384 * (k % 2) + at, size)] for k in kinds
        ]

    def w_part(number, quarter):
        return a_views(number, quarter, (0, 1, 2))

    def o_part(number, quarter):
        return a_views(number, quarter, (3,))

    def u_part(number, quarter):
        low, size = span(quarter, quarter_rows)
        return [(w_vm.at[number] if number else u_own).at[pl.ds(low, size)]]

    def d_part(number, quarter):
        low, size = span(quarter, quarter_rows)
        return [(w_vm.at[4 + number] if number else d_own).at[pl.ds(low, size)]]

    w_gather, o_gather, u_gather, d_gather = [
        Gather(places, links, part) for part in (w_part, o_part, u_part, d_part)
    ]
    bias_copies = [
        links.remote(b_own.at[1], b_vm.at[1], places.core),
        links.remote(b_own.at[0], b_vm.at[2], places.x),
        links.remote(b_own.at[1], b_vm.at[3], places.diagonal),
    ]
    start(bias_copies)
    start(w_gather.core)
    w_gather.begin(0)
    start(o_gather.core)
    x_load = links.near(
        frames.at[pl.ds(places.t * count, count)], x_vm.at[frames_at]
    )
    a_loads = [
        links.near(source, target)
        for source, target in zip(
            a_views(0, None, range(4)),
            [a_vm.at[k // 2, pl.ds(384 * (k % 2), own_rows)] for k in range(4)],
        )
    ]
    u_load = links.near(u_own, w_vm.at[0])
    d_load = links.near(d_own, w_vm.at[4])
    left = lane_numbers() < HEAD_SIZE
    one = jnp.ones((), LOW)
    b_vm[0] = b_own[0]
    row_vm[0:8] = jnp.full((8, wide_count), -1, jnp.int32)
    row_vm[8:16] = jnp.zeros((8, wide_count), jnp.int32)
    row_vm[0:1, 0:count] = seg_ref[pl.ds(places.t, 1)]
    row_vm[8:9, 0:count] = valid_ref[pl.ds(places.t, 1)]
    corner_start = row_blocks(count)[-1][0]
    segments = jnp.broadcast_to(row_vm[0:1], (LANES, wide_count))
    valid = jnp.broadcast_to(row_vm[8:9], (LANES, wide_count))
    mark = lax.broadcasted_iota(jnp.int32, (LANES, wide_count), 0) % HEAD_SIZE
    frame = lax.broadcasted_iota(jnp.int32, (LANES, wide_count), 1)
    same = segments == mark
    query_marks = jnp.where(
        mark < 4,
        jnp.where(same, 0.0, -FAR),
        jnp.where(
            mark == 4,
            -FAR,
            jnp.where(mark == 5, jnp.where(frame < corner_start, -FAR, 0.0), 0.0),
        ),
    )
    key_marks_t = jnp.where(
        mark < 4,
        jnp.where(same, 1.0, 0.0),
        jnp.where(
            mark == 4,
            jnp.where(frame >= count, 1.0, 0.0),
            jnp.where(
                mark == 5,
                jnp.where(valid > 0, 0.0, 1.0),
                jnp.where(mark < 9, 1.0, 0.0),
            ),
        ),
    )
    qf_ref[...] = query_marks.astype(LOW).T
    kf_ref[...] = key_marks_t.astype(LOW).T
    corner_shape = (count - corner_start, wide_count - corner_start)
    open_keys = jnp.broadcast_to(row_vm[8:9, corner_start:], corner_shape) > 0
    itself = lax.broadcasted_iota(jnp.int32, corner_shape, 0) == lax.broadcasted_iota(
        jnp.int32, corner_shape, 1
    )
    corner_ref[...] = jnp.where(open_keys | itself, 0.0, -FAR)
    tail = jnp.zeros((wide_count - count, features), LOW)
    for number in range(3):
        act[number, count:] = tail
    x_load.wait()

    def project(group):
        bias = b_vm[2 * group, 0:1, 0:1152] + b_vm[2 * group + 1, 0:1, 0:1152]
        at = 384 * group
        for low, size in row_blocks(count):
            rows = x_vm[low : low + size]
            pair = (nt(rows, a_vm[2 * group]) + bias[:, 0:768]).astype(LOW)
            value = (nt(rows, a_vm[2 * group + 1, 0:384]) + bias[:, 768:1152]).astype(LOW)
            act[0, low : low + size, at : at + 384] = pair[:, 0:384] * 0.125
            act[1, low : low + size, at : at + 384] = pair[:, 384:768]
            act[2, low : low + size, at : at + 384] = value

    def attend_ahead(first, last):
        def body(pair, carry):
            at = pl.ds(pl.multiple_of(pair * LANES, LANES), LANES)
            keys, values, key_marks = act[1, :, at], act[2, :, at], kf_ref[...]
            key_sides = [jnp.where(left, keys, key_marks), jnp.where(left, key_marks, keys)]
            value_sides = [jnp.where(left, values, one), jnp.where(left, one, values)]
            for low, size in row_blocks(count):
                begin, end = key_range(low, size, count)
                rows = act[0, low : low + size, at]
                marks = qf_ref[low : low + size]
                query_sides = [jnp.where(left, rows, marks), jnp.where(left, marks, rows)]
                scores = [
                    nt(query, key[begin:end]) for query, key in zip(query_sides, key_sides)
                ]
                if low + size == count:
                    scores = [add_corner(s, begin, corner_ref[...], low) for s in scores]
                largest = [jnp.max(s, axis=1, keepdims=True) for s in scores]
                weights = [jnp.exp(s - m).astype(LOW) for s, m in zip(scores, largest)]
                sums = [nn(w, v[begin:end]) for w, v in zip(weights, value_sides)]
                numerator = jnp.where(left, sums[0], sums[1])
                denominator = pltpu.roll(jnp.where(left, sums[1], sums[0]), HEAD_SIZE, 1)
                ctx_vm[low : low + size, at] = numerator / denominator
                lse_vm[low : low + size, at] = jnp.where(
                    left, largest[0], largest[1]
                ) + jnp.log(denominator)
            return carry

        lax.fori_loop(first, last, body, 0)

    def mix(group):
        weights = a_vm[2 * group + 1, 384:768]
        at = 384 * group
        for low, size in row_blocks(count):
            term = nn(ctx_vm[low : low + size, at : at + 384].astype(LOW), weights)
            if group == 0:
                acc[low : low + size] = x_vm[low : low + size].astype(WIDE) + term
            else:
                acc[low : low + size] += term + offset_ref[0:1]

    stores = []
    for copy in a_loads:
        copy.wait()
    arrived(w_gather.core)
    arrived(bias_copies[:1])
    project(0)
    w_gather.begin(1)
    start(u_gather.core)
    attend_ahead(0, 1)
    o_gather.begin(0)
    o_gather.begin(1)
    attend_ahead(1, 2)
    w_gather.second()
    u_gather.begin(0)
    attend_ahead(2, 3)
    arrived(o_gather.core)
    mix(0)
    u_gather.begin(1)
    w_gather.third()
    start(d_gather.core)
    w_gather.fourth()
    arrived(bias_copies[1:])
    w_gather.ready()
    project(1)
    o_gather.second()
    for number, target in enumerate((q_all, k_all, v_all)):
        stores.append(links.near(act.at[number], target))
    attend_ahead(3, 4)
    d_gather.begin(0)
    attend_ahead(4, 5)
    o_gather.third()
    o_gather.fourth()
    u_gather.second()
    attend_ahead(5, 6)
    d_gather.begin(1)
    ctx_store = links.near(ctx_vm.at[frames_at], ctx_all)
    lse_store = links.near(lse_vm.at[frames_at], lse_all)
    o_gather.ready()
    stores.append(links.near(a_vm, a_all))
    mix(1)
    mixed_vm = dsecond
    grid = parts.shape[2:-1]
    outs = (down_out, up_out, inward_out)
    streams, used = [], 0
    for unit, columns, order, base in plan:
        own_buffers = buffers[used : used + len(order)]
        used += len(order)
        streams.append(
            Stream(
                bits,
                places,
                links,
                parts.at[unit],
                own_buffers,
                outs[unit],
                columns,
                order,
                base,
            )
        )
    units = [streams[0:3], streams[3:6], streams[6::2], streams[7::2]]
    gain_one, gain_two = gain_ref[0:1], gain_ref[1:2]
    lse_store.wait()
    for low, size in row_blocks(count):
        mixed = acc[low : low + size]
        mixed_vm[low : low + size] = mixed
        unit, _ = normalize(mixed)
        rows = unit * gain_one + offset_ref[2:3]
        low_vm[low : low + size] = rows.astype(LOW)
        acc[low : low + size] = rows + offset_ref[1:2]
    ctx_store.wait()
    for copy in stores:
        copy.wait()
    cot_load = links.near(
        cotangent.at[pl.ds(places.t * count, count)], cot_vm.at[frames_at]
    )
    low_vm[count:] = tail
    upper[count:] = tail

    def raise_rows(number):
        bias = b_vm[number, 0:1, 1152:1920]
        for low, size in row_blocks(count):
            upward = nn(low_vm[low : low + size], w_vm[number]) + bias
            value, rate = gelu_pair(upward)
            act[number, low : low + size] = value.astype(LOW)
            slope[number, low : low + size] = rate.astype(LOW)
        act[number, count:] = tail

    def lower_rows(number):
        for low, size in row_blocks(count):
            acc[low : low + size] += nn(act[number, low : low + size], w_vm[4 + number])

    w_gather.close()
    o_gather.close()
    sent(bias_copies)
    u_load.wait()
    raise_rows(0)
    d_load.wait()
    lower_rows(0)
    d_gather.second()
    u_gather.third()
    u_gather.fourth()
    arrived(u_gather.core)
    raise_rows(1)
    arrived(d_gather.core)
    lower_rows(1)
    u_gather.ready()
    raise_rows(2)
    raise_rows(3)
    d_gather.third()
    d_gather.fourth()
    d_gather.ready()
    lower_rows(2)
    lower_rows(3)
    cot_load.wait()
    sums = [jnp.zeros((1, features), WIDE) for _ in range(3)]
    for low, size in row_blocks(count):
        unit, rate = normalize(acc[low : low + size])
        out_vm[low : low + size] = (unit * gain_two + offset_ref[3:4]).astype(LOW)
        grad = cot_vm[low : low + size]
        back = normalize_back(grad, unit, rate, gain_two)
        acc[low : low + size] = back
        sums = [
            sums[0] + row_sum(grad * unit),
            sums[1] + row_sum(grad),
            sums[2] + row_sum(back),
        ]
    gain_two_sum, shift_two_sum, down_bias_sum = sums

    class Spread:
        def __init__(self, source, target):
            own = target.at[places.t]
            self.to_core = links.remote(source.at[frames_at], own, places.core)
            self.to_x = links.remote(source.at[frames_at], own, places.x)
            beside = target.at[places.x[1]]
            self.passed = links.remote(beside, beside, places.core)
            self.to_x.start()
            self.to_core.start()
            self.kept = links.near(source.at[frames_at], own)

        def hand_on(self):
            self.to_x.wait_recv()
            self.passed.start()

        def source_free(self):
            self.to_core.wait_send()
            self.to_x.wait_send()
            self.kept.wait()

        def close(self):
            self.to_core.wait_recv()
            self.passed.wait()

    out_spread = Spread(out_vm, out_all)
    low_t[...] = low_vm[...].T
    for low, size in row_blocks(count):
        low_vm[low : low + size] = acc[low : low + size].astype(LOW)
    grad_t[...] = low_vm[...].T

    def back(number):
        total = jnp.zeros((1, features), WIDE)
        for low, size in row_blocks(count):
            inner = nt(low_vm[low : low + size], w_vm[4 + number])
            rows = (slope[number, low : low + size].astype(WIDE) * inner).astype(LOW)
            upper[low : low + size] = rows
            total += row_sum(rows.astype(WIDE))
            acc[low : low + size] += nt(rows, w_vm[number])
        return total

    def grads(number, finish, before=None, after=None):
        for unit, rows, other in ((0, grad_t, act.at[number]), (1, low_t, upper)):
            if before:
                before(unit)
            for low, size in row_blocks(features):
                finish(unit, low, size, nn(rows[low : low + size], other[...]))
            if after:
                after(unit)

    swaps = [
        [links.remote(staged.at[u], landed.at[u], places.core) for u in range(2)]
        for odd in range(2)
    ]
    chunk = grid[-1]
    indices = list(itertools.product(range(2), repeat=bits))

    def put(unit, even, low, value):
        for place, index in enumerate(indices):
            begin = place * chunk
            if low <= begin and begin + chunk <= low + value.shape[0]:
                parts[(unit, even) + index] = value[begin - low : begin - low + chunk]
            elif low <= begin < low + value.shape[0]:
                cut = low + value.shape[0] - begin
                parts[(unit, even) + index + (slice(0, cut),)] = value[begin - low :]
            elif begin < low < begin + chunk:
                cut = low - begin
                parts[(unit, even) + index + (slice(cut, chunk),)] = value[: chunk - cut]

    def give(unit, low, size, value):
        staged[unit, low : low + size] = value.astype(LOW)

    def take(even):
        def finish(unit, low, size, value):
            total = value + landed[unit, low : low + size].astype(WIDE)
            put(unit, even, low, total.astype(LOW))

        return finish

    def allow():
        pl.semaphore_signal(free, inc=1, device_id=places.core, device_id_type=MESH)

    up_bias = {}
    up_bias[3] = back(3)
    grads(3, give, after=lambda unit: swaps[1][unit].start())
    up_bias[2] = back(2)

    def begin_across(unit):
        for stream in units[unit]:
            stream.begin(0, (1, None))

    def begin_own(unit):
        for stream in units[unit]:
            stream.begin(0, (0,))

    grads(2, take(1), lambda unit: swaps[1][unit].wait_recv(), begin_across)
    allow()
    up_bias[1] = back(1)
    sent(swaps[1])
    pl.semaphore_wait(free, 1)
    grads(1, give, after=lambda unit: swaps[0][unit].start())
    up_bias[0] = back(0)
    u_gather.close()
    d_gather.close()
    a_load = links.near(a_all, w_vm.at[pl.ds(0, 4)])
    grads(0, take(0), lambda unit: swaps[0][unit].wait_recv(), begin_own)
    allow()
    sent(swaps[0])
    x_load = links.near(frames.at[pl.ds(places.t * count, count)], upper.at[frames_at])
    head_loads = [
        links.near(source, act.at[n]) for n, source in enumerate((q_all, k_all, v_all))
    ]
    ctx_load = links.near(ctx_all, cot_vm.at[frames_at])
    sums = [jnp.zeros((1, features), WIDE) for _ in range(3)]
    for low, size in row_blocks(count):
        unit, rate = normalize(mixed_vm[low : low + size])
        grad = acc[low : low + size]
        back_rows = normalize_back(grad, unit, rate, gain_one)
        acc[low : low + size] = back_rows
        low_vm[low : low + size] = back_rows.astype(LOW)
        sums = [
            sums[0] + row_sum(grad * unit),
            sums[1] + row_sum(grad),
            sums[2] + row_sum(back_rows),
        ]
    gain_one_sum, shift_one_sum, out_bias_sum = sums
    lse_load = links.near(lse_all, lse_vm.at[frames_at])
    small[...] = jnp.zeros_like(small)
    for place, number in ((0, 0), (1, 2), (3, 1), (4, 3)):
        small[place, 0:1] = up_bias[number]
    for place, row in enumerate(
        (gain_one_sum, gain_two_sum, out_bias_sum, down_bias_sum, shift_one_sum, shift_two_sum)
    ):
        small[2, place : place + 1] = row
    m_low, m_t, x_vm, x_t = low_vm, low_t, upper, grad_t
    m_t[...] = m_low[...].T
    x_load.wait()
    x_t[...] = x_vm[...].T
    a_load.wait()
    ctx_load.wait()
    lanes = lane_numbers()
    mark = lanes % HEAD_SIZE
    value_marks = jnp.where(mark < 3, 1.0, 0.0).astype(LOW)
    grads_vm[count:] = tail
    for number in range(4):
        slope[number, count:] = tail
    for group in range(2):
        for low, size in row_blocks(count):
            at = 384 * group
            rows = nt(m_low[low : low + size], w_vm[2 * group + 1, 384:768])
            grads_vm[low : low + size, at : at + 384] = rows.astype(LOW)
            slope[2 + group, low : low + size, 384:768] = ctx_vm[
                low : low + size, at : at + 384
            ].astype(LOW)
    for copy in head_loads:
        copy.wait()
    lse_load.wait()

    def thirds(values):
        high = values.astype(LOW)
        rest_one = values - high.astype(WIDE)
        middle = rest_one.astype(LOW)
        return (high, middle, (rest_one - middle.astype(WIDE)).astype(LOW))

    def attend(group, first, last):
        def body(pair, carry):
            at = pl.ds(pl.multiple_of((3 * group + pair) * LANES, LANES), LANES)
            at_query = pl.ds(pl.multiple_of(pair * LANES, LANES), LANES)
            at_key = pl.ds(pl.multiple_of(384 + pair * LANES, LANES), LANES)
            keys, values, key_marks = act[1, :, at], act[2, :, at], kf_ref[...]
            key_sides = [jnp.where(left, keys, key_marks), jnp.where(left, key_marks, keys)]
            value_sides = [
                jnp.where(left, values, value_marks),
                jnp.where(left, value_marks, values),
            ]
            query_t[...] = act[0, :, at].T
            pair_grad_t[...] = grads_vm[:, at].T
            query_sum = jnp.zeros((1, LANES), WIDE)
            for number, (low, size) in enumerate(row_blocks(count)):
                begin, end = key_range(low, size, count)
                rows = act[0, low : low + size, at]
                total = pltpu.roll(lse_vm[low : low + size, at], HEAD_SIZE, 1)
                high, middle, rest_low = thirds(-total)
                marks = jnp.where(
                    mark == 6,
                    high,
                    jnp.where(
                        mark == 7,
                        middle,
                        jnp.where(mark == 8, rest_low, qf_ref[low : low + size]),
                    ),
                )
                query_sides = [jnp.where(left, rows, marks), jnp.where(left, marks, rows)]
                grad = grads_vm[low : low + size, at]
                product = grad.astype(WIDE) * ctx_vm[low : low + size, at]
                inner_left = jnp.sum(jnp.where(left, product, 0.0), axis=1, keepdims=True)
                inner_right = jnp.sum(jnp.where(left, 0.0, product), axis=1, keepdims=True)
                high, middle, rest_low = thirds(-jnp.where(left, inner_right, inner_left))
                grad_marks = jnp.where(
                    mark == 0,
                    high,
                    jnp.where(
                        mark == 1, middle, jnp.where(mark == 2, rest_low, jnp.zeros((), LOW))
                    ),
                )
                grad_sides = [
                    jnp.where(left, grad, grad_marks),
                    jnp.where(left, grad_marks, grad),
                ]
                scores = [
                    nt(query, key[begin:end]) for query, key in zip(query_sides, key_sides)
                ]
                if low + size == count:
                    scores = [add_corner(s, begin, corner_ref[...], low) for s in scores]
                probs = [jnp.exp(s) for s in scores]
                prob_grads = [
                    nt(one, value[begin:end]) for one, value in zip(grad_sides, value_sides)
                ]
                probs_low = [p.astype(LOW) for p in probs]
                score_grads = [(p * g).astype(LOW) for p, g in zip(probs, prob_grads)]
                query_grads = [
                    nn(s, key[begin:end]) for s, key in zip(score_grads, key_sides)
                ]
                query_grad = (jnp.where(left, query_grads[0], query_grads[1]) * 0.125).astype(LOW)
                slope[group, low : low + size, at_query] = query_grad
                query_sum += row_sum(query_grad.astype(WIDE))
                for side in range(2):
                    part = slice(HEAD_SIZE * side, HEAD_SIZE * side + HEAD_SIZE)
                    value_term = nn(pair_grad_t[part, low : low + size], probs_low[side])
                    key_term = nn(query_t[part, low : low + size], score_grads[side])
                    if number == 0:
                        dv_t[part, begin:end] = value_term
                        dk_t[part, begin:end] = key_term
                        if end < wide_count:
                            blank = jnp.zeros((HEAD_SIZE, wide_count - end), WIDE)
                            dv_t[part, end:] = blank
                            dk_t[part, end:] = blank
                    else:
                        dv_t[part, begin:end] += value_term
                        dk_t[part, begin:end] += key_term
            key_grad = dk_t[...].astype(LOW).T
            value_grad = dv_t[...].astype(LOW).T
            slope[group, :, at_key] = key_grad
            slope[2 + group, :, at_query] = value_grad
            bias_sums[pair, 0:1] = query_sum
            bias_sums[pair, 1:2] = row_sum(value_grad.astype(WIDE))
            return carry

        lax.fori_loop(first, last, body, 0)

    def other_side(values):
        return pltpu.roll(values, HEAD_SIZE, 1)

    def packed(blocks, odd):
        if odd:
            turned = [(other_side(b[1]), other_side(b[2])) for b in blocks]
            outer = [jnp.where(left, one, two) for one, two in turned]
        else:
            outer = [b[0] for b in blocks]
        joined = []
        for n in range(0, len(blocks), 2):
            if odd:
                joined.append(jnp.where(left, turned[n][1], blocks[n + 1][2]))
            else:
                joined.append(jnp.where(left, blocks[n][1], other_side(blocks[n + 1][1])))
        return jnp.concatenate(outer + joined, axis=1)

    def split(values):
        return [values[:, LANES * p : LANES * (p + 1)] for p in range(3)]

    def weight_grads(group):
        for low, size in row_blocks(features):
            pair = nn(x_t[low : low + size], slope[group])
            value = nn(x_t[low : low + size], slope[2 + group, :, 0:384])
            outward = nn(m_t[low : low + size], slope[2 + group, :, 384:768])
            blocks = [split(pair[:, :384]), split(pair[:, 384:]), split(value), split(outward)]
            staged[group, low : low + size] = packed(blocks, True).astype(LOW)
            put(2, group, low, packed(blocks, False).astype(LOW))

    def bias_grads(group):
        rows = [[bias_sums[p, kind : kind + 1] for p in range(3)] for kind in range(2)]
        for place, odd in ((1 if group else 0, False), (4 if group else 3, True)):
            small[place, 1:2, 0:384] = packed(rows, odd)

    def input_grads(group):
        for low, size in row_blocks(count):
            acc[low : low + size] += nn(slope[group, low : low + size], w_vm[2 * group]) + nn(
                slope[2 + group, low : low + size, 0:384], w_vm[2 * group + 1, 0:384]
            )

    last_swaps = [links.remote(staged.at[g], landed.at[g], places.core) for g in range(2)]

    def combine(group):
        arrived([last_swaps[group]])
        for place, index in enumerate(indices):
            rows = slice(place * chunk, (place + 1) * chunk)
            total = parts[(2, group) + index].astype(WIDE) + landed[group, rows].astype(WIDE)
            parts[(2, group) + index] = total.astype(LOW)


    downs, ups, own_late, far_late = units

    def steps(*streams):
        for stream in streams:
            stream.step()

    steps(ups[1])
    attend(1, 0, 1)
    out_spread.hand_on()
    steps(downs[0])
    attend(1, 1, 3)
    steps(downs[1])
    weight_grads(1)
    pl.semaphore_wait(free, 1)
    start([last_swaps[1]])
    bias_grads(1)
    steps(downs[2], downs[0])
    input_grads(1)
    steps(ups[0])
    combine(1)
    for stream in far_late:
        stream.begin(0)
    attend(0, 0, 1)
    steps(ups[2], downs[1], ups[1])
    attend(0, 1, 2)
    steps(downs[2], ups[0])
    attend(0, 2, 3)
    steps(ups[2])
    bias_grads(0)
    small_core = links.remote(small.at[pl.ds(2, 3)], small_in.at[0], places.core)
    small_core.start()
    input_grads(0)
    out_spread.source_free()
    out_spread.close()
    small_core.wait()
    small[2] += small_in[0, 0]
    small[0] += small_in[0, 1]
    small[1] += small_in[0, 2]
    small_x = links.remote(small.at[pl.ds(1, 2)], small_in.at[1, pl.ds(0, 2)], places.x)
    small_x.start()
    own_out = grads_vm
    for low, size in row_blocks(count):
        own_out[low : low + size] = acc[low : low + size].astype(LOW)
    frames_spread = Spread(own_out, frames_out)
    weight_grads(0)
    start([last_swaps[0]])
    steps(*far_late[:1])
    small_x.wait()
    pair_vm[0, 0] = small[0] + small_in[1, 0]
    pair_vm[0, 1] = small[2] + small_in[1, 1]
    small_steps = [
        links.remote(pair_vm.at[b], pair_in.at[b], places.step[b]) for b in range(bits)
    ]
    small_steps[0].start()
    combine(0)
    for stream in own_late:
        stream.begin(0)

    def small_step(number):
        if number < bits:
            small_steps[number].wait()
            pair_vm[number + 1] = pair_vm[number] + pair_in[number]
            if number + 1 < bits:
                small_steps[number + 1].start()

    early = downs + ups
    steps(*far_late[1:])
    steps(*downs, ups[1])
    small_step(0)
    steps(own_late[0], *far_late)
    steps(own_late[1], own_late[0], ups[0], ups[2])
    small_step(1)
    steps(own_late[2], own_late[1], *far_late)
    steps(own_late[2], *downs, ups[1])
    steps(*own_late)
    for number in range(2, bits):
        small_step(number)
    frames_spread.hand_on()
    while True:
        waiting = [one for one in early + own_late if one.done < len(one.order)]
        waiting += [one for one in far_late if one.done + 1 < len(one.order)]
        if not waiting:
            break
        steps(*waiting)
    steps(*far_late)
    small_out[...] = pair_vm[bits]
    frames_spread.source_free()
    frames_spread.close()
    for stream in streams:
        stream.close()
    sent(last_swaps)


def finish_kernel(
    size,
    bits,
    out_all,
    frames_all,
    down_rows,
    up_rows,
    inward_rows,
    sums,
    out_ref,
    frames_ref,
    inward_ref,
    inward_bias_ref,
    outward_ref,
    up_ref,
    up_bias_ref,
    down_ref,
    gain_ref,
    offset_ref,
    out_vm,
    low_vm,
    wide_vm,
    sems,
):
    pieces = out_vm.shape[0]
    tokens = out_vm.shape[1]
    dp_place = lax.axis_index("dp")
    low_loads, out_loads = [], []
    for n in range(pieces):
        at = pl.ds(n * tokens, tokens)
        low_loads.append(pltpu.make_async_copy(frames_all.at[at], low_vm.at[n], sems.at[0, n]))
        out_loads.append(pltpu.make_async_copy(out_all.at[at], out_vm.at[n], sems.at[1, n]))
    start(low_loads)
    start(out_loads)
    rows = down_rows.shape[0]
    up_ref[0] = up_rows[...]

    def turned(values):
        filled = jnp.concatenate([values, jnp.zeros((LANES - rows, values.shape[1]), WIDE)], axis=0)
        return filled.T[:, :rows]

    def kind(number):
        outer = inward_rows[:, 128 * number : 128 * number + 128]
        inner = inward_rows[:, 512 + 128 * (number // 2) : 640 + 128 * (number // 2)]
        if number % 2:
            inner = pltpu.roll(inner, HEAD_SIZE, 1)
        return outer, inner

    for number in range(3):
        outer, inner = kind(number)
        inward_ref[0, number, :, 0:128] = outer
        inward_ref[0, number, :, 128:192] = inner[:, :HEAD_SIZE]
    outer, inner = kind(3)
    outward_ref[0, 0:128] = turned(outer)
    outward_ref[0, 128:192] = turned(inner)[:HEAD_SIZE]
    down_ref[...] = down_rows[...]

    def own_part(values, part):
        width = values.shape[1]
        return pltpu.roll(values, lax.rem(width - dp_place * part, width), 1)[:, :part]

    share = down_rows.shape[1] // 2**bits
    table = sums[1]
    wide_share = own_part(table, share)
    gain_ref[0] = wide_share[0:2]
    offset_ref[0] = wide_share[2:6]
    lines = up_bias_ref.shape[0]
    part = LANES // 2**bits
    for line in range(lines):
        block = sums[0, 0:8, LANES * line : LANES * (line + 1)]
        up_bias_ref[line] = own_part(block, part)[0:1]
    part = HEAD_SIZE // 2**bits
    for number in range(2):
        outer = sums[0, 0:8, 128 * number : 128 * number + 128]
        inner = sums[0, 0:8, 256:384]
        if number:
            inner = pltpu.roll(inner, HEAD_SIZE, 1)
        for head, block in enumerate((outer, pltpu.roll(outer, HEAD_SIZE, 1), inner)):
            inward_bias_ref[head, number : number + 1] = own_part(block, part)[1:2]
    stores = []
    for n in range(pieces):
        at = pl.ds(n * tokens, tokens)
        low_loads[n].wait()
        wide_vm[n] = low_vm[n].astype(WIDE)
        stores.append(pltpu.make_async_copy(wide_vm.at[n], frames_ref.at[at], sems.at[2, n]))
        stores[-1].start()
        out_loads[n].wait()
        stores.append(pltpu.make_async_copy(out_vm.at[n], out_ref.at[at], sems.at[3, n]))
        stores[-1].start()
    for copy in stores:
        copy.wait()


def anywhere():
    return pl.BlockSpec(memory_space=pl.ANY)


def inside():
    return pl.BlockSpec(memory_space=pltpu.VMEM)


def call(kernel, name, number, inputs, outputs, scratch, semaphores):
    return pl.pallas_call(
        kernel,
        name=name,
        in_specs=[spec for spec, _ in inputs],
        out_specs=[spec for spec, _ in outputs],
        out_shape=[jax.ShapeDtypeStruct(shape, dtype) for _, (shape, dtype) in outputs],
        scratch_shapes=[pltpu.VMEM(shape, dtype) for shape, dtype in scratch]
        + [pltpu.SemaphoreType.DMA(shape) if shape else pltpu.SemaphoreType.REGULAR for shape in semaphores],
        compiler_params=pltpu.CompilerParams(
            collective_id=number,
            has_side_effects=number is not None,
            vmem_limit_bytes=VMEM_BYTES,
        ),
    )(*[value for _, value in inputs])


def shards(
    bits,
    frames,
    segment_ids,
    valid_frames,
    inward_weight,
    inward_bias,
    output_weight,
    upward_weight,
    upward_bias,
    downward_weight,
    norm_gains,
    offsets,
    cotangent,
):
    token_count, features = frames.shape
    count = segment_ids.shape[1]
    wide_count = padded(count)
    hidden = upward_weight.shape[2]
    rows = features // 2**bits
    corner_start = row_blocks(count)[-1][0]
    square = ((wide_count, features), LOW)
    square_wide = ((wide_count, features), WIDE)
    rows_wide = ((count, features), WIDE)
    b_shape = ((4, 8, 1152 + hidden), WIDE)
    marks = ((wide_count, LANES), LOW)
    corner_shape = ((count - corner_start, wide_count - corner_start), WIDE)
    plan = stream_plan(bits, features)
    grid = (2,) * bits + (rows,)
    buffers = []
    for _, columns, order, base in plan:
        buffers += [(shape, LOW) for shape in stream_shapes(bits, rows, columns[1], order, base)]
    own_chunk = ((rows, hidden), WIDE)
    small_shape = ((5, 8, features), WIDE)
    all_rows = ((4, count, features), LOW)
    results = call(
        functools.partial(layer_kernel, count, bits, plan),
        "layer",
        1,
        [
            (anywhere(), frames),
            (anywhere(), cotangent),
            (anywhere(), jnp.swapaxes(inward_weight[0], 1, 2)),
            (anywhere(), output_weight[0]),
            (anywhere(), upward_weight[0]),
            (anywhere(), downward_weight[0]),
            (inside(), jnp.swapaxes(inward_bias[0], 0, 1)),
            (inside(), upward_bias[0]),
            (inside(), segment_ids),
            (inside(), valid_frames),
            (inside(), norm_gains[0]),
            (inside(), offsets[0]),
        ],
        [
            (anywhere(), all_rows),
            (anywhere(), all_rows),
            (anywhere(), ((4, features, hidden), LOW)),
            (anywhere(), square),
            (anywhere(), square),
            (anywhere(), square),
            (anywhere(), rows_wide),
            (anywhere(), rows_wide),
            (inside(), own_chunk),
            (inside(), own_chunk),
            (inside(), own_chunk),
            (inside(), ((2, 8, features), WIDE)),
        ],
        [
            ((8, features, hidden), LOW),
            ((4, wide_count, hidden), LOW),
            ((4, wide_count, hidden), LOW),
            square,
            square,
            square,
            square,
            square,
            square,
            square_wide,
            square_wide,
            square_wide,
            ((3, 2) + grid + (hidden,), LOW),
            ((2, features, hidden), LOW),
            ((2, features, hidden), LOW),
            ((LANES, wide_count), LOW),
            ((LANES, wide_count), LOW),
            ((LANES, wide_count), WIDE),
            ((LANES, wide_count), WIDE),
            ((3, 8, LANES), WIDE),
            small_shape,
            ((2, 3, 8, features), WIDE),
            ((bits + 1, 2, 8, features), WIDE),
            ((bits, 2, 8, features), WIDE),
            b_shape,
            ((2, 8, 1152 + hidden), WIDE),
            ((16, wide_count), jnp.int32),
            marks,
            marks,
            corner_shape,
        ]
        + buffers,
        [(160,), (160,), (32,), ()],
    )
    out_all, frames_all = results[:2]
    down_rows, up_rows, inward_rows, sums = results[8:]
    pieces = 8
    tokens = token_count // pieces
    lines = upward_bias.shape[1]
    (
        layer_output,
        grad_frames,
        grad_inward,
        grad_pair,
        grad_outward,
        grad_up,
        grad_up_bias,
        grad_down,
        grad_gains,
        grad_offsets,
    ) = call(
        functools.partial(finish_kernel, rows, bits),
        "finish",
        None,
        [
            (anywhere(), out_all.reshape(token_count, features)),
            (anywhere(), frames_all.reshape(token_count, features)),
            (inside(), down_rows),
            (inside(), up_rows),
            (inside(), inward_rows),
            (inside(), sums),
        ],
        [
            (anywhere(), ((token_count, features), LOW)),
            (anywhere(), ((token_count, features), WIDE)),
            (inside(), ((1, 3, rows, 192), WIDE)),
            (inside(), ((3, 2, HEAD_SIZE // 2**bits), WIDE)),
            (inside(), ((1, 192, rows), WIDE)),
            (inside(), ((1, rows, hidden), WIDE)),
            (inside(), ((lines, 1, LANES // 2**bits), WIDE)),
            (inside(), ((rows, hidden), WIDE)),
            (inside(), ((1, 2, rows), WIDE)),
            (inside(), ((1, 4, rows), WIDE)),
        ],
        [
            ((pieces, tokens, features), LOW),
            ((pieces, tokens, features), LOW),
            ((pieces, tokens, features), WIDE),
        ],
        [(4, pieces)],
    )
    return (
        layer_output,
        grad_frames,
        grad_inward,
        jnp.swapaxes(grad_pair, 0, 1)[None],
        grad_outward,
        grad_up,
        jnp.swapaxes(grad_up_bias, 0, 1),
        grad_down.T[None],
        grad_gains,
        grad_offsets,
    )


def solution(mesh):
    bits = mesh.shape["dp"].bit_length() - 1
    in_specs = (
        P("dp", None),
        P("dp", None),
        P("dp", None),
        P(None, None, None, "tensor"),
        P(None, None, "tensor", None),
        P(None, "tensor", None),
        P(None, None, "tensor"),
        P(None, "tensor", None),
        P(None, "tensor", None),
        P(),
        P(),
        P("dp", None),
    )
    out_specs = (
        P("dp", None),
        P("dp", None),
        P(None, None, "dp", "tensor"),
        P(None, None, "tensor", "dp"),
        P(None, "tensor", "dp"),
        P(None, "dp", "tensor"),
        P(None, "tensor", "dp"),
        P(None, "tensor", "dp"),
        P(None, None, "dp"),
        P(None, None, "dp"),
    )
    return jax.shard_map(
        functools.partial(shards, bits),
        mesh=mesh,
        in_specs=in_specs,
        out_specs=out_specs,
        check_vma=False,
    )
```

```python
import functools
import itertools

import jax
import jax.numpy as jnp
from jax import lax
from jax.experimental import pallas as pl
from jax.experimental.pallas import tpu as pltpu
from jax.sharding import PartitionSpec as P

HEAD_SIZE = 64
LANES = 128
PAD = 128
LONGEST_CLIP_SHARE = 2
EPSILON = 1e-05
FAR = float(2**30)
LOW = jnp.bfloat16
WIDE = jnp.float32
MESH = pl.DeviceIdType.MESH
VMEM_BYTES = 61 << 20


def nn(left_side, right_side):
    return jnp.dot(left_side, right_side, preferred_element_type=WIDE)


def nt(left_side, right_side):
    return lax.dot_general(
        left_side, right_side, (((1,), (1,)), ((), ())), preferred_element_type=WIDE
    )


def padded(count):
    return -(-count // LANES) * LANES


def row_blocks(count, size=256):
    return [(start, min(size, count - start)) for start in range(0, count, size)]


def key_range(start, size, count):
    reach = count // LONGEST_CLIP_SHARE - 1
    low = max(0, (start - reach) // LANES * LANES)
    high = min(padded(count), padded(start + size + reach))
    return (low, high)


class Places:
    def __init__(self, bits):
        self.dp = lax.axis_index("dp")
        self.t = lax.axis_index("tensor")
        core = self.t % 2
        self.core = (self.dp, self.t + 1 - 2 * core)
        self.x = (self.dp, (self.t + 2) % 4)
        self.diagonal = (self.dp, 3 - self.t)
        self.bit = [(self.dp // 2**b) % 2 for b in range(bits)]
        self.step = [
            (self.dp + (1 - 2 * self.bit[b]) * 2**b, self.t) for b in range(bits)
        ]

    def greet(self, devices):
        barrier = pltpu.get_barrier_semaphore()
        for device in devices:
            pl.semaphore_signal(barrier, inc=1, device_id=device, device_id_type=MESH)
        pl.semaphore_wait(barrier, len(devices))


class Links:
    def __init__(self, send, recv, local):
        self.send, self.recv, self.local = send, recv, local
        self.used = self.used_local = 0

    def remote(self, source, target, device):
        place = self.used
        self.used += 1
        return pltpu.make_async_remote_copy(
            src_ref=source,
            dst_ref=target,
            send_sem=self.send.at[place],
            recv_sem=self.recv.at[place],
            device_id=device,
            device_id_type=MESH,
        )

    def near(self, source, target):
        place = self.used_local
        self.used_local += 1
        copy = pltpu.make_async_copy(source, target, self.local.at[place])
        copy.start()
        return copy


def start(copies):
    for copy in copies:
        copy.start()


def arrived(copies):
    for copy in copies:
        copy.wait_recv()


def sent(copies):
    for copy in copies:
        copy.wait_send()


class Gather:
    def __init__(self, places, links, part):
        self.places = places
        own, opposite = self.quarter(()), self.quarter((0, 1))

        def move(source, target, quarter, device):
            pairs = zip(part(source, quarter), part(target, quarter))
            return [links.remote(s, t, device) for s, t in pairs]

        self.core = move(0, 1, None, places.core)
        self.across = [move(0, 2, own, places.x), move(0, 2, opposite, places.x)]
        self.along = [move(2, 2, own, places.step[b]) for b in range(2)]
        self.passed = [
            move(2, 3, quarter, places.core)
            for quarter in (own, opposite, self.quarter((0,)), self.quarter((1,)))
        ]

    def quarter(self, flips):
        low, high = [
            1 - self.places.bit[b] if b in flips else self.places.bit[b] for b in range(2)
        ]
        return 2 * high + low

    def begin(self, number):
        start(self.across[number])

    def second(self):
        arrived(self.across[0])
        start(self.along[0] + self.along[1] + self.passed[0])

    def third(self):
        arrived(self.across[1])
        start(self.passed[1])

    def fourth(self):
        for b in range(2):
            arrived(self.along[b])
            start(self.passed[2 + b])

    def ready(self):
        for copies in self.passed:
            arrived(copies)

    def close(self):
        for copies in [self.core] + self.across + self.along + self.passed:
            sent(copies)


def lane_numbers():
    return lax.broadcasted_iota(jnp.int32, (1, LANES), 1)


def add_corner(scores, low, corner, corner_start):
    cut = corner_start - low
    return jnp.concatenate([scores[:, :cut], scores[:, cut:] + corner], axis=1)


def normalize(values):
    centred = values - jnp.mean(values, axis=-1, keepdims=True)
    rate = lax.rsqrt(jnp.mean(centred * centred, axis=-1, keepdims=True) + EPSILON)
    return (centred * rate, rate)


def normalize_back(grad, unit, rate, gain):
    scaled = grad * gain
    inner = jnp.mean(scaled * unit, axis=-1, keepdims=True)
    return rate * (scaled - jnp.mean(scaled, axis=-1, keepdims=True) - unit * inner)


def row_sum(values):
    return jnp.sum(values, axis=0, keepdims=True)


def gelu_pair(values):
    phi = 0.5 * (1.0 + lax.erf(values * 0.7071067811865476))
    density = jnp.exp(-0.5 * values * values) * 0.3989422804014327
    return (values * phi, phi + values * density)


class Stream:
    def __init__(self, bits, places, links, parts, buffers, out, columns, order, base):
        self.places = places
        self.dims = ["x"] + list(range(bits))[::-1]
        self.parts, self.buffers, self.out = parts, buffers, out
        self.columns, self.order, self.base = columns, order, base
        self.sends, self.done = [], 0
        for number, dim in enumerate(order):
            device = places.x if dim == "x" else places.step[dim]
            copies = {}
            split = number == 0 and dim != "x" and not base
            for slot in (1, 0) if split else (None,):
                fixed = self.fixed(number)
                fixed[dim] = 1 if dim == "x" else 1 - places.bit[dim]
                target = buffers[number]
                if slot is not None:
                    fixed["x"] = slot
                    target = target.at[slot]
                copies[slot] = links.remote(parts.at[self.index(fixed)], target, device)
            self.sends.append(copies)

    def fixed(self, number):
        fixed = {dim: 0 if dim == "x" else self.places.bit[dim] for dim in self.order[:number]}
        return {**fixed, **self.base}

    def index(self, fixed):
        place = tuple(fixed.get(dim, slice(None)) for dim in self.dims)
        return place + (slice(None), pl.ds(self.columns[0], self.columns[1]))

    def begin(self, number, slots=None):
        for slot, copy in self.sends[number].items():
            if slots is None or slot in slots:
                copy.start()

    def finish(self, number):
        arrived(self.sends[number].values())
        buffer = self.buffers[number]
        ends = slice(self.columns[0], self.columns[0] + self.columns[1])
        if self.base.get("x") == 1 and self.order[number] == "x":
            self.out[:, ends] += buffer[...].astype(WIDE)
            return
        keep = self.fixed(number + 1)
        rest = [dim for dim in self.dims if dim not in keep]
        for values in itertools.product(range(2), repeat=len(rest)):
            fixed = dict(keep)
            fixed.update(zip(rest, values))
            place = self.index(fixed)
            total = self.parts[place].astype(WIDE) + buffer[values].astype(WIDE)
            if number + 1 < len(self.order):
                self.parts[place] = total.astype(LOW)
            else:
                self.out[:, ends] = total

    def step(self):
        self.finish(self.done)
        self.done += 1
        if self.done < len(self.order):
            self.begin(self.done)

    def close(self):
        for copies in self.sends:
            sent(copies.values())


def stream_shapes(bits, rows, columns, order, base):
    dims = ["x"] + list(range(bits))
    shapes = []
    for number in range(len(order)):
        rest = [dim for dim in dims if dim not in order[: number + 1] and dim not in base]
        shapes.append((2,) * len(rest) + (rows, columns))
    return shapes


def stream_plan(bits, features):
    high = tuple(range(2, bits))
    third = features // 3
    down = [(0, 1, "x") + high, (0, 1, "x") + high, (1, 0, "x") + high]
    up = [("x", 1, 0) + high, (1, 0, "x") + high, (0, "x", 1) + high]
    late = [(0, 1) + high, (1, 0) + high, (0, 1) + high]
    plan = []
    for unit, orders in enumerate((down, up, late)):
        for number, order in enumerate(orders):
            columns = (third * number, third)
            if unit < 2:
                plan.append((unit, columns, order, {}))
            else:
                plan.append((unit, columns, order, {"x": 0}))
                plan.append((unit, columns, order + ("x",), {"x": 1}))
    return plan


def layer_kernel(
    count,
    bits,
    plan,
    frames,
    cotangent,
    w_own,
    o_own,
    u_own,
    d_own,
    pair_bias,
    up_bias_ref,
    seg_ref,
    valid_ref,
    gain_ref,
    offset_ref,
    out_all,
    frames_out,
    a_all,
    q_all,
    k_all,
    v_all,
    ctx_all,
    lse_all,
    down_out,
    up_out,
    inward_out,
    small_out,
    w_vm,
    act,
    slope,
    low_vm,
    low_t,
    grad_t,
    upper,
    grads_vm,
    out_vm,
    acc,
    dsecond,
    cot_vm,
    parts,
    staged,
    landed,
    query_t,
    pair_grad_t,
    dk_t,
    dv_t,
    bias_sums,
    small,
    small_in,
    pair_vm,
    pair_in,
    b_vm,
    b_own,
    row_vm,
    qf_ref,
    kf_ref,
    corner_ref,
    *rest,
):
    buffers, (send_sems, recv_sems, local_sems, free) = rest[:-4], rest[-4:]
    places = Places(bits)
    links = Links(send_sems, recv_sems, local_sems)
    wide_count = padded(count)
    features = low_vm.shape[1]
    frames_at = pl.ds(0, count)
    quarter_rows = features // 4
    own_rows = o_own.shape[0]
    part_rows = own_rows // 4
    x_vm, ctx_vm, lse_vm, a_vm = upper, cot_vm, dsecond, slope
    b_own[...] = jnp.zeros_like(b_own)
    for kind, at in ((0, 0), (1, 768)):
        heads = [pair_bias[h, kind : kind + 1].astype(WIDE) for h in range(3)]
        blank = jnp.zeros_like(heads[0])
        b_own[0, 0:1, at : at + 128] = jnp.concatenate([heads[0], heads[1]], axis=1)
        b_own[0, 0:1, at + 128 : at + 256] = jnp.concatenate([heads[2], blank], axis=1)
        b_own[1, 0:1, at + 128 : at + 256] = jnp.concatenate([blank, heads[0]], axis=1)
        b_own[1, 0:1, at + 256 : at + 384] = jnp.concatenate([heads[1], heads[2]], axis=1)
    for line in range(up_bias_ref.shape[0]):
        at = 1152 + LANES * line
        row = up_bias_ref[line : line + 1].astype(WIDE)
        b_own[0, 0:1, at : at + LANES] = row
        b_own[1, 0:1, at : at + LANES] = row
    places.greet([places.core, places.x, places.diagonal] + places.step)

    def span(quarter, rows):
        return (0, 4 * rows) if quarter is None else (quarter * rows, rows)

    def a_views(number, quarter, kinds):
        low, size = span(quarter, part_rows)
        if number == 0:
            return [o_own.at[pl.ds(low, size)] if k == 3 else w_own.at[k, pl.ds(low, size)] for k in kinds]
        group, at = number // 2, own_rows * (number % 2) + low
        return [
            a_vm.at[2 * group + k // 2, pl.ds(384 * (k % 2) + at, size)] for k in kinds
        ]

    def w_part(number, quarter):
        return a_views(number, quarter, (0, 1, 2))

    def o_part(number, quarter):
        return a_views(number, quarter, (3,))

    def u_part(number, quarter):
        low, size = span(quarter, quarter_rows)
        return [(w_vm.at[number] if number else u_own).at[pl.ds(low, size)]]

    def d_part(number, quarter):
        low, size = span(quarter, quarter_rows)
        return [(w_vm.at[4 + number] if number else d_own).at[pl.ds(low, size)]]

    w_gather, o_gather, u_gather, d_gather = [
        Gather(places, links, part) for part in (w_part, o_part, u_part, d_part)
    ]
    bias_copies = [
        links.remote(b_own.at[1], b_vm.at[1], places.core),
        links.remote(b_own.at[0], b_vm.at[2], places.x),
        links.remote(b_own.at[1], b_vm.at[3], places.diagonal),
    ]
    start(bias_copies)
    start(w_gather.core)
    w_gather.begin(0)
    start(o_gather.core)
    x_load = links.near(
        frames.at[pl.ds(places.t * count, count)], x_vm.at[frames_at]
    )
    a_loads = [
        links.near(source, target)
        for source, target in zip(
            a_views(0, None, range(4)),
            [a_vm.at[k // 2, pl.ds(384 * (k % 2), own_rows)] for k in range(4)],
        )
    ]
    u_load = links.near(u_own, w_vm.at[0])
    d_load = links.near(d_own, w_vm.at[4])
    left = lane_numbers() < HEAD_SIZE
    one = jnp.ones((), LOW)
    b_vm[0] = b_own[0]
    row_vm[0:8] = jnp.full((8, wide_count), -1, jnp.int32)
    row_vm[8:16] = jnp.zeros((8, wide_count), jnp.int32)
    row_vm[0:1, 0:count] = seg_ref[pl.ds(places.t, 1)]
    row_vm[8:9, 0:count] = valid_ref[pl.ds(places.t, 1)]
    corner_start = row_blocks(count)[-1][0]
    segments = jnp.broadcast_to(row_vm[0:1], (LANES, wide_count))
    valid = jnp.broadcast_to(row_vm[8:9], (LANES, wide_count))
    mark = lax.broadcasted_iota(jnp.int32, (LANES, wide_count), 0) % HEAD_SIZE
    frame = lax.broadcasted_iota(jnp.int32, (LANES, wide_count), 1)
    same = segments == mark
    query_marks = jnp.where(
        mark < 4,
        jnp.where(same, 0.0, -FAR),
        jnp.where(
            mark == 4,
            -FAR,
            jnp.where(mark == 5, jnp.where(frame < corner_start, -FAR, 0.0), 0.0),
        ),
    )
    key_marks_t = jnp.where(
        mark < 4,
        jnp.where(same, 1.0, 0.0),
        jnp.where(
            mark == 4,
            jnp.where(frame >= count, 1.0, 0.0),
            jnp.where(
                mark == 5,
                jnp.where(valid > 0, 0.0, 1.0),
                jnp.where(mark < 9, 1.0, 0.0),
            ),
        ),
    )
    qf_ref[...] = query_marks.astype(LOW).T
    kf_ref[...] = key_marks_t.astype(LOW).T
    corner_shape = (count - corner_start, wide_count - corner_start)
    open_keys = jnp.broadcast_to(row_vm[8:9, corner_start:], corner_shape) > 0
    itself = lax.broadcasted_iota(jnp.int32, corner_shape, 0) == lax.broadcasted_iota(
        jnp.int32, corner_shape, 1
    )
    corner_ref[...] = jnp.where(open_keys | itself, 0.0, -FAR)
    tail = jnp.zeros((wide_count - count, features), LOW)
    for number in range(3):
        act[number, count:] = tail
    x_load.wait()

    def project(group):
        bias = b_vm[2 * group, 0:1, 0:1152] + b_vm[2 * group + 1, 0:1, 0:1152]
        at = 384 * group
        for low, size in row_blocks(count):
            rows = x_vm[low : low + size]
            pair = (nt(rows, a_vm[2 * group]) + bias[:, 0:768]).astype(LOW)
            value = (nt(rows, a_vm[2 * group + 1, 0:384]) + bias[:, 768:1152]).astype(LOW)
            act[0, low : low + size, at : at + 384] = pair[:, 0:384] * 0.125
            act[1, low : low + size, at : at + 384] = pair[:, 384:768]
            act[2, low : low + size, at : at + 384] = value

    def attend_ahead(first, last):
        def body(pair, carry):
            at = pl.ds(pl.multiple_of(pair * LANES, LANES), LANES)
            keys, values, key_marks = act[1, :, at], act[2, :, at], kf_ref[...]
            key_sides = [jnp.where(left, keys, key_marks), jnp.where(left, key_marks, keys)]
            value_sides = [jnp.where(left, values, one), jnp.where(left, one, values)]
            for low, size in row_blocks(count):
                begin, end = key_range(low, size, count)
                rows = act[0, low : low + size, at]
                marks = qf_ref[low : low + size]
                query_sides = [jnp.where(left, rows, marks), jnp.where(left, marks, rows)]
                scores = [
                    nt(query, key[begin:end]) for query, key in zip(query_sides, key_sides)
                ]
                if low + size == count:
                    scores = [add_corner(s, begin, corner_ref[...], low) for s in scores]
                largest = [jnp.max(s, axis=1, keepdims=True) for s in scores]
                weights = [jnp.exp(s - m).astype(LOW) for s, m in zip(scores, largest)]
                sums = [nn(w, v[begin:end]) for w, v in zip(weights, value_sides)]
                numerator = jnp.where(left, sums[0], sums[1])
                denominator = pltpu.roll(jnp.where(left, sums[1], sums[0]), HEAD_SIZE, 1)
                ctx_vm[low : low + size, at] = numerator / denominator
                lse_vm[low : low + size, at] = jnp.where(
                    left, largest[0], largest[1]
                ) + jnp.log(denominator)
            return carry

        lax.fori_loop(first, last, body, 0)

    def mix(group):
        weights = a_vm[2 * group + 1, 384:768]
        at = 384 * group
        for low, size in row_blocks(count):
            term = nn(ctx_vm[low : low + size, at : at + 384].astype(LOW), weights)
            if group == 0:
                acc[low : low + size] = x_vm[low : low + size].astype(WIDE) + term
            else:
                acc[low : low + size] += term + offset_ref[0:1]

    stores = []
    for copy in a_loads:
        copy.wait()
    arrived(w_gather.core)
    arrived(bias_copies[:1])
    project(0)
    w_gather.begin(1)
    start(u_gather.core)
    attend_ahead(0, 1)
    o_gather.begin(0)
    o_gather.begin(1)
    attend_ahead(1, 2)
    w_gather.second()
    u_gather.begin(0)
    attend_ahead(2, 3)
    arrived(o_gather.core)
    mix(0)
    d_gather.begin(0)
    w_gather.third()
    start(d_gather.core)
    w_gather.fourth()
    arrived(bias_copies[1:])
    w_gather.ready()
    project(1)
    o_gather.second()
    for number, target in enumerate((q_all, k_all, v_all)):
        stores.append(links.near(act.at[number], target))
    attend_ahead(3, 4)
    u_gather.begin(1)
    attend_ahead(4, 5)
    o_gather.third()
    o_gather.fourth()
    attend_ahead(5, 6)
    u_gather.second()
    d_gather.begin(1)
    ctx_store = links.near(ctx_vm.at[frames_at], ctx_all)
    lse_store = links.near(lse_vm.at[frames_at], lse_all)
    o_gather.ready()
    stores.append(links.near(a_vm, a_all))
    mix(1)
    mixed_vm = dsecond
    grid = parts.shape[2:-1]
    outs = (down_out, up_out, inward_out)
    streams, used = [], 0
    for unit, columns, order, base in plan:
        own_buffers = buffers[used : used + len(order)]
        used += len(order)
        streams.append(
            Stream(
                bits,
                places,
                links,
                parts.at[unit],
                own_buffers,
                outs[unit],
                columns,
                order,
                base,
            )
        )
    units = [streams[0:3], streams[3:6], streams[6::2], streams[7::2]]
    gain_one, gain_two = gain_ref[0:1], gain_ref[1:2]
    lse_store.wait()
    for low, size in row_blocks(count):
        mixed = acc[low : low + size]
        mixed_vm[low : low + size] = mixed
        unit, _ = normalize(mixed)
        rows = unit * gain_one + offset_ref[2:3]
        low_vm[low : low + size] = rows.astype(LOW)
        acc[low : low + size] = rows + offset_ref[1:2]
    ctx_store.wait()
    for copy in stores:
        copy.wait()
    cot_load = links.near(
        cotangent.at[pl.ds(places.t * count, count)], cot_vm.at[frames_at]
    )
    low_vm[count:] = tail
    upper[count:] = tail

    def raise_rows(number):
        bias = b_vm[number, 0:1, 1152:1920]
        for low, size in row_blocks(count):
            upward = nn(low_vm[low : low + size], w_vm[number]) + bias
            value, rate = gelu_pair(upward)
            act[number, low : low + size] = value.astype(LOW)
            slope[number, low : low + size] = rate.astype(LOW)
        act[number, count:] = tail

    def lower_rows(number):
        for low, size in row_blocks(count):
            acc[low : low + size] += nn(act[number, low : low + size], w_vm[4 + number])

    w_gather.close()
    o_gather.close()
    sent(bias_copies)
    u_load.wait()
    raise_rows(0)
    d_gather.second()
    d_load.wait()
    lower_rows(0)
    u_gather.third()
    u_gather.fourth()
    arrived(u_gather.core)
    raise_rows(1)
    arrived(d_gather.core)
    lower_rows(1)
    u_gather.ready()
    raise_rows(2)
    raise_rows(3)
    d_gather.third()
    d_gather.fourth()
    d_gather.ready()
    lower_rows(2)
    lower_rows(3)
    cot_load.wait()
    sums = [jnp.zeros((1, features), WIDE) for _ in range(3)]
    for low, size in row_blocks(count):
        unit, rate = normalize(acc[low : low + size])
        out_vm[low : low + size] = (unit * gain_two + offset_ref[3:4]).astype(LOW)
        grad = cot_vm[low : low + size]
        back = normalize_back(grad, unit, rate, gain_two)
        acc[low : low + size] = back
        sums = [
            sums[0] + row_sum(grad * unit),
            sums[1] + row_sum(grad),
            sums[2] + row_sum(back),
        ]
    gain_two_sum, shift_two_sum, down_bias_sum = sums

    class Spread:
        def __init__(self, source, target):
            own = target.at[places.t]
            self.to_core = links.remote(source.at[frames_at], own, places.core)
            self.to_x = links.remote(source.at[frames_at], own, places.x)
            beside = target.at[places.x[1]]
            self.passed = links.remote(beside, beside, places.core)
            self.to_x.start()
            self.to_core.start()
            self.kept = links.near(source.at[frames_at], own)

        def hand_on(self):
            self.to_x.wait_recv()
            self.passed.start()

        def source_free(self):
            self.to_core.wait_send()
            self.to_x.wait_send()
            self.kept.wait()

        def close(self):
            self.to_core.wait_recv()
            self.passed.wait()

    out_spread = Spread(out_vm, out_all)
    ctx_load = links.near(ctx_all, cot_vm.at[frames_at])
    low_t[...] = low_vm[...].T
    for low, size in row_blocks(count):
        low_vm[low : low + size] = acc[low : low + size].astype(LOW)
    grad_t[...] = low_vm[...].T

    def back(number):
        total = jnp.zeros((1, features), WIDE)
        for low, size in row_blocks(count):
            inner = nt(low_vm[low : low + size], w_vm[4 + number])
            rows = (slope[number, low : low + size].astype(WIDE) * inner).astype(LOW)
            upper[low : low + size] = rows
            total += row_sum(rows.astype(WIDE))
            acc[low : low + size] += nt(rows, w_vm[number])
        return total

    def grads(unit, number, finish):
        rows, other = ((grad_t, act.at[number]), (low_t, upper))[unit]
        for low, size in row_blocks(features):
            finish(unit, low, size, nn(rows[low : low + size], other[...]))

    swaps = [
        [links.remote(staged.at[odd], landed.at[odd], places.core) for odd in range(2)]
        for _ in range(2)
    ]
    chunk = grid[-1]
    indices = list(itertools.product(range(2), repeat=bits))

    def put(unit, even, low, value):
        for place, index in enumerate(indices):
            begin = place * chunk
            if low <= begin and begin + chunk <= low + value.shape[0]:
                parts[(unit, even) + index] = value[begin - low : begin - low + chunk]
            elif low <= begin < low + value.shape[0]:
                cut = low + value.shape[0] - begin
                parts[(unit, even) + index + (slice(0, cut),)] = value[begin - low :]
            elif begin < low < begin + chunk:
                cut = low - begin
                parts[(unit, even) + index + (slice(cut, chunk),)] = value[: chunk - cut]

    def give(odd):
        def finish(unit, low, size, value):
            staged[odd, low : low + size] = value.astype(LOW)

        return finish

    def take(even):
        def finish(unit, low, size, value):
            total = value + landed[1 - even, low : low + size].astype(WIDE)
            put(unit, even, low, total.astype(LOW))

        return finish

    def allow():
        pl.semaphore_signal(free, inc=1, device_id=places.core, device_id_type=MESH)

    def hand_over(unit, number, odd):
        grads(unit, number, give(odd))
        swaps[unit][odd].start()

    def combined(unit, number, even, slots):
        swaps[unit][1 - even].wait_recv()
        grads(unit, number, take(even))
        for stream in units[unit]:
            stream.begin(0, slots)
        allow()

    up_bias = {}
    hand_over(0, 3, 0)
    hand_over(0, 1, 1)
    up_bias[3] = back(3)
    combined(0, 2, 1, (1, None))
    combined(0, 0, 0, (0,))
    head_loads = [
        links.near(source, act.at[n]) for n, source in enumerate((q_all, k_all, v_all))
    ]
    sent(swaps[0])
    pl.semaphore_wait(free, 1)
    hand_over(1, 3, 0)
    up_bias[2] = back(2)
    combined(1, 2, 1, (1, None))
    up_bias[1] = back(1)
    pl.semaphore_wait(free, 1)
    hand_over(1, 1, 1)
    up_bias[0] = back(0)
    u_gather.close()
    d_gather.close()
    a_load = links.near(a_all, w_vm.at[pl.ds(0, 4)])
    combined(1, 0, 0, (0,))
    sent(swaps[1])
    x_load = links.near(frames.at[pl.ds(places.t * count, count)], upper.at[frames_at])
    sums = [jnp.zeros((1, features), WIDE) for _ in range(3)]
    for low, size in row_blocks(count):
        unit, rate = normalize(mixed_vm[low : low + size])
        grad = acc[low : low + size]
        back_rows = normalize_back(grad, unit, rate, gain_one)
        acc[low : low + size] = back_rows
        low_vm[low : low + size] = back_rows.astype(LOW)
        sums = [
            sums[0] + row_sum(grad * unit),
            sums[1] + row_sum(grad),
            sums[2] + row_sum(back_rows),
        ]
    gain_one_sum, shift_one_sum, out_bias_sum = sums
    lse_load = links.near(lse_all, lse_vm.at[frames_at])
    small[...] = jnp.zeros_like(small)
    for place, number in ((0, 0), (1, 2), (3, 1), (4, 3)):
        small[place, 0:1] = up_bias[number]
    for place, row in enumerate(
        (gain_one_sum, gain_two_sum, out_bias_sum, down_bias_sum, shift_one_sum, shift_two_sum)
    ):
        small[2, place : place + 1] = row
    m_low, m_t, x_vm, x_t = low_vm, low_t, upper, grad_t
    m_t[...] = m_low[...].T
    x_load.wait()
    x_t[...] = x_vm[...].T
    a_load.wait()
    ctx_load.wait()
    lanes = lane_numbers()
    mark = lanes % HEAD_SIZE
    value_marks = jnp.where(mark < 3, 1.0, 0.0).astype(LOW)
    grads_vm[count:] = tail
    for number in range(4):
        slope[number, count:] = tail
    for group in range(2):
        for low, size in row_blocks(count):
            at = 384 * group
            rows = nt(m_low[low : low + size], w_vm[2 * group + 1, 384:768])
            grads_vm[low : low + size, at : at + 384] = rows.astype(LOW)
            slope[2 + group, low : low + size, 384:768] = ctx_vm[
                low : low + size, at : at + 384
            ].astype(LOW)
    for copy in head_loads:
        copy.wait()
    lse_load.wait()

    def thirds(values):
        high = values.astype(LOW)
        rest_one = values - high.astype(WIDE)
        middle = rest_one.astype(LOW)
        return (high, middle, (rest_one - middle.astype(WIDE)).astype(LOW))

    def attend(group, first, last):
        def body(pair, carry):
            at = pl.ds(pl.multiple_of((3 * group + pair) * LANES, LANES), LANES)
            at_query = pl.ds(pl.multiple_of(pair * LANES, LANES), LANES)
            at_key = pl.ds(pl.multiple_of(384 + pair * LANES, LANES), LANES)
            keys, values, key_marks = act[1, :, at], act[2, :, at], kf_ref[...]
            key_sides = [jnp.where(left, keys, key_marks), jnp.where(left, key_marks, keys)]
            value_sides = [
                jnp.where(left, values, value_marks),
                jnp.where(left, value_marks, values),
            ]
            query_t[...] = act[0, :, at].T
            pair_grad_t[...] = grads_vm[:, at].T
            query_sum = jnp.zeros((1, LANES), WIDE)
            for number, (low, size) in enumerate(row_blocks(count)):
                begin, end = key_range(low, size, count)
                rows = act[0, low : low + size, at]
                total = pltpu.roll(lse_vm[low : low + size, at], HEAD_SIZE, 1)
                high, middle, rest_low = thirds(-total)
                marks = jnp.where(
                    mark == 6,
                    high,
                    jnp.where(
                        mark == 7,
                        middle,
                        jnp.where(mark == 8, rest_low, qf_ref[low : low + size]),
                    ),
                )
                query_sides = [jnp.where(left, rows, marks), jnp.where(left, marks, rows)]
                grad = grads_vm[low : low + size, at]
                product = grad.astype(WIDE) * ctx_vm[low : low + size, at]
                inner_left = jnp.sum(jnp.where(left, product, 0.0), axis=1, keepdims=True)
                inner_right = jnp.sum(jnp.where(left, 0.0, product), axis=1, keepdims=True)
                high, middle, rest_low = thirds(-jnp.where(left, inner_right, inner_left))
                grad_marks = jnp.where(
                    mark == 0,
                    high,
                    jnp.where(
                        mark == 1, middle, jnp.where(mark == 2, rest_low, jnp.zeros((), LOW))
                    ),
                )
                grad_sides = [
                    jnp.where(left, grad, grad_marks),
                    jnp.where(left, grad_marks, grad),
                ]
                scores = [
                    nt(query, key[begin:end]) for query, key in zip(query_sides, key_sides)
                ]
                if low + size == count:
                    scores = [add_corner(s, begin, corner_ref[...], low) for s in scores]
                probs = [jnp.exp(s) for s in scores]
                prob_grads = [
                    nt(one, value[begin:end]) for one, value in zip(grad_sides, value_sides)
                ]
                probs_low = [p.astype(LOW) for p in probs]
                score_grads = [(p * g).astype(LOW) for p, g in zip(probs, prob_grads)]
                query_grads = [
                    nn(s, key[begin:end]) for s, key in zip(score_grads, key_sides)
                ]
                query_grad = (jnp.where(left, query_grads[0], query_grads[1]) * 0.125).astype(LOW)
                slope[group, low : low + size, at_query] = query_grad
                query_sum += row_sum(query_grad.astype(WIDE))
                for side in range(2):
                    part = slice(HEAD_SIZE * side, HEAD_SIZE * side + HEAD_SIZE)
                    value_term = nn(pair_grad_t[part, low : low + size], probs_low[side])
                    key_term = nn(query_t[part, low : low + size], score_grads[side])
                    if number == 0:
                        dv_t[part, begin:end] = value_term
                        dk_t[part, begin:end] = key_term
                        if end < wide_count:
                            blank = jnp.zeros((HEAD_SIZE, wide_count - end), WIDE)
                            dv_t[part, end:] = blank
                            dk_t[part, end:] = blank
                    else:
                        dv_t[part, begin:end] += value_term
                        dk_t[part, begin:end] += key_term
            key_grad = dk_t[...].astype(LOW).T
            value_grad = dv_t[...].astype(LOW).T
            slope[group, :, at_key] = key_grad
            slope[2 + group, :, at_query] = value_grad
            bias_sums[pair, 0:1] = query_sum
            bias_sums[pair, 1:2] = row_sum(value_grad.astype(WIDE))
            return carry

        lax.fori_loop(first, last, body, 0)

    def other_side(values):
        return pltpu.roll(values, HEAD_SIZE, 1)

    def packed(blocks, odd):
        if odd:
            turned = [(other_side(b[1]), other_side(b[2])) for b in blocks]
            outer = [jnp.where(left, one, two) for one, two in turned]
        else:
            outer = [b[0] for b in blocks]
        joined = []
        for n in range(0, len(blocks), 2):
            if odd:
                joined.append(jnp.where(left, turned[n][1], blocks[n + 1][2]))
            else:
                joined.append(jnp.where(left, blocks[n][1], other_side(blocks[n + 1][1])))
        return jnp.concatenate(outer + joined, axis=1)

    def split(values):
        return [values[:, LANES * p : LANES * (p + 1)] for p in range(3)]

    def weight_grads(group):
        for low, size in row_blocks(features):
            pair = nn(x_t[low : low + size], slope[group])
            value = nn(x_t[low : low + size], slope[2 + group, :, 0:384])
            outward = nn(m_t[low : low + size], slope[2 + group, :, 384:768])
            blocks = [split(pair[:, :384]), split(pair[:, 384:]), split(value), split(outward)]
            staged[1 - group, low : low + size] = packed(blocks, True).astype(LOW)
            put(2, group, low, packed(blocks, False).astype(LOW))

    def bias_grads(group):
        rows = [[bias_sums[p, kind : kind + 1] for p in range(3)] for kind in range(2)]
        for place, odd in ((1 if group else 0, False), (4 if group else 3, True)):
            small[place, 1:2, 0:384] = packed(rows, odd)

    def input_grads(group):
        for low, size in row_blocks(count):
            acc[low : low + size] += nn(slope[group, low : low + size], w_vm[2 * group]) + nn(
                slope[2 + group, low : low + size, 0:384], w_vm[2 * group + 1, 0:384]
            )

    last_swaps = [links.remote(staged.at[1 - g], landed.at[1 - g], places.core) for g in range(2)]

    def combine(group):
        arrived([last_swaps[group]])
        for place, index in enumerate(indices):
            rows = slice(place * chunk, (place + 1) * chunk)
            total = parts[(2, group) + index].astype(WIDE) + landed[1 - group, rows].astype(WIDE)
            parts[(2, group) + index] = total.astype(LOW)


    downs, ups, own_late, far_late = units

    def steps(*streams):
        for stream in streams:
            stream.step()

    steps(downs[0], downs[2])
    attend(1, 0, 1)
    out_spread.hand_on()
    steps(downs[1])
    attend(1, 1, 2)
    steps(ups[1])
    attend(1, 2, 3)
    steps(downs[0])
    weight_grads(1)
    pl.semaphore_wait(free, 1)
    start([last_swaps[1]])
    bias_grads(1)
    steps(ups[2], ups[0])
    input_grads(1)
    steps(downs[1], downs[2])
    combine(1)
    for stream in far_late:
        stream.begin(0)
    attend(0, 0, 1)
    attend(0, 1, 2)
    steps(ups[1], downs[0])
    attend(0, 2, 3)
    steps(ups[2], ups[0])
    bias_grads(0)
    small_core = links.remote(small.at[pl.ds(2, 3)], small_in.at[0], places.core)
    small_core.start()
    input_grads(0)
    out_spread.source_free()
    out_spread.close()
    small_core.wait()
    small[2] += small_in[0, 0]
    small[0] += small_in[0, 1]
    small[1] += small_in[0, 2]
    small_x = links.remote(small.at[pl.ds(1, 2)], small_in.at[1, pl.ds(0, 2)], places.x)
    small_x.start()
    own_out = grads_vm
    for low, size in row_blocks(count):
        own_out[low : low + size] = acc[low : low + size].astype(LOW)
    frames_spread = Spread(own_out, frames_out)
    weight_grads(0)
    pl.semaphore_wait(free, 1)
    start([last_swaps[0]])
    steps(far_late[0], downs[2])
    small_x.wait()
    pair_vm[0, 0] = small[0] + small_in[1, 0]
    pair_vm[0, 1] = small[2] + small_in[1, 1]
    small_steps = [
        links.remote(pair_vm.at[b], pair_in.at[b], places.step[b]) for b in range(bits)
    ]
    small_steps[0].start()
    combine(0)
    for stream in own_late:
        stream.begin(0)

    def small_step(number):
        if number < bits:
            small_steps[number].wait()
            pair_vm[number + 1] = pair_vm[number] + pair_in[number]
            if number + 1 < bits:
                small_steps[number + 1].start()

    early = downs + ups
    steps(far_late[2], downs[1], ups[1])
    steps(own_late[0], far_late[1], far_late[0])
    small_step(0)
    steps(own_late[1], ups[0], ups[2])
    steps(own_late[2], own_late[0], far_late[2], far_late[1])
    steps(own_late[1], own_late[2], *far_late)
    small_step(1)
    steps(*own_late)
    for number in range(2, bits):
        small_step(number)
    frames_spread.hand_on()
    while True:
        waiting = [one for one in early + own_late if one.done < len(one.order)]
        waiting += [one for one in far_late if one.done + 1 < len(one.order)]
        if not waiting:
            break
        steps(*waiting)
    steps(*far_late)
    small_out[...] = pair_vm[bits]
    frames_spread.source_free()
    frames_spread.close()
    for stream in streams:
        stream.close()
    sent(last_swaps)


def finish_kernel(
    bits,
    out_all,
    frames_all,
    down_rows,
    up_rows,
    inward_rows,
    sums,
    out_ref,
    frames_ref,
    inward_ref,
    outward_ref,
    up_ref,
    down_ref,
    inward_bias_ref,
    up_bias_ref,
    gain_ref,
    offset_ref,
    out_vm,
    low_vm,
    wide_vm,
    rows_vm,
    sums_vm,
    inward_vm,
    outward_vm,
    sems,
    few_sems,
):
    pieces, tokens = out_vm.shape[:2]
    rows = rows_vm.shape[1]
    dp_place = lax.axis_index("dp")
    few = [
        pltpu.make_async_copy(source, target, few_sems.at[n])
        for n, (source, target) in enumerate(
            (
                (sums, sums_vm),
                (inward_rows, rows_vm.at[0]),
                (down_rows, rows_vm.at[1]),
                (up_rows, rows_vm.at[2]),
                (rows_vm.at[1], down_ref),
                (rows_vm.at[2], up_ref.at[0]),
                (inward_vm, inward_ref),
                (outward_vm, outward_ref),
            )
        )
    ]
    start(few[:4])
    spots = [pl.ds(n * tokens, tokens) for n in range(pieces)]
    low_loads = [
        pltpu.make_async_copy(frames_all.at[at], low_vm.at[n], sems.at[0, n])
        for n, at in enumerate(spots)
    ]
    out_loads = [
        pltpu.make_async_copy(out_all.at[at], out_vm.at[n], sems.at[1, n])
        for n, at in enumerate(spots)
    ]
    for n in range(pieces):
        low_loads[n].start()
        out_loads[n].start()
    for copy in few[:4]:
        copy.wait()
    start(few[4:6])

    def turned(values):
        filled = jnp.concatenate([values, jnp.zeros((LANES - rows, values.shape[1]), WIDE)], axis=0)
        return filled.T[:, :rows]

    def kind(number):
        outer = rows_vm[0, :, 128 * number : 128 * number + 128]
        inner = rows_vm[0, :, 512 + 128 * (number // 2) : 640 + 128 * (number // 2)]
        if number % 2:
            inner = pltpu.roll(inner, HEAD_SIZE, 1)
        return outer, inner

    for number in range(3):
        outer, inner = kind(number)
        inward_vm[0, number, :, 0:128] = outer
        inward_vm[0, number, :, 128:192] = inner[:, :HEAD_SIZE]
    outer, inner = kind(3)
    outward_vm[0, 0:128] = turned(outer)
    outward_vm[0, 128:192] = turned(inner)[:HEAD_SIZE]
    start(few[6:])

    def own_part(values, part):
        width = values.shape[1]
        return pltpu.roll(values, lax.rem(width - dp_place * part, width), 1)[:, :part]

    share = rows_vm.shape[2] // 2**bits
    wide_share = own_part(sums_vm[1], share)
    gain_ref[0] = wide_share[0:2]
    offset_ref[0] = wide_share[2:6]
    lines = up_bias_ref.shape[0]
    part = LANES // 2**bits
    for line in range(lines):
        block = sums_vm[0, 0:8, LANES * line : LANES * (line + 1)]
        up_bias_ref[line] = own_part(block, part)[0:1]
    part = HEAD_SIZE // 2**bits
    for number in range(2):
        outer = sums_vm[0, 0:8, 128 * number : 128 * number + 128]
        inner = sums_vm[0, 0:8, 256:384]
        if number:
            inner = pltpu.roll(inner, HEAD_SIZE, 1)
        for head, block in enumerate((outer, pltpu.roll(outer, HEAD_SIZE, 1), inner)):
            inward_bias_ref[head, number : number + 1] = own_part(block, part)[1:2]
    stores = few[4:]
    for n, at in enumerate(spots):
        low_loads[n].wait()
        wide_vm[n] = low_vm[n].astype(WIDE)
        stores.append(pltpu.make_async_copy(wide_vm.at[n], frames_ref.at[at], sems.at[2, n]))
        stores[-1].start()
        out_loads[n].wait()
        stores.append(pltpu.make_async_copy(out_vm.at[n], out_ref.at[at], sems.at[3, n]))
        stores[-1].start()
    for copy in stores:
        copy.wait()


def anywhere():
    return pl.BlockSpec(memory_space=pl.ANY)


def inside():
    return pl.BlockSpec(memory_space=pltpu.VMEM)


def call(kernel, name, number, inputs, outputs, scratch, semaphores):
    return pl.pallas_call(
        kernel,
        name=name,
        in_specs=[spec for spec, _ in inputs],
        out_specs=[spec for spec, _ in outputs],
        out_shape=[jax.ShapeDtypeStruct(shape, dtype) for _, (shape, dtype) in outputs],
        scratch_shapes=[pltpu.VMEM(shape, dtype) for shape, dtype in scratch]
        + [pltpu.SemaphoreType.DMA(shape) if shape else pltpu.SemaphoreType.REGULAR for shape in semaphores],
        compiler_params=pltpu.CompilerParams(
            collective_id=number,
            has_side_effects=number is not None,
            vmem_limit_bytes=VMEM_BYTES,
        ),
    )(*[value for _, value in inputs])


def shards(
    bits,
    frames,
    segment_ids,
    valid_frames,
    inward_weight,
    inward_bias,
    output_weight,
    upward_weight,
    upward_bias,
    downward_weight,
    norm_gains,
    offsets,
    cotangent,
):
    token_count, features = frames.shape
    count = segment_ids.shape[1]
    wide_count = padded(count)
    hidden = upward_weight.shape[2]
    rows = features // 2**bits
    corner_start = row_blocks(count)[-1][0]
    square = ((wide_count, features), LOW)
    square_wide = ((wide_count, features), WIDE)
    rows_wide = ((count, features), WIDE)
    b_shape = ((4, 8, 1152 + hidden), WIDE)
    marks = ((wide_count, LANES), LOW)
    corner_shape = ((count - corner_start, wide_count - corner_start), WIDE)
    plan = stream_plan(bits, features)
    grid = (2,) * bits + (rows,)
    buffers = []
    for _, columns, order, base in plan:
        buffers += [(shape, LOW) for shape in stream_shapes(bits, rows, columns[1], order, base)]
    own_chunk = ((rows, hidden), WIDE)
    small_shape = ((5, 8, features), WIDE)
    all_rows = ((4, count, features), LOW)
    results = call(
        functools.partial(layer_kernel, count, bits, plan),
        "layer",
        1,
        [
            (anywhere(), frames),
            (anywhere(), cotangent),
            (anywhere(), jnp.swapaxes(inward_weight[0], 1, 2)),
            (anywhere(), output_weight[0]),
            (anywhere(), upward_weight[0]),
            (anywhere(), downward_weight[0]),
            (inside(), jnp.swapaxes(inward_bias[0], 0, 1)),
            (inside(), upward_bias[0]),
            (inside(), segment_ids),
            (inside(), valid_frames),
            (inside(), norm_gains[0]),
            (inside(), offsets[0]),
        ],
        [
            (anywhere(), all_rows),
            (anywhere(), all_rows),
            (anywhere(), ((4, features, hidden), LOW)),
            (anywhere(), square),
            (anywhere(), square),
            (anywhere(), square),
            (anywhere(), rows_wide),
            (anywhere(), rows_wide),
            (inside(), own_chunk),
            (inside(), own_chunk),
            (inside(), own_chunk),
            (inside(), ((2, 8, features), WIDE)),
        ],
        [
            ((8, features, hidden), LOW),
            ((4, wide_count, hidden), LOW),
            ((4, wide_count, hidden), LOW),
            square,
            square,
            square,
            square,
            square,
            square,
            square_wide,
            square_wide,
            square_wide,
            ((3, 2) + grid + (hidden,), LOW),
            ((2, features, hidden), LOW),
            ((2, features, hidden), LOW),
            ((LANES, wide_count), LOW),
            ((LANES, wide_count), LOW),
            ((LANES, wide_count), WIDE),
            ((LANES, wide_count), WIDE),
            ((3, 8, LANES), WIDE),
            small_shape,
            ((2, 3, 8, features), WIDE),
            ((bits + 1, 2, 8, features), WIDE),
            ((bits, 2, 8, features), WIDE),
            b_shape,
            ((2, 8, 1152 + hidden), WIDE),
            ((16, wide_count), jnp.int32),
            marks,
            marks,
            corner_shape,
        ]
        + buffers,
        [(160,), (160,), (32,), ()],
    )
    out_all, frames_all = results[:2]
    down_rows, up_rows, inward_rows, sums = results[8:]
    pieces = 8
    tokens = token_count // pieces
    lines = upward_bias.shape[1]
    inward_shape = ((1, 3, rows, 192), WIDE)
    outward_shape = ((1, 192, rows), WIDE)
    (
        layer_output,
        grad_frames,
        grad_inward,
        grad_outward,
        grad_up,
        grad_down,
        grad_pair,
        grad_up_bias,
        grad_gains,
        grad_offsets,
    ) = call(
        functools.partial(finish_kernel, bits),
        "finish",
        None,
        [
            (anywhere(), out_all.reshape(token_count, features)),
            (anywhere(), frames_all.reshape(token_count, features)),
            (anywhere(), down_rows),
            (anywhere(), up_rows),
            (anywhere(), inward_rows),
            (anywhere(), sums),
        ],
        [
            (anywhere(), ((token_count, features), LOW)),
            (anywhere(), ((token_count, features), WIDE)),
            (anywhere(), inward_shape),
            (anywhere(), outward_shape),
            (anywhere(), ((1, rows, hidden), WIDE)),
            (anywhere(), ((rows, hidden), WIDE)),
            (inside(), ((3, 2, HEAD_SIZE // 2**bits), WIDE)),
            (inside(), ((lines, 1, LANES // 2**bits), WIDE)),
            (inside(), ((1, 2, rows), WIDE)),
            (inside(), ((1, 4, rows), WIDE)),
        ],
        [
            ((pieces, tokens, features), LOW),
            ((pieces, tokens, features), LOW),
            ((pieces, tokens, features), WIDE),
            ((3, rows, hidden), WIDE),
            ((2, 8, features), WIDE),
            inward_shape,
            outward_shape,
        ],
        [(4, pieces), (8,)],
    )
    return (
        layer_output,
        grad_frames,
        grad_inward,
        jnp.swapaxes(grad_pair, 0, 1)[None],
        grad_outward,
        grad_up,
        jnp.swapaxes(grad_up_bias, 0, 1),
        grad_down.T[None],
        grad_gains,
        grad_offsets,
    )


def solution(mesh):
    bits = mesh.shape["dp"].bit_length() - 1
    in_specs = (
        P("dp", None),
        P("dp", None),
        P("dp", None),
        P(None, None, None, "tensor"),
        P(None, None, "tensor", None),
        P(None, "tensor", None),
        P(None, None, "tensor"),
        P(None, "tensor", None),
        P(None, "tensor", None),
        P(),
        P(),
        P("dp", None),
    )
    out_specs = (
        P("dp", None),
        P("dp", None),
        P(None, None, "dp", "tensor"),
        P(None, None, "tensor", "dp"),
        P(None, "tensor", "dp"),
        P(None, "dp", "tensor"),
        P(None, "tensor", "dp"),
        P(None, "tensor", "dp"),
        P(None, None, "dp"),
        P(None, None, "dp"),
    )
    return jax.shard_map(
        functools.partial(shards, bits),
        mesh=mesh,
        in_specs=in_specs,
        out_specs=out_specs,
        check_vma=False,
    )
```

```python
import functools
import itertools

import jax
import jax.numpy as jnp
from jax import lax
from jax.experimental import pallas as pl
from jax.experimental.pallas import tpu as pltpu
from jax.sharding import PartitionSpec as P

HEAD_SIZE = 64
LANES = 128
PAD = 128
LONGEST_CLIP_SHARE = 2
EPSILON = 1e-05
FAR = float(2**30)
LOW = jnp.bfloat16
WIDE = jnp.float32
MESH = pl.DeviceIdType.MESH
VMEM_BYTES = 61 << 20


def nn(left_side, right_side):
    return jnp.dot(left_side, right_side, preferred_element_type=WIDE)


def nt(left_side, right_side):
    return lax.dot_general(
        left_side, right_side, (((1,), (1,)), ((), ())), preferred_element_type=WIDE
    )


def padded(count):
    return -(-count // LANES) * LANES


def row_blocks(count, size=256):
    return [(start, min(size, count - start)) for start in range(0, count, size)]


def key_range(start, size, count):
    reach = count // LONGEST_CLIP_SHARE - 1
    low = max(0, (start - reach) // LANES * LANES)
    high = min(padded(count), padded(start + size + reach))
    return (low, high)


class Places:
    def __init__(self, bits):
        self.dp = lax.axis_index("dp")
        self.t = lax.axis_index("tensor")
        core = self.t % 2
        self.core = (self.dp, self.t + 1 - 2 * core)
        self.x = (self.dp, (self.t + 2) % 4)
        self.diagonal = (self.dp, 3 - self.t)
        self.bit = [(self.dp // 2**b) % 2 for b in range(bits)]
        self.step = [
            (self.dp + (1 - 2 * self.bit[b]) * 2**b, self.t) for b in range(bits)
        ]

    def greet(self, devices):
        barrier = pltpu.get_barrier_semaphore()
        for device in devices:
            pl.semaphore_signal(barrier, inc=1, device_id=device, device_id_type=MESH)
        pl.semaphore_wait(barrier, len(devices))


class Links:
    def __init__(self, send, recv, local):
        self.send, self.recv, self.local = send, recv, local
        self.used = self.used_local = 0

    def remote(self, source, target, device):
        place = self.used
        self.used += 1
        return pltpu.make_async_remote_copy(
            src_ref=source,
            dst_ref=target,
            send_sem=self.send.at[place],
            recv_sem=self.recv.at[place],
            device_id=device,
            device_id_type=MESH,
        )

    def near(self, source, target):
        place = self.used_local
        self.used_local += 1
        copy = pltpu.make_async_copy(source, target, self.local.at[place])
        copy.start()
        return copy


def start(copies):
    for copy in copies:
        copy.start()


def arrived(copies):
    for copy in copies:
        copy.wait_recv()


def sent(copies):
    for copy in copies:
        copy.wait_send()


class Gather:
    def __init__(self, places, links, part):
        self.places = places
        own, opposite = self.quarter(()), self.quarter((0, 1))

        def move(source, target, quarter, device):
            pairs = zip(part(source, quarter), part(target, quarter))
            return [links.remote(s, t, device) for s, t in pairs]

        self.core = move(0, 1, None, places.core)
        self.across = [move(0, 2, own, places.x), move(0, 2, opposite, places.x)]
        self.along = [move(2, 2, own, places.step[b]) for b in range(2)]
        self.passed = [
            move(2, 3, quarter, places.core)
            for quarter in (own, opposite, self.quarter((0,)), self.quarter((1,)))
        ]

    def quarter(self, flips):
        low, high = [
            1 - self.places.bit[b] if b in flips else self.places.bit[b] for b in range(2)
        ]
        return 2 * high + low

    def begin(self, number):
        start(self.across[number])

    def second(self):
        arrived(self.across[0])
        start(self.along[0] + self.along[1] + self.passed[0])

    def third(self):
        arrived(self.across[1])
        start(self.passed[1])

    def fourth(self):
        for b in range(2):
            arrived(self.along[b])
            start(self.passed[2 + b])

    def ready(self):
        for copies in self.passed:
            arrived(copies)

    def close(self):
        for copies in [self.core] + self.across + self.along + self.passed:
            sent(copies)


def lane_numbers():
    return lax.broadcasted_iota(jnp.int32, (1, LANES), 1)


def add_corner(scores, low, corner, corner_start):
    cut = corner_start - low
    return jnp.concatenate([scores[:, :cut], scores[:, cut:] + corner], axis=1)


def normalize(values):
    centred = values - jnp.mean(values, axis=-1, keepdims=True)
    rate = lax.rsqrt(jnp.mean(centred * centred, axis=-1, keepdims=True) + EPSILON)
    return (centred * rate, rate)


def normalize_back(grad, unit, rate, gain):
    scaled = grad * gain
    inner = jnp.mean(scaled * unit, axis=-1, keepdims=True)
    return rate * (scaled - jnp.mean(scaled, axis=-1, keepdims=True) - unit * inner)


def row_sum(values):
    return jnp.sum(values, axis=0, keepdims=True)


def gelu_pair(values):
    phi = 0.5 * (1.0 + lax.erf(values * 0.7071067811865476))
    density = jnp.exp(-0.5 * values * values) * 0.3989422804014327
    return (values * phi, phi + values * density)


class Stream:
    def __init__(self, bits, places, links, parts, buffers, out, columns, order, base):
        self.places = places
        self.dims = ["x"] + list(range(bits))[::-1]
        self.parts, self.buffers, self.out = parts, buffers, out
        self.columns, self.order, self.base = columns, order, base
        self.sends, self.done = [], 0
        for number, dim in enumerate(order):
            device = places.x if dim == "x" else places.step[dim]
            copies = {}
            split = number == 0 and dim != "x" and not base
            for slot in (1, 0) if split else (None,):
                fixed = self.fixed(number)
                fixed[dim] = 1 if dim == "x" else 1 - places.bit[dim]
                target = buffers[number]
                if slot is not None:
                    fixed["x"] = slot
                    target = target.at[slot]
                copies[slot] = links.remote(parts.at[self.index(fixed)], target, device)
            self.sends.append(copies)

    def fixed(self, number):
        fixed = {dim: 0 if dim == "x" else self.places.bit[dim] for dim in self.order[:number]}
        return {**fixed, **self.base}

    def index(self, fixed):
        place = tuple(fixed.get(dim, slice(None)) for dim in self.dims)
        return place + (slice(None), pl.ds(self.columns[0], self.columns[1]))

    def begin(self, number, slots=None):
        for slot, copy in self.sends[number].items():
            if slots is None or slot in slots:
                copy.start()

    def finish(self, number):
        arrived(self.sends[number].values())
        buffer = self.buffers[number]
        ends = slice(self.columns[0], self.columns[0] + self.columns[1])
        if self.base.get("x") == 1 and self.order[number] == "x":
            self.out[:, ends] += buffer[...].astype(WIDE)
            return
        keep = self.fixed(number + 1)
        rest = [dim for dim in self.dims if dim not in keep]
        for values in itertools.product(range(2), repeat=len(rest)):
            fixed = dict(keep)
            fixed.update(zip(rest, values))
            place = self.index(fixed)
            total = self.parts[place].astype(WIDE) + buffer[values].astype(WIDE)
            if number + 1 < len(self.order):
                self.parts[place] = total.astype(LOW)
            else:
                self.out[:, ends] = total

    def step(self):
        self.finish(self.done)
        self.done += 1
        if self.done < len(self.order):
            self.begin(self.done)

    def close(self):
        for copies in self.sends:
            sent(copies.values())


def stream_shapes(bits, rows, columns, order, base):
    dims = ["x"] + list(range(bits))
    shapes = []
    for number in range(len(order)):
        rest = [dim for dim in dims if dim not in order[: number + 1] and dim not in base]
        shapes.append((2,) * len(rest) + (rows, columns))
    return shapes


def stream_plan(bits, features):
    high = tuple(range(2, bits))
    third = features // 3
    down = [(0, 1, "x") + high, (0, 1, "x") + high, (1, 0, "x") + high]
    up = [("x", 1, 0) + high, (1, 0, "x") + high, (0, "x", 1) + high]
    late = [(0, 1) + high, (1, 0) + high, (0, 1) + high]
    plan = []
    for unit, orders in enumerate((down, up, late)):
        for number, order in enumerate(orders):
            columns = (third * number, third)
            if unit < 2:
                plan.append((unit, columns, order, {}))
            else:
                plan.append((unit, columns, order, {"x": 0}))
                plan.append((unit, columns, order + ("x",), {"x": 1}))
    return plan


def layer_kernel(
    count,
    bits,
    plan,
    frames,
    cotangent,
    w_own,
    o_own,
    u_own,
    d_own,
    pair_bias,
    up_bias_ref,
    seg_ref,
    valid_ref,
    gain_ref,
    offset_ref,
    out_all,
    frames_out,
    a_all,
    q_all,
    k_all,
    v_all,
    ctx_all,
    lse_all,
    down_out,
    up_out,
    inward_out,
    small_out,
    w_vm,
    act,
    slope,
    low_vm,
    low_t,
    grad_t,
    upper,
    grads_vm,
    out_vm,
    acc,
    dsecond,
    cot_vm,
    parts,
    staged,
    landed,
    query_t,
    pair_grad_t,
    dk_t,
    dv_t,
    bias_sums,
    small,
    small_in,
    pair_vm,
    pair_in,
    b_vm,
    b_own,
    row_vm,
    qf_ref,
    kf_ref,
    corner_ref,
    *rest,
):
    buffers, (send_sems, recv_sems, local_sems, free) = rest[:-4], rest[-4:]
    places = Places(bits)
    links = Links(send_sems, recv_sems, local_sems)
    wide_count = padded(count)
    features = low_vm.shape[1]
    frames_at = pl.ds(0, count)
    quarter_rows = features // 4
    own_rows = o_own.shape[0]
    part_rows = own_rows // 4
    x_vm, ctx_vm, lse_vm, a_vm = upper, cot_vm, dsecond, slope
    b_own[...] = jnp.zeros_like(b_own)
    for kind, at in ((0, 0), (1, 768)):
        heads = [pair_bias[h, kind : kind + 1].astype(WIDE) for h in range(3)]
        blank = jnp.zeros_like(heads[0])
        b_own[0, 0:1, at : at + 128] = jnp.concatenate([heads[0], heads[1]], axis=1)
        b_own[0, 0:1, at + 128 : at + 256] = jnp.concatenate([heads[2], blank], axis=1)
        b_own[1, 0:1, at + 128 : at + 256] = jnp.concatenate([blank, heads[0]], axis=1)
        b_own[1, 0:1, at + 256 : at + 384] = jnp.concatenate([heads[1], heads[2]], axis=1)
    for line in range(up_bias_ref.shape[0]):
        at = 1152 + LANES * line
        row = up_bias_ref[line : line + 1].astype(WIDE)
        b_own[0, 0:1, at : at + LANES] = row
        b_own[1, 0:1, at : at + LANES] = row
    places.greet([places.core, places.x, places.diagonal] + places.step)

    def span(quarter, rows):
        return (0, 4 * rows) if quarter is None else (quarter * rows, rows)

    def a_views(number, quarter, kinds):
        low, size = span(quarter, part_rows)
        if number == 0:
            return [o_own.at[pl.ds(low, size)] if k == 3 else w_own.at[k, pl.ds(low, size)] for k in kinds]
        group, at = number // 2, own_rows * (number % 2) + low
        return [
            a_vm.at[2 * group + k // 2, pl.ds(384 * (k % 2) + at, size)] for k in kinds
        ]

    def w_part(number, quarter):
        return a_views(number, quarter, (0, 1, 2))

    def o_part(number, quarter):
        return a_views(number, quarter, (3,))

    def u_part(number, quarter):
        low, size = span(quarter, quarter_rows)
        return [(w_vm.at[number] if number else u_own).at[pl.ds(low, size)]]

    def d_part(number, quarter):
        low, size = span(quarter, quarter_rows)
        return [(w_vm.at[4 + number] if number else d_own).at[pl.ds(low, size)]]

    w_gather, o_gather, u_gather, d_gather = [
        Gather(places, links, part) for part in (w_part, o_part, u_part, d_part)
    ]
    bias_copies = [
        links.remote(b_own.at[1], b_vm.at[1], places.core),
        links.remote(b_own.at[0], b_vm.at[2], places.x),
        links.remote(b_own.at[1], b_vm.at[3], places.diagonal),
    ]
    start(bias_copies)
    start(w_gather.core)
    w_gather.begin(0)
    start(o_gather.core)
    x_load = links.near(
        frames.at[pl.ds(places.t * count, count)], x_vm.at[frames_at]
    )
    a_loads = [
        links.near(source, target)
        for source, target in zip(
            a_views(0, None, range(4)),
            [a_vm.at[k // 2, pl.ds(384 * (k % 2), own_rows)] for k in range(4)],
        )
    ]
    u_load = links.near(u_own, w_vm.at[0])
    d_load = links.near(d_own, w_vm.at[4])
    left = lane_numbers() < HEAD_SIZE
    one = jnp.ones((), LOW)
    b_vm[0] = b_own[0]
    row_vm[0:8] = jnp.full((8, wide_count), -1, jnp.int32)
    row_vm[8:16] = jnp.zeros((8, wide_count), jnp.int32)
    row_vm[0:1, 0:count] = seg_ref[pl.ds(places.t, 1)]
    row_vm[8:9, 0:count] = valid_ref[pl.ds(places.t, 1)]
    corner_start = row_blocks(count)[-1][0]
    segments = jnp.broadcast_to(row_vm[0:1], (LANES, wide_count))
    valid = jnp.broadcast_to(row_vm[8:9], (LANES, wide_count))
    mark = lax.broadcasted_iota(jnp.int32, (LANES, wide_count), 0) % HEAD_SIZE
    frame = lax.broadcasted_iota(jnp.int32, (LANES, wide_count), 1)
    same = segments == mark
    query_marks = jnp.where(
        mark < 4,
        jnp.where(same, 0.0, -FAR),
        jnp.where(
            mark == 4,
            -FAR,
            jnp.where(mark == 5, jnp.where(frame < corner_start, -FAR, 0.0), 0.0),
        ),
    )
    key_marks_t = jnp.where(
        mark < 4,
        jnp.where(same, 1.0, 0.0),
        jnp.where(
            mark == 4,
            jnp.where(frame >= count, 1.0, 0.0),
            jnp.where(
                mark == 5,
                jnp.where(valid > 0, 0.0, 1.0),
                jnp.where(mark < 9, 1.0, 0.0),
            ),
        ),
    )
    qf_ref[...] = query_marks.astype(LOW).T
    kf_ref[...] = key_marks_t.astype(LOW).T
    corner_shape = (count - corner_start, wide_count - corner_start)
    open_keys = jnp.broadcast_to(row_vm[8:9, corner_start:], corner_shape) > 0
    itself = lax.broadcasted_iota(jnp.int32, corner_shape, 0) == lax.broadcasted_iota(
        jnp.int32, corner_shape, 1
    )
    corner_ref[...] = jnp.where(open_keys | itself, 0.0, -FAR)
    tail = jnp.zeros((wide_count - count, features), LOW)
    for number in range(3):
        act[number, count:] = tail
    x_load.wait()

    def project(group):
        bias = b_vm[2 * group, 0:1, 0:1152] + b_vm[2 * group + 1, 0:1, 0:1152]
        at = 384 * group
        for low, size in row_blocks(count):
            rows = x_vm[low : low + size]
            pair = (nt(rows, a_vm[2 * group]) + bias[:, 0:768]).astype(LOW)
            value = (nt(rows, a_vm[2 * group + 1, 0:384]) + bias[:, 768:1152]).astype(LOW)
            act[0, low : low + size, at : at + 384] = pair[:, 0:384] * 0.125
            act[1, low : low + size, at : at + 384] = pair[:, 384:768]
            act[2, low : low + size, at : at + 384] = value

    def attend_ahead(first, last):
        def body(pair, carry):
            at = pl.ds(pl.multiple_of(pair * LANES, LANES), LANES)
            keys, values, key_marks = act[1, :, at], act[2, :, at], kf_ref[...]
            key_sides = [jnp.where(left, keys, key_marks), jnp.where(left, key_marks, keys)]
            value_sides = [jnp.where(left, values, one), jnp.where(left, one, values)]
            for low, size in row_blocks(count):
                begin, end = key_range(low, size, count)
                rows = act[0, low : low + size, at]
                marks = qf_ref[low : low + size]
                query_sides = [jnp.where(left, rows, marks), jnp.where(left, marks, rows)]
                scores = [
                    nt(query, key[begin:end]) for query, key in zip(query_sides, key_sides)
                ]
                if low + size == count:
                    scores = [add_corner(s, begin, corner_ref[...], low) for s in scores]
                largest = [jnp.max(s, axis=1, keepdims=True) for s in scores]
                weights = [jnp.exp(s - m).astype(LOW) for s, m in zip(scores, largest)]
                sums = [nn(w, v[begin:end]) for w, v in zip(weights, value_sides)]
                numerator = jnp.where(left, sums[0], sums[1])
                denominator = pltpu.roll(jnp.where(left, sums[1], sums[0]), HEAD_SIZE, 1)
                ctx_vm[low : low + size, at] = numerator / denominator
                lse_vm[low : low + size, at] = jnp.where(
                    left, largest[0], largest[1]
                ) + jnp.log(denominator)
            return carry

        lax.fori_loop(first, last, body, 0)

    def mix(group):
        weights = a_vm[2 * group + 1, 384:768]
        at = 384 * group
        for low, size in row_blocks(count):
            term = nn(ctx_vm[low : low + size, at : at + 384].astype(LOW), weights)
            if group == 0:
                acc[low : low + size] = x_vm[low : low + size].astype(WIDE) + term
            else:
                acc[low : low + size] += term + offset_ref[0:1]

    stores = []
    for copy in a_loads:
        copy.wait()
    arrived(w_gather.core)
    arrived(bias_copies[:1])
    project(0)
    w_gather.begin(1)
    start(u_gather.core)
    attend_ahead(0, 1)
    o_gather.begin(0)
    o_gather.begin(1)
    attend_ahead(1, 2)
    w_gather.second()
    u_gather.begin(0)
    attend_ahead(2, 3)
    arrived(o_gather.core)
    mix(0)
    d_gather.begin(0)
    w_gather.third()
    start(d_gather.core)
    w_gather.fourth()
    arrived(bias_copies[1:])
    w_gather.ready()
    project(1)
    o_gather.second()
    for number, target in enumerate((q_all, k_all, v_all)):
        stores.append(links.near(act.at[number], target))
    attend_ahead(3, 4)
    u_gather.begin(1)
    attend_ahead(4, 5)
    o_gather.third()
    o_gather.fourth()
    attend_ahead(5, 6)
    u_gather.second()
    d_gather.begin(1)
    ctx_store = links.near(ctx_vm.at[frames_at], ctx_all)
    lse_store = links.near(lse_vm.at[frames_at], lse_all)
    o_gather.ready()
    stores.append(links.near(a_vm, a_all))
    mix(1)
    mixed_vm = dsecond
    grid = parts.shape[2:-1]
    outs = (down_out, up_out, inward_out)
    streams, used = [], 0
    for unit, columns, order, base in plan:
        own_buffers = buffers[used : used + len(order)]
        used += len(order)
        streams.append(
            Stream(
                bits,
                places,
                links,
                parts.at[unit],
                own_buffers,
                outs[unit],
                columns,
                order,
                base,
            )
        )
    units = [streams[0:3], streams[3:6], streams[6::2], streams[7::2]]
    gain_one, gain_two = gain_ref[0:1], gain_ref[1:2]
    lse_store.wait()
    for low, size in row_blocks(count):
        mixed = acc[low : low + size]
        mixed_vm[low : low + size] = mixed
        unit, _ = normalize(mixed)
        rows = unit * gain_one + offset_ref[2:3]
        low_vm[low : low + size] = rows.astype(LOW)
        acc[low : low + size] = rows + offset_ref[1:2]
    ctx_store.wait()
    for copy in stores:
        copy.wait()
    cot_load = links.near(
        cotangent.at[pl.ds(places.t * count, count)], cot_vm.at[frames_at]
    )
    low_vm[count:] = tail
    upper[count:] = tail

    def raise_rows(number):
        bias = b_vm[number, 0:1, 1152:1920]
        for low, size in row_blocks(count):
            upward = nn(low_vm[low : low + size], w_vm[number]) + bias
            value, rate = gelu_pair(upward)
            act[number, low : low + size] = value.astype(LOW)
            slope[number, low : low + size] = rate.astype(LOW)
        act[number, count:] = tail

    def lower_rows(number):
        for low, size in row_blocks(count):
            acc[low : low + size] += nn(act[number, low : low + size], w_vm[4 + number])

    w_gather.close()
    o_gather.close()
    sent(bias_copies)
    u_load.wait()
    raise_rows(0)
    d_gather.second()
    d_load.wait()
    lower_rows(0)
    u_gather.third()
    u_gather.fourth()
    arrived(u_gather.core)
    raise_rows(1)
    arrived(d_gather.core)
    lower_rows(1)
    u_gather.ready()
    raise_rows(2)
    raise_rows(3)
    d_gather.third()
    d_gather.fourth()
    d_gather.ready()
    lower_rows(2)
    lower_rows(3)
    cot_load.wait()
    sums = [jnp.zeros((1, features), WIDE) for _ in range(3)]
    for low, size in row_blocks(count):
        unit, rate = normalize(acc[low : low + size])
        out_vm[low : low + size] = (unit * gain_two + offset_ref[3:4]).astype(LOW)
        grad = cot_vm[low : low + size]
        back = normalize_back(grad, unit, rate, gain_two)
        acc[low : low + size] = back
        sums = [
            sums[0] + row_sum(grad * unit),
            sums[1] + row_sum(grad),
            sums[2] + row_sum(back),
        ]
    gain_two_sum, shift_two_sum, down_bias_sum = sums

    class Spread:
        def __init__(self, source, target):
            own = target.at[places.t]
            self.to_core = links.remote(source.at[frames_at], own, places.core)
            self.to_x = links.remote(source.at[frames_at], own, places.x)
            beside = target.at[places.x[1]]
            self.passed = links.remote(beside, beside, places.core)
            self.to_x.start()
            self.to_core.start()
            self.kept = links.near(source.at[frames_at], own)

        def hand_on(self):
            self.to_x.wait_recv()
            self.passed.start()

        def source_free(self):
            self.to_core.wait_send()
            self.to_x.wait_send()
            self.kept.wait()

        def close(self):
            self.to_core.wait_recv()
            self.passed.wait()

    out_spread = Spread(out_vm, out_all)
    ctx_load = links.near(ctx_all, cot_vm.at[frames_at])
    low_t[...] = low_vm[...].T
    for low, size in row_blocks(count):
        low_vm[low : low + size] = acc[low : low + size].astype(LOW)
    grad_t[...] = low_vm[...].T

    def back(number):
        total = jnp.zeros((1, features), WIDE)
        for low, size in row_blocks(count):
            inner = nt(low_vm[low : low + size], w_vm[4 + number])
            rows = (slope[number, low : low + size].astype(WIDE) * inner).astype(LOW)
            upper[low : low + size] = rows
            total += row_sum(rows.astype(WIDE))
            acc[low : low + size] += nt(rows, w_vm[number])
        return total

    def grads(unit, number, finish):
        rows, other = ((grad_t, act.at[number]), (low_t, upper))[unit]
        for low, size in row_blocks(features):
            finish(unit, low, size, nn(rows[low : low + size], other[...]))

    swaps = [
        [links.remote(staged.at[odd], landed.at[odd], places.core) for odd in range(2)]
        for _ in range(2)
    ]
    chunk = grid[-1]
    indices = list(itertools.product(range(2), repeat=bits))

    def put(unit, even, low, value):
        for place, index in enumerate(indices):
            begin = place * chunk
            if low <= begin and begin + chunk <= low + value.shape[0]:
                parts[(unit, even) + index] = value[begin - low : begin - low + chunk]
            elif low <= begin < low + value.shape[0]:
                cut = low + value.shape[0] - begin
                parts[(unit, even) + index + (slice(0, cut),)] = value[begin - low :]
            elif begin < low < begin + chunk:
                cut = low - begin
                parts[(unit, even) + index + (slice(cut, chunk),)] = value[: chunk - cut]

    def give(odd):
        def finish(unit, low, size, value):
            staged[odd, low : low + size] = value.astype(LOW)

        return finish

    def take(even):
        def finish(unit, low, size, value):
            total = value + landed[1 - even, low : low + size].astype(WIDE)
            put(unit, even, low, total.astype(LOW))

        return finish

    def allow():
        pl.semaphore_signal(free, inc=1, device_id=places.core, device_id_type=MESH)

    def hand_over(unit, number, odd):
        grads(unit, number, give(odd))
        swaps[unit][odd].start()

    def combined(unit, number, even, slots):
        swaps[unit][1 - even].wait_recv()
        grads(unit, number, take(even))
        for stream in units[unit]:
            stream.begin(0, slots)
        allow()

    up_bias = {}
    hand_over(0, 3, 0)
    hand_over(0, 1, 1)
    up_bias[3] = back(3)
    combined(0, 2, 1, (1, None))
    combined(0, 0, 0, (0,))
    head_loads = [
        links.near(source, act.at[n]) for n, source in enumerate((q_all, k_all, v_all))
    ]
    sent(swaps[0])
    pl.semaphore_wait(free, 1)
    hand_over(1, 3, 0)
    up_bias[2] = back(2)
    combined(1, 2, 1, (1, None))
    up_bias[1] = back(1)
    pl.semaphore_wait(free, 1)
    hand_over(1, 1, 1)
    up_bias[0] = back(0)
    u_gather.close()
    d_gather.close()
    a_load = links.near(a_all, w_vm.at[pl.ds(0, 4)])
    combined(1, 0, 0, (0,))
    sent(swaps[1])
    x_load = links.near(frames.at[pl.ds(places.t * count, count)], upper.at[frames_at])
    sums = [jnp.zeros((1, features), WIDE) for _ in range(3)]
    for low, size in row_blocks(count):
        unit, rate = normalize(mixed_vm[low : low + size])
        grad = acc[low : low + size]
        back_rows = normalize_back(grad, unit, rate, gain_one)
        acc[low : low + size] = back_rows
        low_vm[low : low + size] = back_rows.astype(LOW)
        sums = [
            sums[0] + row_sum(grad * unit),
            sums[1] + row_sum(grad),
            sums[2] + row_sum(back_rows),
        ]
    gain_one_sum, shift_one_sum, out_bias_sum = sums
    lse_load = links.near(lse_all, lse_vm.at[frames_at])
    small[...] = jnp.zeros_like(small)
    for place, number in ((0, 0), (1, 2), (3, 1), (4, 3)):
        small[place, 0:1] = up_bias[number]
    for place, row in enumerate(
        (gain_one_sum, gain_two_sum, out_bias_sum, down_bias_sum, shift_one_sum, shift_two_sum)
    ):
        small[2, place : place + 1] = row
    m_low, m_t, x_vm, x_t = low_vm, low_t, upper, grad_t
    m_t[...] = m_low[...].T
    x_load.wait()
    x_t[...] = x_vm[...].T
    a_load.wait()
    ctx_load.wait()
    lanes = lane_numbers()
    mark = lanes % HEAD_SIZE
    value_marks = jnp.where(mark < 3, 1.0, 0.0).astype(LOW)
    grads_vm[count:] = tail
    for number in range(4):
        slope[number, count:] = tail
    for group in range(2):
        for low, size in row_blocks(count):
            at = 384 * group
            rows = nt(m_low[low : low + size], w_vm[2 * group + 1, 384:768])
            grads_vm[low : low + size, at : at + 384] = rows.astype(LOW)
            slope[2 + group, low : low + size, 384:768] = ctx_vm[
                low : low + size, at : at + 384
            ].astype(LOW)
    for copy in head_loads:
        copy.wait()
    lse_load.wait()

    def thirds(values):
        high = values.astype(LOW)
        rest_one = values - high.astype(WIDE)
        middle = rest_one.astype(LOW)
        return (high, middle, (rest_one - middle.astype(WIDE)).astype(LOW))

    def attend(group, first, last):
        def body(pair, carry):
            at = pl.ds(pl.multiple_of((3 * group + pair) * LANES, LANES), LANES)
            at_query = pl.ds(pl.multiple_of(pair * LANES, LANES), LANES)
            at_key = pl.ds(pl.multiple_of(384 + pair * LANES, LANES), LANES)
            keys, values, key_marks = act[1, :, at], act[2, :, at], kf_ref[...]
            key_sides = [jnp.where(left, keys, key_marks), jnp.where(left, key_marks, keys)]
            value_sides = [
                jnp.where(left, values, value_marks),
                jnp.where(left, value_marks, values),
            ]
            query_t[...] = act[0, :, at].T
            pair_grad_t[...] = grads_vm[:, at].T
            query_sum = jnp.zeros((1, LANES), WIDE)
            for number, (low, size) in enumerate(row_blocks(count)):
                begin, end = key_range(low, size, count)
                rows = act[0, low : low + size, at]
                total = pltpu.roll(lse_vm[low : low + size, at], HEAD_SIZE, 1)
                high, middle, rest_low = thirds(-total)
                marks = jnp.where(
                    mark == 6,
                    high,
                    jnp.where(
                        mark == 7,
                        middle,
                        jnp.where(mark == 8, rest_low, qf_ref[low : low + size]),
                    ),
                )
                query_sides = [jnp.where(left, rows, marks), jnp.where(left, marks, rows)]
                grad = grads_vm[low : low + size, at]
                product = grad.astype(WIDE) * ctx_vm[low : low + size, at]
                inner_left = jnp.sum(jnp.where(left, product, 0.0), axis=1, keepdims=True)
                inner_right = jnp.sum(jnp.where(left, 0.0, product), axis=1, keepdims=True)
                high, middle, rest_low = thirds(-jnp.where(left, inner_right, inner_left))
                grad_marks = jnp.where(
                    mark == 0,
                    high,
                    jnp.where(
                        mark == 1, middle, jnp.where(mark == 2, rest_low, jnp.zeros((), LOW))
                    ),
                )
                grad_sides = [
                    jnp.where(left, grad, grad_marks),
                    jnp.where(left, grad_marks, grad),
                ]
                scores = [
                    nt(query, key[begin:end]) for query, key in zip(query_sides, key_sides)
                ]
                if low + size == count:
                    scores = [add_corner(s, begin, corner_ref[...], low) for s in scores]
                probs = [jnp.exp(s) for s in scores]
                prob_grads = [
                    nt(one, value[begin:end]) for one, value in zip(grad_sides, value_sides)
                ]
                probs_low = [p.astype(LOW) for p in probs]
                score_grads = [(p * g).astype(LOW) for p, g in zip(probs, prob_grads)]
                query_grads = [
                    nn(s, key[begin:end]) for s, key in zip(score_grads, key_sides)
                ]
                query_grad = (jnp.where(left, query_grads[0], query_grads[1]) * 0.125).astype(LOW)
                slope[group, low : low + size, at_query] = query_grad
                query_sum += row_sum(query_grad.astype(WIDE))
                for side in range(2):
                    part = slice(HEAD_SIZE * side, HEAD_SIZE * side + HEAD_SIZE)
                    value_term = nn(pair_grad_t[part, low : low + size], probs_low[side])
                    key_term = nn(query_t[part, low : low + size], score_grads[side])
                    if number == 0:
                        dv_t[part, begin:end] = value_term
                        dk_t[part, begin:end] = key_term
                        if end < wide_count:
                            blank = jnp.zeros((HEAD_SIZE, wide_count - end), WIDE)
                            dv_t[part, end:] = blank
                            dk_t[part, end:] = blank
                    else:
                        dv_t[part, begin:end] += value_term
                        dk_t[part, begin:end] += key_term
            key_grad = dk_t[...].astype(LOW).T
            value_grad = dv_t[...].astype(LOW).T
            slope[group, :, at_key] = key_grad
            slope[2 + group, :, at_query] = value_grad
            bias_sums[pair, 0:1] = query_sum
            bias_sums[pair, 1:2] = row_sum(value_grad.astype(WIDE))
            return carry

        lax.fori_loop(first, last, body, 0)

    def other_side(values):
        return pltpu.roll(values, HEAD_SIZE, 1)

    def packed(blocks, odd):
        if odd:
            turned = [(other_side(b[1]), other_side(b[2])) for b in blocks]
            outer = [jnp.where(left, one, two) for one, two in turned]
        else:
            outer = [b[0] for b in blocks]
        joined = []
        for n in range(0, len(blocks), 2):
            if odd:
                joined.append(jnp.where(left, turned[n][1], blocks[n + 1][2]))
            else:
                joined.append(jnp.where(left, blocks[n][1], other_side(blocks[n + 1][1])))
        return jnp.concatenate(outer + joined, axis=1)

    def split(values):
        return [values[:, LANES * p : LANES * (p + 1)] for p in range(3)]

    def weight_grads(group):
        for low, size in row_blocks(features):
            pair = nn(x_t[low : low + size], slope[group])
            value = nn(x_t[low : low + size], slope[2 + group, :, 0:384])
            outward = nn(m_t[low : low + size], slope[2 + group, :, 384:768])
            blocks = [split(pair[:, :384]), split(pair[:, 384:]), split(value), split(outward)]
            staged[1 - group, low : low + size] = packed(blocks, True).astype(LOW)
            put(2, group, low, packed(blocks, False).astype(LOW))

    def bias_grads(group):
        rows = [[bias_sums[p, kind : kind + 1] for p in range(3)] for kind in range(2)]
        for place, odd in ((1 if group else 0, False), (4 if group else 3, True)):
            small[place, 1:2, 0:384] = packed(rows, odd)

    def input_grads(group):
        for low, size in row_blocks(count):
            acc[low : low + size] += nn(slope[group, low : low + size], w_vm[2 * group]) + nn(
                slope[2 + group, low : low + size, 0:384], w_vm[2 * group + 1, 0:384]
            )

    last_swaps = [links.remote(staged.at[1 - g], landed.at[1 - g], places.core) for g in range(2)]

    def combine(group):
        arrived([last_swaps[group]])
        for place, index in enumerate(indices):
            rows = slice(place * chunk, (place + 1) * chunk)
            total = parts[(2, group) + index].astype(WIDE) + landed[1 - group, rows].astype(WIDE)
            parts[(2, group) + index] = total.astype(LOW)


    downs, ups, own_late, far_late = units

    def steps(*streams):
        for stream in streams:
            stream.step()

    steps(downs[0], downs[2])
    attend(1, 0, 1)
    out_spread.hand_on()
    steps(downs[1])
    attend(1, 1, 2)
    steps(ups[1])
    attend(1, 2, 3)
    steps(downs[0])
    weight_grads(1)
    pl.semaphore_wait(free, 1)
    start([last_swaps[1]])
    bias_grads(1)
    steps(ups[2], ups[0])
    input_grads(1)
    steps(downs[1], downs[2])
    combine(1)
    for stream in far_late:
        stream.begin(0)
    attend(0, 0, 1)
    attend(0, 1, 2)
    steps(ups[1], downs[0])
    attend(0, 2, 3)
    steps(downs[2], downs[1], ups[2], ups[0])
    bias_grads(0)
    small_core = links.remote(small.at[pl.ds(2, 3)], small_in.at[0], places.core)
    small_core.start()
    input_grads(0)
    out_spread.source_free()
    out_spread.close()
    small_core.wait()
    small[2] += small_in[0, 0]
    small[0] += small_in[0, 1]
    small[1] += small_in[0, 2]
    small_x = links.remote(small.at[pl.ds(1, 2)], small_in.at[1, pl.ds(0, 2)], places.x)
    small_x.start()
    steps(ups[1])
    own_out = grads_vm
    for low, size in row_blocks(count):
        own_out[low : low + size] = acc[low : low + size].astype(LOW)
    frames_spread = Spread(own_out, frames_out)
    weight_grads(0)
    pl.semaphore_wait(free, 1)
    start([last_swaps[0]])
    steps(far_late[0])
    small_x.wait()
    pair_vm[0, 0] = small[0] + small_in[1, 0]
    pair_vm[0, 1] = small[2] + small_in[1, 1]
    small_steps = [
        links.remote(pair_vm.at[b], pair_in.at[b], places.step[b]) for b in range(bits)
    ]
    small_steps[0].start()
    combine(0)
    for stream in own_late:
        stream.begin(0)

    def small_step(number):
        if number < bits:
            small_steps[number].wait()
            pair_vm[number + 1] = pair_vm[number] + pair_in[number]
            if number + 1 < bits:
                small_steps[number + 1].start()

    early = downs + ups
    steps(far_late[2], ups[2], ups[0], far_late[0])
    steps(own_late[0], far_late[1], far_late[2])
    small_step(0)
    steps(own_late[1], own_late[2], own_late[0], far_late[1])
    steps(own_late[1], own_late[2])
    frames_spread.hand_on()
    steps(*far_late)
    small_step(1)
    steps(*own_late)
    for number in range(2, bits):
        small_step(number)
    while True:
        waiting = [one for one in early + own_late if one.done < len(one.order)]
        waiting += [one for one in far_late if one.done + 1 < len(one.order)]
        if not waiting:
            break
        steps(*waiting)
    steps(*far_late)
    small_out[...] = pair_vm[bits]
    frames_spread.source_free()
    frames_spread.close()
    for stream in streams:
        stream.close()
    sent(last_swaps)


def finish_kernel(
    bits,
    out_all,
    frames_all,
    down_rows,
    up_rows,
    inward_rows,
    sums,
    out_ref,
    frames_ref,
    inward_ref,
    outward_ref,
    up_ref,
    down_ref,
    inward_bias_ref,
    up_bias_ref,
    gain_ref,
    offset_ref,
    out_vm,
    low_vm,
    wide_vm,
    rows_vm,
    sums_vm,
    inward_vm,
    outward_vm,
    sems,
    few_sems,
):
    pieces, tokens = out_vm.shape[:2]
    rows = rows_vm.shape[1]
    dp_place = lax.axis_index("dp")
    few = [
        pltpu.make_async_copy(source, target, few_sems.at[n])
        for n, (source, target) in enumerate(
            (
                (sums, sums_vm),
                (inward_rows, rows_vm.at[0]),
                (down_rows, rows_vm.at[1]),
                (up_rows, rows_vm.at[2]),
                (rows_vm.at[1], down_ref),
                (rows_vm.at[2], up_ref.at[0]),
                (inward_vm, inward_ref),
                (outward_vm, outward_ref),
            )
        )
    ]
    start(few[:4])
    spots = [pl.ds(n * tokens, tokens) for n in range(pieces)]
    low_loads = [
        pltpu.make_async_copy(frames_all.at[at], low_vm.at[n], sems.at[0, n])
        for n, at in enumerate(spots)
    ]
    out_loads = [
        pltpu.make_async_copy(out_all.at[at], out_vm.at[n], sems.at[1, n])
        for n, at in enumerate(spots)
    ]
    for n in range(pieces):
        low_loads[n].start()
        out_loads[n].start()
    stores = few[4:]
    for n, at in enumerate(spots):
        low_loads[n].wait()
        wide_vm[n] = low_vm[n].astype(WIDE)
        stores.append(pltpu.make_async_copy(wide_vm.at[n], frames_ref.at[at], sems.at[2, n]))
        stores[-1].start()
        out_loads[n].wait()
        stores.append(pltpu.make_async_copy(out_vm.at[n], out_ref.at[at], sems.at[3, n]))
        stores[-1].start()
    for copy in few[:4]:
        copy.wait()
    start(few[4:6])

    def turned(values):
        filled = jnp.concatenate([values, jnp.zeros((LANES - rows, values.shape[1]), WIDE)], axis=0)
        return filled.T[:, :rows]

    def kind(number):
        outer = rows_vm[0, :, 128 * number : 128 * number + 128]
        inner = rows_vm[0, :, 512 + 128 * (number // 2) : 640 + 128 * (number // 2)]
        if number % 2:
            inner = pltpu.roll(inner, HEAD_SIZE, 1)
        return outer, inner

    for number in range(3):
        outer, inner = kind(number)
        inward_vm[0, number, :, 0:128] = outer
        inward_vm[0, number, :, 128:192] = inner[:, :HEAD_SIZE]
    outer, inner = kind(3)
    outward_vm[0, 0:128] = turned(outer)
    outward_vm[0, 128:192] = turned(inner)[:HEAD_SIZE]
    start(few[6:])

    def own_part(values, part):
        width = values.shape[1]
        return pltpu.roll(values, lax.rem(width - dp_place * part, width), 1)[:, :part]

    share = rows_vm.shape[2] // 2**bits
    wide_share = own_part(sums_vm[1], share)
    gain_ref[0] = wide_share[0:2]
    offset_ref[0] = wide_share[2:6]
    lines = up_bias_ref.shape[0]
    part = LANES // 2**bits
    for line in range(lines):
        block = sums_vm[0, 0:8, LANES * line : LANES * (line + 1)]
        up_bias_ref[line] = own_part(block, part)[0:1]
    part = HEAD_SIZE // 2**bits
    for number in range(2):
        outer = sums_vm[0, 0:8, 128 * number : 128 * number + 128]
        inner = sums_vm[0, 0:8, 256:384]
        if number:
            inner = pltpu.roll(inner, HEAD_SIZE, 1)
        for head, block in enumerate((outer, pltpu.roll(outer, HEAD_SIZE, 1), inner)):
            inward_bias_ref[head, number : number + 1] = own_part(block, part)[1:2]
    for copy in stores:
        copy.wait()


def anywhere():
    return pl.BlockSpec(memory_space=pl.ANY)


def inside():
    return pl.BlockSpec(memory_space=pltpu.VMEM)


def call(kernel, name, number, inputs, outputs, scratch, semaphores):
    return pl.pallas_call(
        kernel,
        name=name,
        in_specs=[spec for spec, _ in inputs],
        out_specs=[spec for spec, _ in outputs],
        out_shape=[jax.ShapeDtypeStruct(shape, dtype) for _, (shape, dtype) in outputs],
        scratch_shapes=[pltpu.VMEM(shape, dtype) for shape, dtype in scratch]
        + [pltpu.SemaphoreType.DMA(shape) if shape else pltpu.SemaphoreType.REGULAR for shape in semaphores],
        compiler_params=pltpu.CompilerParams(
            collective_id=number,
            has_side_effects=number is not None,
            vmem_limit_bytes=VMEM_BYTES,
        ),
    )(*[value for _, value in inputs])


def shards(
    bits,
    frames,
    segment_ids,
    valid_frames,
    inward_weight,
    inward_bias,
    output_weight,
    upward_weight,
    upward_bias,
    downward_weight,
    norm_gains,
    offsets,
    cotangent,
):
    token_count, features = frames.shape
    count = segment_ids.shape[1]
    wide_count = padded(count)
    hidden = upward_weight.shape[2]
    rows = features // 2**bits
    corner_start = row_blocks(count)[-1][0]
    square = ((wide_count, features), LOW)
    square_wide = ((wide_count, features), WIDE)
    rows_wide = ((count, features), WIDE)
    b_shape = ((4, 8, 1152 + hidden), WIDE)
    marks = ((wide_count, LANES), LOW)
    corner_shape = ((count - corner_start, wide_count - corner_start), WIDE)
    plan = stream_plan(bits, features)
    grid = (2,) * bits + (rows,)
    buffers = []
    for _, columns, order, base in plan:
        buffers += [(shape, LOW) for shape in stream_shapes(bits, rows, columns[1], order, base)]
    own_chunk = ((rows, hidden), WIDE)
    small_shape = ((5, 8, features), WIDE)
    all_rows = ((4, count, features), LOW)
    results = call(
        functools.partial(layer_kernel, count, bits, plan),
        "layer",
        1,
        [
            (anywhere(), frames),
            (anywhere(), cotangent),
            (anywhere(), jnp.swapaxes(inward_weight[0], 1, 2)),
            (anywhere(), output_weight[0]),
            (anywhere(), upward_weight[0]),
            (anywhere(), downward_weight[0]),
            (inside(), jnp.swapaxes(inward_bias[0], 0, 1)),
            (inside(), upward_bias[0]),
            (inside(), segment_ids),
            (inside(), valid_frames),
            (inside(), norm_gains[0]),
            (inside(), offsets[0]),
        ],
        [
            (anywhere(), all_rows),
            (anywhere(), all_rows),
            (anywhere(), ((4, features, hidden), LOW)),
            (anywhere(), square),
            (anywhere(), square),
            (anywhere(), square),
            (anywhere(), rows_wide),
            (anywhere(), rows_wide),
            (inside(), own_chunk),
            (inside(), own_chunk),
            (inside(), own_chunk),
            (inside(), ((2, 8, features), WIDE)),
        ],
        [
            ((8, features, hidden), LOW),
            ((4, wide_count, hidden), LOW),
            ((4, wide_count, hidden), LOW),
            square,
            square,
            square,
            square,
            square,
            square,
            square_wide,
            square_wide,
            square_wide,
            ((3, 2) + grid + (hidden,), LOW),
            ((2, features, hidden), LOW),
            ((2, features, hidden), LOW),
            ((LANES, wide_count), LOW),
            ((LANES, wide_count), LOW),
            ((LANES, wide_count), WIDE),
            ((LANES, wide_count), WIDE),
            ((3, 8, LANES), WIDE),
            small_shape,
            ((2, 3, 8, features), WIDE),
            ((bits + 1, 2, 8, features), WIDE),
            ((bits, 2, 8, features), WIDE),
            b_shape,
            ((2, 8, 1152 + hidden), WIDE),
            ((16, wide_count), jnp.int32),
            marks,
            marks,
            corner_shape,
        ]
        + buffers,
        [(160,), (160,), (32,), ()],
    )
    out_all, frames_all = results[:2]
    down_rows, up_rows, inward_rows, sums = results[8:]
    pieces = 8
    tokens = token_count // pieces
    lines = upward_bias.shape[1]
    inward_shape = ((1, 3, rows, 192), WIDE)
    outward_shape = ((1, 192, rows), WIDE)
    (
        layer_output,
        grad_frames,
        grad_inward,
        grad_outward,
        grad_up,
        grad_down,
        grad_pair,
        grad_up_bias,
        grad_gains,
        grad_offsets,
    ) = call(
        functools.partial(finish_kernel, bits),
        "finish",
        None,
        [
            (anywhere(), out_all.reshape(token_count, features)),
            (anywhere(), frames_all.reshape(token_count, features)),
            (anywhere(), down_rows),
            (anywhere(), up_rows),
            (anywhere(), inward_rows),
            (anywhere(), sums),
        ],
        [
            (anywhere(), ((token_count, features), LOW)),
            (anywhere(), ((token_count, features), WIDE)),
            (anywhere(), inward_shape),
            (anywhere(), outward_shape),
            (anywhere(), ((1, rows, hidden), WIDE)),
            (anywhere(), ((rows, hidden), WIDE)),
            (inside(), ((3, 2, HEAD_SIZE // 2**bits), WIDE)),
            (inside(), ((lines, 1, LANES // 2**bits), WIDE)),
            (inside(), ((1, 2, rows), WIDE)),
            (inside(), ((1, 4, rows), WIDE)),
        ],
        [
            ((pieces, tokens, features), LOW),
            ((pieces, tokens, features), LOW),
            ((pieces, tokens, features), WIDE),
            ((3, rows, hidden), WIDE),
            ((2, 8, features), WIDE),
            inward_shape,
            outward_shape,
        ],
        [(4, pieces), (8,)],
    )
    return (
        layer_output,
        grad_frames,
        grad_inward,
        jnp.swapaxes(grad_pair, 0, 1)[None],
        grad_outward,
        grad_up,
        jnp.swapaxes(grad_up_bias, 0, 1),
        grad_down.T[None],
        grad_gains,
        grad_offsets,
    )


def solution(mesh):
    bits = mesh.shape["dp"].bit_length() - 1
    in_specs = (
        P("dp", None),
        P("dp", None),
        P("dp", None),
        P(None, None, None, "tensor"),
        P(None, None, "tensor", None),
        P(None, "tensor", None),
        P(None, None, "tensor"),
        P(None, "tensor", None),
        P(None, "tensor", None),
        P(),
        P(),
        P("dp", None),
    )
    out_specs = (
        P("dp", None),
        P("dp", None),
        P(None, None, "dp", "tensor"),
        P(None, None, "tensor", "dp"),
        P(None, "tensor", "dp"),
        P(None, "dp", "tensor"),
        P(None, "tensor", "dp"),
        P(None, "tensor", "dp"),
        P(None, None, "dp"),
        P(None, None, "dp"),
    )
    return jax.shard_map(
        functools.partial(shards, bits),
        mesh=mesh,
        in_specs=in_specs,
        out_specs=out_specs,
        check_vma=False,
    )
```
